256 devices in a mesh: wide: 32 (over z, y), narrow: 8 (over x, core).
Axes of the slice: x: 4, y: 4, z: 8, core: 2. Of those that a mesh axis runs over, the one named last changes fastest.
Arguments:
- right_side: float32 [224, 896, 256], P('narrow', 'wide'), may hold values from -60 to 60
- initial_guess: float32 [224, 896, 256], P('narrow', 'wide'), may hold values from -6 to 6
- class_map: int32 [224, 896], P('narrow', 'wide'), may hold values from 0 to 7
- class_conductivity: float32 [8], replicated, may hold values from 0.2 to 2
- window_index: int32 [8, 32, 1024], P('narrow', 'wide'), may hold values from 0 to 1023, each once within a row
- local_inverse: float32 [8, 32, 1024, 1024], P('narrow', 'wide'), may hold values from -1 to 1
- coarse_basis: float32 [8, 32, 4, 1024], P('narrow', 'wide'), may hold values from -0.1875 to 0.1875
- coarse_inverse: float32 [1024, 1024], P('wide', 'narrow'), may hold values from -8 to 8
Outputs:
- solution: float32 [224, 896, 256], P('narrow', 'wide')
- residual: float32 [224, 896, 256], P('narrow', 'wide')
The draws below stay inside these ranges and needn't reach their ends.
All inputs are finite; a program needn't handle non-finite values.
Results may differ from the reference program's by a relative error of at most 0.00013.
Values sent between devices are 32-bit elements; how exact they have to be, the bound alone decides.
No kernel may reach another device: no remote copies, remote signals or barrier semaphores. Data moves between devices by JAX's collectives and lax.ppermute only.
A program may use at most 64 MiB of HBM per device.

```python
import math
import jax
import jax.numpy as jnp
from jax import lax

ES = 32
OV = 2
MODES = 4
ITERS = 3
CLASSES = 8
NRHS = 256
CS = 28
LOCAL = 1024
SROWS = 8
SCOLS = 32
NX = 224
NY = 896
NC = 1024


def draw_right_side(key, part):
    key_noise = jax.random.fold_in(key, 11)
    col_pos = jnp.arange(NY, dtype=jnp.float32)[None, :, None]
    across = jnp.exp(math.log(10.0) * col_pos / (NY - 1))
    sample = jax.random.truncated_normal(key_noise, -6.0, 6.0, (NX, NY, NRHS), jnp.float32)
    return sample * across


def draw_local_inverse(key, part):
    key_off = jax.random.fold_in(key, 23)
    shape_full = (SROWS, SCOLS, LOCAL, LOCAL)
    identity = jnp.eye(LOCAL, dtype=jnp.float32)
    sample = jax.random.truncated_normal(key_off, -6.0, 6.0, shape_full, jnp.float32)
    return 0.25 * (identity + sample * (0.6 / math.sqrt(LOCAL)))


def draw_coarse_inverse(key, part):
    key_off = jax.random.fold_in(key, 31)
    rows_all = jnp.arange(NC, dtype=jnp.int32)
    mode_of = rows_all % MODES
    srow_of = rows_all // MODES % SROWS
    scol_of = rows_all // (MODES * SROWS)
    paired = (srow_of * SCOLS + scol_of) * MODES + mode_of
    identity = (paired[:, None] == rows_all[None, :]).astype(jnp.float32)
    sample = jax.random.truncated_normal(key_off, -6.0, 6.0, (NC, NC), jnp.float32)
    return 4.0 * identity + sample * (2.0 / math.sqrt(NC))


def set_ends(array, key, low, high):
    index_at = [jax.random.randint(jax.random.fold_in(key, axis), (), 0, length) for axis, length in enumerate(array.shape)]
    widest = array.shape.index(max(array.shape))
    neighbour = index_at[:widest] + [(index_at[widest] + 1) % array.shape[widest]] + index_at[widest + 1:]
    return array.at[tuple(index_at)].set(low).at[tuple(neighbour)].set(high)


def block_scale(stream_key, shape, cuts, least, high):
    factor_of = 1.0
    for position, parts in cuts:
        heights = jax.random.uniform(jax.random.fold_in(jax.random.fold_in(stream_key, 6), position), (parts,), jnp.float32, least / len(cuts), high / len(cuts))
        factor_of = factor_of * jnp.repeat(jnp.exp(heights), shape[position] // parts).reshape((-1,) + (1,) * (len(shape) - 1 - position))
    return factor_of


def normal_values(stream_key, dims, scale, reach, shards=(), kind=jnp.bfloat16):
    drawn = scale * jax.random.normal(stream_key, dims, jnp.float32)
    if shards:
        drawn = drawn * block_scale(stream_key, dims, shards, -0.22, 0.18)
    return jnp.clip(drawn, -reach, reach).astype(kind)


def setup_inputs(seed: int = 0) -> dict:
    streams_of = jax.random.split(jax.random.key(seed), 9)
    right_side = draw_right_side(jax.random.fold_in(streams_of[8], 71), 0)
    initial_guess = normal_values(streams_of[1], (NX, NY, NRHS), 1.0, 6.0, ((0, 8), (1, 32)), jnp.float32)
    class_map = set_ends(jax.random.randint(streams_of[2], (NX, NY), 0, CLASSES), jax.random.fold_in(streams_of[2], 1), 0, CLASSES - 1).astype(jnp.int32)
    class_conductivity = jnp.clip(jnp.exp(jax.random.uniform(streams_of[3], (CLASSES,), jnp.float32, math.log(0.2), math.log(2.0))), 0.2, 2.0)
    window_index = jax.vmap(lambda own: jax.random.permutation(own, LOCAL))(jax.random.split(streams_of[4], SROWS * SCOLS)).reshape((SROWS, SCOLS, LOCAL)).astype(jnp.int32)
    local_inverse = draw_local_inverse(jax.random.fold_in(streams_of[8], 71), 0)
    coarse_basis = normal_values(streams_of[6], (SROWS, SCOLS, MODES, LOCAL), LOCAL ** -0.5, 0.1875, ((0, 8), (1, 32)), jnp.float32)
    coarse_inverse = draw_coarse_inverse(jax.random.fold_in(streams_of[8], 71), 0)
    return dict(right_side=right_side, initial_guess=initial_guess, class_map=class_map, class_conductivity=class_conductivity, window_index=window_index, local_inverse=local_inverse, coarse_basis=coarse_basis, coarse_inverse=coarse_inverse)


HIGHEST = lax.Precision.HIGHEST
REACTION = 0.01
NEIGHBOURS = ((0, 1), (2, 1), (1, 0), (1, 2))


def apply_operator(padded_field, conduct):
    height = padded_field.shape[0] - 2
    breadth = padded_field.shape[1] - 2
    centre = padded_field[1:height + 1, 1:breadth + 1]
    own_conduct = conduct[1:height + 1, 1:breadth + 1]
    result = REACTION * centre
    for row_shift, col_shift in NEIGHBOURS:
        beside = padded_field[row_shift:row_shift + height, col_shift:col_shift + breadth]
        face_weight = 0.5 * (own_conduct + conduct[row_shift:row_shift + height, col_shift:col_shift + breadth])
        result = result + face_weight[:, :, None] * (centre - beside)
    return result


def reference(right_side, initial_guess, class_map, class_conductivity, window_index, local_inverse, coarse_basis, coarse_inverse):
    conduct = class_conductivity[class_map]
    conduct_pad = jnp.pad(conduct, 1)

    def operate(values):
        return apply_operator(jnp.pad(values, ((1, 1), (1, 1), (0, 0))), conduct_pad)

    row_index = jnp.arange(SROWS, dtype=jnp.int32)[:, None] * CS + jnp.arange(ES, dtype=jnp.int32)[None, :]
    col_index = jnp.arange(SCOLS, dtype=jnp.int32)[:, None] * CS + jnp.arange(ES, dtype=jnp.int32)[None, :]
    inverse_order = jnp.argsort(window_index, axis=-1).astype(jnp.int32)
    solution = initial_guess
    residual = right_side - operate(solution)
    for iteration in range(ITERS):
        padded_res = jnp.pad(residual, ((OV, OV), (OV, OV), (0, 0)))
        windows = padded_res[row_index[:, None, :, None], col_index[None, :, None, :]]
        windows = windows.reshape(SROWS, SCOLS, ES * ES, NRHS)
        gathered = jnp.take_along_axis(windows, window_index[:, :, :, None], axis=2)
        local_part = jnp.einsum("abkl,ablr->abkr", local_inverse, gathered, precision=HIGHEST)
        coarse_rhs = jnp.einsum("abmk,abkr->abmr", coarse_basis, gathered, precision=HIGHEST).reshape(NC, NRHS)
        coarse_sol = jnp.dot(coarse_inverse, coarse_rhs, precision=HIGHEST, preferred_element_type=jnp.float32)
        coarse_sol = coarse_sol.reshape(SCOLS, SROWS, MODES, NRHS).transpose(1, 0, 2, 3)
        extended = local_part + jnp.einsum("abmk,abmr->abkr", coarse_basis, coarse_sol, precision=HIGHEST)
        windowed = jnp.take_along_axis(extended, inverse_order[:, :, :, None], axis=2)
        windowed = windowed.reshape(SROWS, SCOLS, ES, ES, NRHS)
        direction = windowed[:, :, OV:OV + CS, OV:OV + CS].transpose(0, 2, 1, 3, 4).reshape(NX, NY, NRHS)
        image = operate(direction)
        stepsize = jnp.sum(residual * image, axis=(0, 1)) / jnp.sum(image * image, axis=(0, 1))
        solution = solution + stepsize * direction
        residual = residual - stepsize * image
    return solution, residual
```

```python
import jax
import jax.numpy as jnp
from jax import lax
from jax.sharding import PartitionSpec as P

OV = 2
MODES = 4
CS = 28
ES = CS + 2 * OV
XS = ES + 2
LOCAL = ES * ES
OWN = CS * CS
NB = 9 * MODES

HIGHEST = lax.Precision.HIGHEST
REACTION = 0.01
F32 = jnp.float32
BF16 = jnp.bfloat16


def shift(x, axis, step):
    count = lax.axis_size(axis)
    return lax.ppermute(x, axis, [(i, i + step) for i in range(count) if 0 <= i + step < count])


def pack(parts, columns):
    flat = jnp.concatenate([p.reshape(-1) for p in parts])
    rows = -(-flat.shape[0] // columns)
    return jnp.pad(flat, (0, rows * columns - flat.shape[0])).reshape(rows, columns)


def unpack(flat, shapes):
    out = []
    at = 0
    flat = flat.reshape(-1)
    for shape in shapes:
        size = 1
        for length in shape:
            size *= length
        out.append(lax.slice_in_dim(flat, at, at + size).reshape(shape))
        at += size
    return out


def halves(x):
    high = lax.reduce_precision(x, 8, 7)
    low = lax.reduce_precision(x - high, 8, 7)
    return high.astype(BF16), low.astype(BF16)


def dot(a, b):
    return jnp.dot(a, b, preferred_element_type=F32)


def dot_exact(a, b):
    return jnp.dot(a, b, precision=HIGHEST, preferred_element_type=F32)


def extended(field, width):
    left = shift(field[:, CS - width :], "wide", 1)
    right = shift(field[:, :width], "wide", -1)
    field = jnp.concatenate([left, field, right], axis=1)
    above = shift(field[CS - width :], "narrow", 1)
    below = shift(field[:width], "narrow", -1)
    return jnp.concatenate([above, field, below], axis=0)


def crossed(field):
    left = shift(field[:, CS - 1 :], "wide", 1)
    right = shift(field[:, :1], "wide", -1)
    above = shift(field[CS - 1 :], "narrow", 1)
    below = shift(field[:1], "narrow", -1)
    middle = jnp.concatenate([left, field, right], axis=1)
    sides = ((0, 0), (1, 1), (0, 0))
    return jnp.concatenate([jnp.pad(above, sides), middle, jnp.pad(below, sides)], axis=0)


def operate(padded, weights):
    diag, up, down, left, right = weights
    n = padded.shape[0] - 2
    return (
        diag[:, :, None] * padded[1 : n + 1, 1 : n + 1]
        - up[:, :, None] * padded[:n, 1 : n + 1]
        - down[:, :, None] * padded[2:, 1 : n + 1]
        - left[:, :, None] * padded[1 : n + 1, :n]
        - right[:, :, None] * padded[1 : n + 1, 2:]
    )


def own_cells(field):
    return field[..., OV : OV + CS, OV : OV + CS]


def to_all(x, axis):
    count = lax.axis_size(axis)
    copies = jnp.broadcast_to(x[None], (count,) + x.shape)
    return lax.all_to_all(copies, axis, 0, 0, tiled=True)


def local(
    right_side,
    initial_guess,
    class_map,
    class_conductivity,
    window_index,
    local_inverse,
    coarse_basis,
    coarse_inverse,
):
    nw = lax.axis_size("wide")
    nn = lax.axis_size("narrow")
    columns = right_side.shape[2]
    classes = class_conductivity.shape[0]
    matches = class_map[:, :, None] == jnp.arange(classes, dtype=jnp.int32)[None, None, :]
    conduct = jnp.sum(jnp.where(matches, class_conductivity[None, None, :], 0.0), axis=2)
    onehot = window_index[0, 0][:, None] == jnp.arange(LOCAL, dtype=jnp.int32)[None, :]
    basis = dot_exact(coarse_basis[0, 0], onehot.astype(F32))
    basis_own = own_cells(basis.reshape(MODES, ES, ES))

    small = jnp.concatenate([conduct[None], basis_own], axis=0)
    kinds = small.shape[0]
    rows_c, cols_c = coarse_inverse.shape
    sides = []
    for cut, cut2, step in (
        (slice(CS - 3, CS), slice(CS - 2, CS), 1),
        (slice(0, 3), slice(0, 2), -1),
    ):
        sent = pack(
            [initial_guess[:, cut], right_side[:, cut2], small[:, :, cut], coarse_inverse], columns
        )
        got = shift(sent, "wide", step)
        shapes = ((CS, 3, columns), (CS, 2, columns), (kinds, CS, 3), (rows_c, cols_c))
        sides.append(unpack(got, shapes))
    (gl, rl, sl, cl), (gr, rr, sr, cr) = sides
    guess = jnp.concatenate([gl, initial_guess, gr], axis=1)
    right = jnp.concatenate([rl, right_side, rr], axis=1)
    small = jnp.concatenate([sl, small, sr], axis=2)
    sides = []
    for cut, cut2, step in (
        (slice(CS - 3, CS), slice(CS - 2, CS), 1),
        (slice(0, 3), slice(0, 2), -1),
    ):
        sent = pack([guess[cut], right[cut2], small[:, cut]], columns)
        got = shift(sent, "narrow", step)
        sides.append(unpack(got, ((3, XS, columns), (2, ES, columns), (kinds, 3, XS))))
    (ga, ra, sa), (gb, rb, sb) = sides
    guess = jnp.concatenate([ga, guess, gb], axis=0)
    right = jnp.concatenate([ra, right, rb], axis=0)
    small = jnp.concatenate([sa, small, sb], axis=1)

    near = small[0]
    here = near[1:-1, 1:-1]
    cell = jnp.arange(ES, dtype=jnp.int32) - OV
    row = cell + lax.axis_index("narrow") * CS
    col = cell + lax.axis_index("wide") * CS
    inside = ((row >= 0) & (row < nn * CS))[:, None] & ((col >= 0) & (col < nw * CS))[None, :]
    faces = [
        jnp.where(inside, 0.5 * (here + beside), 0.0)
        for beside in (near[:-2, 1:-1], near[2:, 1:-1], near[1:-1, :-2], near[1:-1, 2:])
    ]
    diag = jnp.where(inside, REACTION + (faces[0] + faces[1]) + (faces[2] + faces[3]), 0.0)
    weights = (diag, *faces)
    weights_own = tuple(own_cells(w) for w in weights)

    region = jnp.where(jnp.arange(XS) < 3, 0, jnp.where(jnp.arange(XS) < 3 + CS, 1, 2))
    of_row = region[None, :] == jnp.arange(3)[:, None]
    of_col = of_row
    chosen = of_col[:, None, None, None, :] & of_row[None, :, None, :, None]
    modes = jnp.where(chosen, small[1:][None, None], 0.0).reshape(NB, XS, XS)
    n = ES
    modes_a = (
        diag[None] * modes[:, 1:-1, 1:-1]
        - faces[0][None] * modes[:, :n, 1:-1]
        - faces[1][None] * modes[:, 2:, 1:-1]
        - faces[2][None] * modes[:, 1:-1, :n]
        - faces[3][None] * modes[:, 1:-1, 2:]
    )
    modes_a = modes_a.reshape(NB, LOCAL)
    modes_a_own = own_cells(modes_a.reshape(NB, ES, ES)).reshape(NB, OWN)
    next_coarse = dot_exact(basis, modes_a.T)
    basis_flat = basis_own.reshape(MODES, OWN)

    inverse3 = jnp.stack([cl, coarse_inverse, cr]).reshape(3, nn, MODES, cols_c)
    inverse3 = jnp.pad(inverse3, ((0, 0), (1, 1), (0, 0), (0, 0)))
    inverse9 = jnp.stack([inverse3[:, d : d + nn] for d in range(3)], axis=1)
    inverse9 = inverse9.transpose(2, 0, 1, 3, 4).reshape(nn * NB, cols_c)

    select = onehot.astype(BF16)
    select_own = own_cells(select.reshape(LOCAL, ES, ES)).reshape(LOCAL, OWN)
    in_order = []
    for part in halves(local_inverse[0, 0]):
        rows = lax.dot_general(
            select_own, part, (((0,), (0,)), ((), ())), preferred_element_type=F32
        ).astype(BF16)
        in_order.append(dot(rows, select).astype(BF16))
    inverse_high, inverse_low = in_order

    def solve_local(window):
        high, low = halves(window)
        return dot(inverse_high, high) + (dot(inverse_high, low) + dot(inverse_low, high))

    def coarse(rhs, sums):
        sent = rhs if sums is None else jnp.concatenate([rhs, sums], axis=0)
        got = to_all(sent, "wide")
        part = dot_exact(inverse9, got[:, :MODES].reshape(nw * MODES, columns))
        part = part.reshape(nn, NB, columns)
        if sums is not None:
            mine = jnp.sum(got[:, MODES:], axis=0)
            part = jnp.concatenate(
                [part, jnp.broadcast_to(mine[None], (nn,) + mine.shape)], axis=1
            )
        total = jnp.sum(lax.all_to_all(part, "narrow", 0, 0, tiled=True), axis=0)
        return total[:NB], total[NB:]

    def over_modes(table, values):
        return lax.dot_general(
            table,
            values,
            (((0,), (0,)), ((), ())),
            precision=HIGHEST,
            preferred_element_type=F32,
        )

    def inner(residual, image):
        return jnp.stack([jnp.sum(residual * image, axis=0), jnp.sum(image * image, axis=0)])

    centre = slice(4 * MODES, 5 * MODES)

    window0 = right - operate(guess, weights)
    residual0 = window0[OV : OV + CS, OV : OV + CS].reshape(OWN, columns)
    window = window0.reshape(LOCAL, columns)
    rhs = dot_exact(basis, window)

    v0 = solve_local(window)
    near_v = operate(extended(v0.reshape(CS, CS, columns), 3), weights).reshape(LOCAL, columns)
    c0, _ = coarse(rhs, None)
    window = near_v + over_modes(modes_a, c0)
    p0 = v0 + over_modes(basis_flat, c0[centre])
    q0 = window.reshape(ES, ES, columns)[OV : OV + CS, OV : OV + CS].reshape(OWN, columns)
    rhs = dot_exact(basis, near_v) + dot_exact(next_coarse, c0)
    sums0 = inner(residual0, q0)

    v1 = solve_local(window)
    near_v = operate(extended(v1.reshape(CS, CS, columns), 3), weights).reshape(LOCAL, columns)
    c1, total = coarse(rhs, sums0)
    s0 = total[0] / total[1]
    window = near_v + over_modes(modes_a, c1)
    p1 = v1 + over_modes(basis_flat, c1[centre])
    q1 = window.reshape(ES, ES, columns)[OV : OV + CS, OV : OV + CS].reshape(OWN, columns)
    rhs = dot_exact(basis, near_v) + dot_exact(next_coarse, c1)
    residual1 = residual0 - s0 * q0
    image1 = q0 - s0 * q1
    direction1 = p0 - s0 * p1
    sums1 = inner(residual1, image1)

    v2 = solve_local(window)
    near_v = operate(crossed(v2.reshape(CS, CS, columns)), weights_own).reshape(OWN, columns)
    c2, total = coarse(rhs, sums1)
    s1 = total[0] / total[1]
    q2 = near_v + over_modes(modes_a_own, c2)
    p2 = v2 + over_modes(basis_flat, c2[centre])
    residual2 = residual1 - s1 * image1
    image2 = image1 - s1 * (q1 - s0 * q2)
    direction2 = direction1 - s1 * (p1 - s0 * p2)
    sums2 = inner(residual2, image2)
    total = jnp.sum(to_all(sums2, "narrow"), axis=0)
    total = jnp.sum(to_all(total, "wide"), axis=0)
    s2 = total[0] / total[1]

    cells = (CS, CS, columns)
    start = initial_guess.reshape(OWN, columns)
    answer = start + s0 * p0 + s1 * direction1 + s2 * direction2
    return answer.reshape(cells), (residual2 - s2 * image2).reshape(cells)


def solution(mesh):
    in_specs = (
        P("narrow", "wide", None),
        P("narrow", "wide", None),
        P("narrow", "wide"),
        P(),
        P("narrow", "wide", None),
        P("narrow", "wide", None, None),
        P("narrow", "wide", None, None),
        P("wide", "narrow"),
    )
    out_specs = (P("narrow", "wide", None), P("narrow", "wide", None))
    return jax.shard_map(local, mesh=mesh, in_specs=in_specs, out_specs=out_specs, check_vma=False)
```

```python
import functools

import jax
import jax.numpy as jnp
import numpy as np
from jax import lax
from jax.experimental import pallas as pl
from jax.experimental.pallas import tpu as pltpu
from jax.sharding import PartitionSpec as P

OV = 2
MODES = 4
CS = 28
ES = CS + 2 * OV
LOCAL = ES * ES
LANES = 128
XROWS = ES + 2
XCOLS = 48
OWNROWS = CS * ES
FIRST = OV * ES
SLOT = 40
NB = 9 * MODES

HIGHEST = lax.Precision.HIGHEST
REACTION = 0.01
F32 = jnp.float32
BF16 = jnp.bfloat16
VMEM_LIMIT = 40 * 2**20


def shift(x, axis, step):
    count = lax.axis_size(axis)
    return lax.ppermute(x, axis, [(i, i + step) for i in range(count) if 0 <= i + step < count])


def call(body, out, args, scratch=()):
    spec = pl.BlockSpec(memory_space=pltpu.VMEM)
    return pl.pallas_call(
        body,
        out_shape=[jax.ShapeDtypeStruct(shape, kind) for shape, kind in out],
        in_specs=[spec] * len(args),
        out_specs=[spec] * len(out),
        scratch_shapes=list(scratch),
        compiler_params=pltpu.CompilerParams(vmem_limit_bytes=VMEM_LIMIT),
    )(*args)


def dot(a, b):
    return jnp.dot(a, b, preferred_element_type=F32)


def dot_rows(a, b):
    return lax.dot_general(a, b, (((1,), (1,)), ((), ())), preferred_element_type=F32)


def dot_exact(a, b):
    return jnp.dot(a, b, precision=HIGHEST, preferred_element_type=F32)


def halves(x):
    high = x.astype(BF16)
    return high, (x - high.astype(F32)).astype(BF16)


def thirds(x):
    high = x.astype(BF16)
    rest = x - high.astype(F32)
    mid = rest.astype(BF16)
    return high, mid, (rest - mid.astype(F32)).astype(BF16)


def dot_halves(left_high, left_low, x):
    high, low = halves(x)
    return dot(left_high, high) + (dot(left_high, low) + dot(left_low, high))


def put_sides(field, row0, rows, from_left, from_right, base=0):
    for e in range(3):
        for i in range(rows):
            field[row0 + i, 7 + e : 8 + e, :] = from_left[e, base + i : base + i + 1, :]
            field[row0 + i, 38 + e : 39 + e, :] = from_right[e, base + i : base + i + 1, :]


def prepare(
    guess, right, classes, values, order, basis, tail, head, small, basis_out, select
):
    nclass = values.shape[1]
    for i in range(LOCAL // 64):
        place = lax.broadcasted_iota(jnp.int32, (64, LOCAL), 0) + i * 64
        select[i * 64 : i * 64 + 64, :] = jnp.where(place == order[...], 1.0, 0.0).astype(BF16)
    table = jnp.concatenate(
        [
            jnp.zeros((1, LOCAL), F32),
            basis[...],
            jnp.ones((1, LOCAL), F32),
            jnp.zeros((2, LOCAL), F32),
        ],
        axis=0,
    )
    parts = [p.astype(F32) for p in thirds(table)]
    stacked = jnp.concatenate(parts + [jnp.zeros((8, LOCAL), F32)], axis=0).astype(BF16)
    got = dot_rows(stacked, select[...])
    basis_out[...] = got[0:8] + (got[8:16] + got[16:24])
    rest = jnp.zeros((LANES - 8, LOCAL), F32)
    cells = None
    for p in parts:
        term = dot_rows(
            select[FIRST : FIRST + OWNROWS, :], jnp.concatenate([p, rest], axis=0).astype(BF16)
        )
        cells = term if cells is None else cells + term
    small[...] = cells.reshape(CS, ES, LANES)
    conduct = jnp.zeros((CS, CS), F32)
    for k in range(nclass):
        conduct = jnp.where(classes[...] == k, values[0:1, k : k + 1], conduct)
    sub = lax.broadcasted_iota(jnp.int32, (ES, CS), 0)
    lane = lax.broadcasted_iota(jnp.int32, (ES, CS), 1)
    lane0 = lax.broadcasted_iota(jnp.int32, (ES, LANES), 1) == 0
    for i in range(CS):
        spread = jnp.where(sub == lane + OV, jnp.broadcast_to(conduct[i : i + 1, :], (ES, CS)), 0.0)
        column = jnp.sum(spread, axis=1, keepdims=True)
        small[i] = jnp.where(lane0, column, small[i])
    c = guess.shape[2]
    for e in range(3):
        for i in range(CS):
            for sent, j in ((tail, CS - 3 + e), (head, e)):
                sent[e, i : i + 1, 0:c] = guess[i, j : j + 1, :]
                sent[e, i : i + 1, c : 2 * c] = right[i, j : j + 1, :]
                sent[e, i : i + 1, 2 * c :] = small[i, OV + j : OV + j + 1, :]


def reorder(inverse, select, high_out, low_out, rows):
    step = 256
    for part, out in ((0, high_out), (1, low_out)):
        for n in range(0, LOCAL, step):
            block = halves(inverse[:, n : n + step])[part]
            rows[:, n : n + step] = dot(select[FIRST : FIRST + OWNROWS, :], block).astype(BF16)
        for n in range(0, LOCAL, step):
            out[:, n : n + step] = dot_rows(rows[...], select[n : n + step, :]).astype(BF16)


def first_rows(guess, right, small, from_left, from_right, tail, head):
    c = guess.shape[2]
    for sent, base in ((tail, CS - 3), (head, 0)):
        sent[...] = jnp.zeros(sent.shape, F32)
        for r in range(3):
            sent[r, 10 : 10 + CS, 0:c] = guess[base + r]
            sent[r, 10 : 10 + CS, c : 2 * c] = right[base + r]
            sent[r, 8 : 8 + ES, 2 * c :] = small[base + r]
        put_sides(sent, 0, 3, from_left, from_right, base)


def field_rows(field, from_left, from_right, tail, head):
    for sent, base in ((tail, CS - 3), (head, 0)):
        sent[...] = jnp.zeros(sent.shape, F32)
        for r in range(3):
            sent[r, 8 : 8 + ES, :] = field[base + r]
        put_sides(sent, 0, 3, from_left, from_right, base)


def stencil(wide, weights, row, lanes, wrow=None):
    diag, up, down, left, right = weights
    k = row if wrow is None else wrow
    return (
        diag[k] * wide[row + 1, 8:40, lanes]
        - up[k] * wide[row, 8:40, lanes]
        - down[k] * wide[row + 2, 8:40, lanes]
        - left[k] * wide[row + 1, 7:39, lanes]
        - right[k] * wide[row + 1, 9:41, lanes]
    )


def solve_and_send(window, inverse_high, inverse_low, basis, sums, field, tail, head, sent):
    high, low = halves(window)
    field[...] = (
        dot(inverse_high[...], high) + (dot(inverse_high[...], low) + dot(inverse_low[...], high))
    ).reshape(field.shape)
    for e in range(3):
        for i in range(CS):
            tail[e, i : i + 1, :] = field[i, CS + OV - 3 + e : CS + OV - 2 + e, :]
            head[e, i : i + 1, :] = field[i, OV + e : OV + e + 1, :]
    parts = [p.astype(F32) for p in halves(basis[...])]
    table = jnp.concatenate(parts, axis=0).astype(BF16)
    got = dot(table, high)
    rhs = got[0:8] + (got[8:16] + dot(table, low)[0:8])
    line = lax.broadcasted_iota(jnp.int32, rhs.shape, 0)
    rhs = jnp.concatenate([rhs[1:5], jnp.zeros((4, rhs.shape[1]), F32)], axis=0)
    if sums is not None:
        rhs = jnp.where(line == 4, sums[0], jnp.where(line == 5, sums[1], rhs))
    for k in range(sent.shape[0]):
        sent[k] = rhs


def first(
    guess,
    right,
    small,
    from_left,
    from_right,
    above,
    below,
    basis,
    inverse_high,
    inverse_low,
    spread,
    of_row,
    of_col,
    diag,
    up,
    down,
    left,
    right_w,
    modes_a_high,
    modes_a_low,
    modes_high,
    modes_low,
    residual,
    field,
    tail,
    head,
    sent,
    wide,
    modes,
    window,
):
    c = guess.shape[2]
    for i in range(CS):
        wide[3 + i, 10 : 10 + CS, 0:c] = guess[i]
        wide[3 + i, 10 : 10 + CS, c : 2 * c] = right[i]
        wide[3 + i, 8:40, 2 * c :] = small[i]
    put_sides(wide, 3, CS, from_left, from_right)
    wide[0:3] = above[...]
    wide[31:34] = below[...]

    s = 2 * c

    @pl.loop(0, XROWS)
    def _(i):
        cells = wide[i, :, s : s + LANES]
        cells = jnp.where(lax.broadcasted_iota(jnp.int32, cells.shape, 1) < 8, cells, 0.0)
        modes[i] = dot_exact(cells, spread[...]) * of_row[i] * of_col[...]

    weights = (diag, up, down, left, right_w)

    @pl.loop(0, ES)
    def _(u):
        def cond(row, at):
            return jnp.broadcast_to(wide[row, at : at + ES, s : s + 1], (ES, LANES))

        here = cond(u + 1, 8)
        inside = jnp.broadcast_to(wide[u + 1, 8:40, s + 5 : s + 6], (ES, LANES))
        total = jnp.full((ES, LANES), REACTION, F32)
        for ref, row, at in ((up, u, 8), (down, u + 2, 8), (left, u + 1, 7), (right_w, u + 1, 9)):
            face = 0.5 * (here + cond(row, at))
            total = total + face
            ref[u] = face * inside
        diag[u] = total * inside

    @pl.loop(0, ES)
    def _(u):
        for k in range(c // LANES):
            lanes = slice(k * LANES, (k + 1) * LANES)
            there = slice(c + k * LANES, c + (k + 1) * LANES)
            window[u, :, lanes] = wide[u + 1, 8:40, there] - stencil(wide, weights, u, lanes)

    def tables(u, _):
        values = stencil(modes, weights, u, slice(None))
        high, low = halves(values)
        modes_a_high[pl.ds(u * ES, ES), :] = high
        modes_a_low[pl.ds(u * ES, ES), :] = low
        return 0

    lax.fori_loop(0, ES, tables, 0)

    def own_tables(i, _):
        high, low = halves(modes[i + 3, 8:40, :])
        modes_high[pl.ds(i * ES, ES), :] = high
        modes_low[pl.ds(i * ES, ES), :] = low
        return 0

    lax.fori_loop(0, CS, own_tables, 0)
    residual[...] = window[OV : OV + CS]
    solve_and_send(
        window[...].reshape(LOCAL, c),
        inverse_high,
        inverse_low,
        basis,
        None,
        field,
        tail,
        head,
        sent,
    )


def partial(got, table, out):
    c = got.shape[2]
    out[...] = dot_exact(table[...], got[...].reshape(-1, c)).reshape(out.shape)


def coarse_table(before, own, after, pick, spread, ones, out):
    stacked = jnp.concatenate([before[...], own[...], after[...]], axis=0)
    out[...] = dot_exact(dot_exact(pick[...], stacked), spread[...]) + ones[...]


def summed(got):
    total = got[0]
    for k in range(1, got.shape[0]):
        total = total + got[k]
    return total


def assemble(wide, field, from_left, from_right, above, below):
    wide[3:31, 8:40, :] = field[...]
    put_sides(wide, 3, CS, from_left, from_right)
    wide[0:3] = above[...]
    wide[31:34] = below[...]


def column_mask(lanes):
    col = lax.broadcasted_iota(jnp.int32, (ES, lanes), 0)
    return (col >= OV) & (col < OV + CS)


def spread_coarse(table_high, table_low, coarse):
    high, low = halves(coarse)
    return dot(table_high[...], high) + (dot(table_high[...], low) + dot(table_low[...], high))


def coarse_rows(total):
    rows, c = total.shape
    total = jnp.where(lax.broadcasted_iota(jnp.int32, (rows, c), 0) < NB, total, 0.0)
    return jnp.concatenate([total, jnp.zeros((LANES - rows, c), F32)], axis=0)


def step0(
    field,
    from_left,
    from_right,
    above,
    below,
    got,
    diag,
    up,
    down,
    left,
    right_w,
    modes_a_high,
    modes_a_low,
    basis,
    inverse_high,
    inverse_low,
    residual,
    image_own,
    coarse,
    field_out,
    tail,
    head,
    sent,
    wide,
    window,
):
    weights = (diag, up, down, left, right_w)
    c = field.shape[2]
    assemble(wide, field, from_left, from_right, above, below)
    total = coarse_rows(summed(got))
    coarse[...] = total
    window[...] = spread_coarse(modes_a_high, modes_a_low, total).reshape(window.shape)

    @pl.loop(0, ES)
    def _(u):
        for k in range(c // LANES):
            lanes = slice(k * LANES, (k + 1) * LANES)
            window[u, :, lanes] = window[u, :, lanes] + stencil(wide, weights, u, lanes)

    mask = column_mask(c)

    def reduce(i, carry):
        num, den = carry
        image = jnp.where(mask, window[i + OV], 0.0)
        image_own[i] = image
        return num + residual[i] * image, den + image * image

    zero = jnp.zeros((ES, c), F32)
    num, den = lax.fori_loop(0, CS, reduce, (zero, zero))
    sums = (jnp.sum(num, axis=0, keepdims=True), jnp.sum(den, axis=0, keepdims=True))
    solve_and_send(
        window[...].reshape(LOCAL, c),
        inverse_high,
        inverse_low,
        basis,
        sums,
        field_out,
        tail,
        head,
        sent,
    )


def step1(
    field,
    from_left,
    from_right,
    above,
    below,
    got,
    diag,
    up,
    down,
    left,
    right_w,
    modes_a_high,
    modes_a_low,
    basis,
    inverse_high,
    inverse_low,
    residual,
    image0,
    image_own,
    coarse,
    field_out,
    tail,
    head,
    sent,
    scale_out,
    wide,
    window,
):
    weights = (diag, up, down, left, right_w)
    c = field.shape[2]
    assemble(wide, field, from_left, from_right, above, below)
    total = summed(got)
    scale = total[NB : NB + 1] / total[NB + 1 : NB + 2]
    scale_out[...] = jnp.broadcast_to(scale, scale_out.shape)
    total = coarse_rows(total)
    coarse[...] = total
    window[...] = spread_coarse(modes_a_high, modes_a_low, total).reshape(window.shape)

    @pl.loop(0, ES)
    def _(u):
        for k in range(c // LANES):
            lanes = slice(k * LANES, (k + 1) * LANES)
            window[u, :, lanes] = window[u, :, lanes] + stencil(wide, weights, u, lanes)

    mask = column_mask(c)

    def reduce(i, carry):
        num, den = carry
        before = image0[i]
        mine = jnp.where(mask, window[i + OV], 0.0)
        image_own[i] = mine
        image = before - scale * mine
        left_over = residual[i] - scale * before
        return num + left_over * image, den + image * image

    zero = jnp.zeros((ES, c), F32)
    num, den = lax.fori_loop(0, CS, reduce, (zero, zero))
    sums = (jnp.sum(num, axis=0, keepdims=True), jnp.sum(den, axis=0, keepdims=True))
    solve_and_send(
        window[...].reshape(LOCAL, c),
        inverse_high,
        inverse_low,
        basis,
        sums,
        field_out,
        tail,
        head,
        sent,
    )


def step2(
    field,
    from_left,
    from_right,
    above,
    below,
    got,
    diag,
    up,
    down,
    left,
    right_w,
    modes_a_high,
    modes_a_low,
    residual,
    image0,
    image1,
    scale_in,
    residual_out,
    image_out,
    coarse,
    sent,
    scale_out,
    wide,
    window,
):
    weights = (diag, up, down, left, right_w)
    c = field.shape[2]
    wide[3:31, 8:40, :] = field[...]
    for i in range(CS):
        wide[3 + i, 9:10, :] = from_left[0, i : i + 1, :]
        wide[3 + i, 38:39, :] = from_right[0, i : i + 1, :]
    wide[2, 8:40, :] = above[...]
    wide[31, 8:40, :] = below[...]
    total = summed(got)
    scale = total[NB : NB + 1] / total[NB + 1 : NB + 2]
    scale_out[...] = jnp.broadcast_to(scale, scale_out.shape)
    earlier = scale_in[0:1]
    total = coarse_rows(total)
    coarse[...] = total
    own = slice(FIRST, FIRST + OWNROWS)
    high, low = halves(total)
    table = modes_a_high[own, :]
    window[...] = (
        dot(table, high) + (dot(table, low) + dot(modes_a_low[own, :], high))
    ).reshape(window.shape)
    mask = column_mask(LANES)

    def reduce(i, carry):
        out = []
        for k in range(c // LANES):
            lanes = slice(k * LANES, (k + 1) * LANES)
            num, den = carry[2 * k], carry[2 * k + 1]
            mine = window[i, :, lanes] + stencil(wide, weights, i + OV, lanes)
            mine = jnp.where(mask, mine, 0.0)
            s0 = earlier[:, lanes]
            s1 = scale[:, lanes]
            q0 = image0[i, :, lanes]
            q1 = image1[i, :, lanes]
            before = q0 - s0 * q1
            left_over = residual[i, :, lanes] - s0 * q0 - s1 * before
            image = before - s1 * (q1 - s0 * mine)
            residual_out[i, :, lanes] = left_over
            image_out[i, :, lanes] = image
            out += [num + left_over * image, den + image * image]
        return tuple(out)

    zero = jnp.zeros((ES, LANES), F32)
    sums = lax.fori_loop(0, CS, reduce, (zero,) * (2 * (c // LANES)))
    sums = [jnp.sum(x, axis=0, keepdims=True) for x in sums]
    num = jnp.concatenate(sums[0::2], axis=1)
    den = jnp.concatenate(sums[1::2], axis=1)
    line = lax.broadcasted_iota(jnp.int32, sent.shape[1:], 0)
    rows = jnp.where(line == 0, num, jnp.where(line == 1, den, 0.0))
    for k in range(sent.shape[0]):
        sent[k] = rows


def resend(got, sent):
    total = summed(got)
    for k in range(sent.shape[0]):
        sent[k] = total


def directions(
    guess,
    field0,
    field1,
    field2,
    coarse0,
    coarse1,
    coarse2,
    modes_high,
    modes_low,
    scale0,
    scale1,
    partial_out,
    last_out,
    p0,
    p1,
    p2,
):
    for p, coarse, field in ((p0, coarse0, field0), (p1, coarse1, field1), (p2, coarse2, field2)):
        p[...] = spread_coarse(modes_high, modes_low, coarse[...]).reshape(p.shape)
    s0 = scale0[0:1]
    s1 = scale1[0:1]

    @pl.loop(0, CS)
    def _(i):
        first_p = p0[i] + field0[i]
        second = p1[i] + field1[i]
        direction1 = first_p - s0 * second
        direction2 = direction1 - s1 * (second - s0 * (p2[i] + field2[i]))
        partial_out[i] = s0 * first_p + s1 * direction1
        last_out[i] = direction2


def finish(got, guess, partial_in, last, residual, image, answer, residual_out):
    total = summed(got)
    scale = total[0:1] / total[1:2]

    @pl.loop(0, CS)
    def _(i):
        answer[i] = guess[i] + (
            partial_in[i, OV : OV + CS, :] + scale * last[i, OV : OV + CS, :]
        )
        residual_out[i] = (
            residual[i, OV : OV + CS, :] - scale * image[i, OV : OV + CS, :]
        )


def mode_tables():
    spread = np.zeros((LANES, LANES), np.float32)
    of_row = np.zeros((XROWS, 1, LANES), np.float32)
    of_col = np.zeros((XCOLS, LANES), np.float32)
    region = [0] * 3 + [1] * CS + [2] * 3
    for db in range(3):
        for da in range(3):
            for m in range(MODES):
                lane = (db * 3 + da) * MODES + m
                spread[1 + m, lane] = 1.0
                for e in range(XROWS):
                    of_row[e, 0, lane] = region[e] == da
                    of_col[7 + e, lane] = region[e] == db
    return spread, of_row, of_col


def coarse_tables(nw, nn):
    pick = np.zeros((nn * SLOT, 3 * nn * MODES), np.float32)
    spread = np.zeros((nw * MODES, nw * 8), np.float32)
    ones = np.zeros((nn * SLOT, nw * 8), np.float32)
    for to in range(nn):
        for db in range(3):
            for da in range(3):
                a = to + da - 1
                for m in range(MODES):
                    if 0 <= a < nn:
                        row = to * SLOT + (db * 3 + da) * MODES + m
                        pick[row, (db * nn + a) * MODES + m] = 1.0
        for b in range(nw):
            ones[to * SLOT + NB, b * 8 + 4] = 1.0
            ones[to * SLOT + NB + 1, b * 8 + 5] = 1.0
    for b in range(nw):
        for m in range(MODES):
            spread[b * MODES + m, b * 8 + m] = 1.0
    return pick, spread, ones


def local(
    right_side,
    initial_guess,
    class_map,
    class_conductivity,
    window_index,
    local_inverse,
    coarse_basis,
    coarse_inverse,
):
    nw = lax.axis_size("wide")
    nn = lax.axis_size("narrow")
    c = right_side.shape[2]
    lanes = 2 * c + LANES
    own = ((CS, ES, c), F32)
    side = ((3, CS, c), F32)
    rows = ((3, XCOLS, c), F32)
    to_wide = ((nw, 8, c), F32)
    weight = ((ES, ES, LANES), F32)
    extended = pltpu.VMEM((XROWS, XCOLS, c), F32)
    window = pltpu.VMEM((ES, ES, c), F32)
    inverse = ((OWNROWS, LOCAL), BF16)
    mode_spread, of_row, of_col = mode_tables()
    pick, coarse_spread, ones = coarse_tables(nw, nn)

    def exchange(x, axis):
        return lax.all_to_all(x, axis, 0, 0, tiled=True)

    tail, head, small, basis, select = call(
        prepare,
        [
            ((3, CS, lanes), F32),
            ((3, CS, lanes), F32),
            ((CS, ES, LANES), F32),
            ((8, LOCAL), F32),
            ((LOCAL, LOCAL), BF16),
        ],
        [
            initial_guess,
            right_side,
            class_map,
            class_conductivity.reshape(1, -1),
            window_index.reshape(1, LOCAL),
            coarse_basis.reshape(MODES, LOCAL),
        ],
    )
    before = shift(coarse_inverse, "wide", 1)
    after = shift(coarse_inverse, "wide", -1)
    from_left = shift(tail, "wide", 1)
    from_right = shift(head, "wide", -1)
    inverse_high, inverse_low = call(
        reorder,
        [inverse, inverse],
        [local_inverse.reshape(LOCAL, LOCAL), select],
        [pltpu.VMEM((OWNROWS, LOCAL), BF16)],
    )
    tail, head = call(
        first_rows,
        [((3, XCOLS, lanes), F32)] * 2,
        [initial_guess, right_side, small, from_left, from_right],
    )
    above = shift(tail, "narrow", 1)
    below = shift(head, "narrow", -1)
    (table,) = call(
        coarse_table,
        [((nn * SLOT, nw * 8), F32)],
        [before, coarse_inverse, after, pick, coarse_spread, ones],
    )
    out = call(
        first,
        [weight] * 5
        + [((LOCAL, LANES), BF16)] * 2
        + [((OWNROWS, LANES), BF16)] * 2
        + [own, own, side, side, to_wide],
        [
            initial_guess,
            right_side,
            small,
            from_left,
            from_right,
            above,
            below,
            basis,
            inverse_high,
            inverse_low,
            mode_spread,
            of_row,
            of_col,
        ],
        [
            pltpu.VMEM((XROWS, XCOLS, lanes), F32),
            pltpu.VMEM((XROWS, XCOLS, LANES), F32),
            window,
        ],
    )
    weights = out[:5]
    modes_a = out[5:7]
    modes = out[7:9]
    residual, field0, tail, head, sent = out[9:]

    def coarse(sent):
        got = exchange(sent, "wide")
        (parts,) = call(partial, [((nn, SLOT, c), F32)], [got, table])
        return exchange(parts, "narrow")

    def beside(field, tail, head):
        from_left = shift(tail, "wide", 1)
        from_right = shift(head, "wide", -1)
        tail, head = call(field_rows, [rows, rows], [field, from_left, from_right])
        return from_left, from_right, shift(tail, "narrow", 1), shift(head, "narrow", -1)

    solver = [basis, inverse_high, inverse_low, residual]
    coarse_out = ((LANES, c), F32)
    scale_out = ((8, c), F32)
    near = beside(field0, tail, head)
    got = coarse(sent)
    image0, coarse0, field1, tail, head, sent = call(
        step0,
        [own, coarse_out, own, side, side, to_wide],
        [field0, *near, got, *weights, *modes_a, *solver],
        [extended, window],
    )
    near = beside(field1, tail, head)
    got = coarse(sent)
    image1, coarse1, field2, tail, head, sent, scale0 = call(
        step1,
        [own, coarse_out, own, side, side, to_wide, scale_out],
        [field1, *near, got, *weights, *modes_a, *solver, image0],
        [extended, window],
    )
    near = (
        shift(tail[2:3], "wide", 1),
        shift(head[0:1], "wide", -1),
        shift(field2[CS - 1], "narrow", 1),
        shift(field2[0], "narrow", -1),
    )
    got = coarse(sent)
    residual, image, coarse2, sent, scale1 = call(
        step2,
        [own, own, coarse_out, ((nn, 8, c), F32), scale_out],
        [field2, *near, got, *weights, *modes_a, residual, image0, image1, scale0],
        [extended, pltpu.VMEM((CS, ES, c), F32)],
    )
    got = exchange(sent, "narrow")
    (sent,) = call(resend, [to_wide], [got])
    got = exchange(sent, "wide")
    before_last, last = call(
        directions,
        [own, own],
        [initial_guess, field0, field1, field2, coarse0, coarse1, coarse2, *modes, scale0, scale1],
        [pltpu.VMEM((CS, ES, c), F32)] * 3,
    )
    return tuple(
        call(
            finish,
            [((CS, CS, c), F32)] * 2,
            [got, initial_guess, before_last, last, residual, image],
        )
    )


def solution(mesh):
    in_specs = (
        P("narrow", "wide", None),
        P("narrow", "wide", None),
        P("narrow", "wide"),
        P(),
        P("narrow", "wide", None),
        P("narrow", "wide", None, None),
        P("narrow", "wide", None, None),
        P("wide", "narrow"),
    )
    out_specs = (P("narrow", "wide", None), P("narrow", "wide", None))
    return jax.shard_map(local, mesh=mesh, in_specs=in_specs, out_specs=out_specs, check_vma=False)
```

```python
import jax
import jax.numpy as jnp
import numpy as np
from jax import lax
from jax.experimental import pallas as pl
from jax.experimental.pallas import tpu as pltpu
from jax.sharding import PartitionSpec as P

OV = 2
MODES = 4
CS = 28
ES = CS + 2 * OV
LOCAL = ES * ES
LANES = 128
XROWS = ES + 2
XCOLS = 48
OWNROWS = CS * ES
FIRST = OV * ES
SLOT = 40
NB = 9 * MODES
INSIDE = NB + MODES
SMALL_AT = ((5, 0), (5, LANES), (6, 0))
NEAR = {CS - 3: (None, 3, 4), 0: (3, 4, None)}
CONDUCT = LANES - 1

HIGHEST = lax.Precision.HIGHEST
REACTION = 0.01
F32 = jnp.float32
BF16 = jnp.bfloat16
VMEM_LIMIT = 60 * 2**20


def shift(x, axis, step):
    count = lax.axis_size(axis)
    return lax.ppermute(x, axis, [(i, i + step) for i in range(count) if 0 <= i + step < count])


class Copies:
    def __init__(self, buffers, places, sems):
        self.buffers = buffers
        self.copies = [
            pltpu.make_async_copy(b, p, sems.at[k]) for k, (b, p) in enumerate(zip(buffers, places))
        ]
        self.started = [False] * len(buffers)
        self.wait = None

    def flush(self, *refs):
        for k, buffer in enumerate(self.buffers):
            if not self.started[k] and (not refs or any(buffer is r for r in refs)):
                self.copies[k].start()
                self.started[k] = True

    def close(self):
        self.flush()
        for copy in self.copies:
            copy.wait()


def call(body, out, args, scratch=(), late=()):
    delayed = [k for group in late for k in group]
    na, no = len(args), len(out)

    def kernel(*refs):
        sources, places = refs[:na], refs[na : na + no]
        refs = refs[na + no :]
        inputs, buffers, refs = refs[:na], refs[na : na + no], refs[na + no :]
        extra, sems_in, sems_out = refs[:-2], refs[-2], refs[-1]
        copies = [pltpu.make_async_copy(sources[k], inputs[k], sems_in.at[k]) for k in range(na)]
        early = [k for k in range(na) if k not in delayed]
        for k in early + delayed:
            copies[k].start()
        for k in early:
            copies[k].wait()

        def wait(group):
            for k in late[group]:
                copies[k].wait()

        io = Copies(buffers, places, sems_out)
        io.wait = wait
        body(io, *inputs, *buffers, *extra)
        io.close()

    spec = pl.BlockSpec(memory_space=pl.ANY)
    return pl.pallas_call(
        kernel,
        out_shape=[jax.ShapeDtypeStruct(shape, kind) for shape, kind in out],
        in_specs=[spec] * na,
        out_specs=[spec] * no,
        scratch_shapes=[pltpu.VMEM(x.shape, x.dtype) for x in args]
        + [pltpu.VMEM(shape, kind) for shape, kind in out]
        + list(scratch)
        + [pltpu.SemaphoreType.DMA((na,)), pltpu.SemaphoreType.DMA((no,))],
        compiler_params=pltpu.CompilerParams(vmem_limit_bytes=VMEM_LIMIT),
    )(*args)


def dot(a, b):
    return jnp.dot(a, b, preferred_element_type=F32)


def dot_rows(a, b):
    return lax.dot_general(a, b, (((1,), (1,)), ((), ())), preferred_element_type=F32)


def dot_exact(a, b):
    return jnp.dot(a, b, precision=HIGHEST, preferred_element_type=F32)


def halves(x):
    high = x.astype(BF16)
    return high, (x - high.astype(F32)).astype(BF16)


def thirds(x):
    high = x.astype(BF16)
    rest = x - high.astype(F32)
    mid = rest.astype(BF16)
    return high, mid, (rest - mid.astype(F32)).astype(BF16)


def dot_halves(left_high, left_low, x):
    high, low = halves(x)
    return dot(left_high, high) + (dot(left_high, low) + dot(left_low, high))


def put_first_sides(field, row0, rows, from_left, from_right, c, base=0):
    for got, at, near in ((from_left, 7, NEAR[CS - 3]), (from_right, 38, NEAR[0])):
        for e in range(3):
            k, lane = SMALL_AT[e]
            for i in range(rows):
                row, col = row0 + i, slice(at + e, at + e + 1)
                here = slice(base + i, base + i + 1)
                field[row, col, 0:c] = got[e, here, :]
                if near[e] is not None:
                    field[row, col, c : 2 * c] = got[near[e], here, :]
                field[row, col, 2 * c :] = got[k, here, lane : lane + LANES]


def put_sides(field, row0, rows, from_left, from_right, base=0):
    for e in range(3):
        for i in range(rows):
            field[row0 + i, 7 + e : 8 + e, :] = from_left[e, base + i : base + i + 1, :]
            field[row0 + i, 38 + e : 39 + e, :] = from_right[e, base + i : base + i + 1, :]


def fill_select(order, select):
    for i in range(LOCAL // 64):
        place = lax.broadcasted_iota(jnp.int32, (64, LOCAL), 0) + i * 64
        select[i * 64 : i * 64 + 64, :] = jnp.where(place == order[...], 1.0, 0.0).astype(BF16)


def prepare(
    io,
    guess, right, classes, values, order, basis, coarse_own, tail, head, small, basis_out, select
):
    nclass = values.shape[1]
    fill_select(order, select)
    parts = [p.astype(F32) for p in thirds(basis[...])]
    blank = jnp.zeros((MODES, LOCAL), F32)
    stacked = jnp.concatenate([x for p in parts for x in (p, blank)] + [blank, blank], axis=0)
    got = dot_rows(stacked.astype(BF16), select[...])
    basis_out[...] = got[0:8] + (got[8:16] + got[16:24])
    ones = jnp.ones((8, LOCAL), F32)
    none = jnp.zeros((LANES - INSIDE - 8, LOCAL), F32)
    cells = None
    for k, p in enumerate(parts):
        copies = [p] * 9 + [blank, ones if k == 0 else ones * 0.0, none]
        term = dot_rows(
            select[FIRST : FIRST + OWNROWS, :], jnp.concatenate(copies, axis=0).astype(BF16)
        )
        cells = term if cells is None else cells + term
    small[...] = cells.reshape(CS, ES, LANES)
    conduct = jnp.zeros((CS, CS), F32)
    for k in range(nclass):
        conduct = jnp.where(classes[...] == k, values[0:1, k : k + 1], conduct)
    sub = lax.broadcasted_iota(jnp.int32, (ES, CS), 0)
    lane = lax.broadcasted_iota(jnp.int32, (ES, CS), 1)
    here = lax.broadcasted_iota(jnp.int32, (ES, LANES), 1) == CONDUCT
    for i in range(CS):
        spread = jnp.where(sub == lane + OV, jnp.broadcast_to(conduct[i : i + 1, :], (ES, CS)), 0.0)
        column = jnp.sum(spread, axis=1, keepdims=True)
        small[i] = jnp.where(here, column, small[i])
    rows, cols = coarse_own.shape
    for sent, base in ((tail, CS - 3), (head, 0)):
        sent[5:7] = jnp.zeros((2,) + sent.shape[1:], F32)
        sent[6, 0:rows, LANES : LANES + cols] = coarse_own[...]
        for e in range(3):
            k, at = SMALL_AT[e]
            for i in range(CS):
                j = base + e
                sent[e, i : i + 1, :] = guess[i, j : j + 1, :]
                if NEAR[base][e] is not None:
                    sent[NEAR[base][e], i : i + 1, :] = right[i, j : j + 1, :]
                sent[k, i : i + 1, at : at + LANES] = small[i, OV + j : OV + j + 1, :]
    io.flush(tail, head)


def reorder(io, order, inverse, high_out, low_out, select, rows):
    step = 256
    fill_select(order, select)
    io.wait(0)
    for part, out in ((0, high_out), (1, low_out)):
        for n in range(0, LOCAL, step):
            block = halves(inverse[:, n : n + step])[part]
            rows[:, n : n + step] = dot(select[FIRST : FIRST + OWNROWS, :], block).astype(BF16)
        for n in range(0, LOCAL, step):
            out[:, n : n + step] = dot_rows(rows[...], select[n : n + step, :]).astype(BF16)
        io.flush(out)


def first_rows(io, guess, right, small, from_left, from_right, tail, head):
    c = guess.shape[2]
    for sent, base in ((tail, CS - 3), (head, 0)):
        sent[...] = jnp.zeros(sent.shape, F32)
        for r in range(3):
            sent[r, 10 : 10 + CS, 0:c] = guess[base + r]
            sent[r, 10 : 10 + CS, c : 2 * c] = right[base + r]
            sent[r, 8 : 8 + ES, 2 * c :] = small[base + r]
        put_first_sides(sent, 0, 3, from_left, from_right, c, base)


def field_rows(io, edges, from_left, from_right, tail, head):
    for sent, base in ((tail, CS - 3), (head, 0)):
        sent[...] = jnp.zeros(sent.shape, F32)
        for r in range(3):
            sent[r, 8 : 8 + ES, :] = edges[r + (3 if base else 0)]
        put_sides(sent, 0, 3, from_left, from_right, base)


def stencil(wide, weights, row, lanes, wrow=None):
    diag, up, down, left, right = weights
    k = row if wrow is None else wrow
    return (
        diag[k] * wide[row + 1, 8:40, lanes]
        - up[k] * wide[row, 8:40, lanes]
        - down[k] * wide[row + 2, 8:40, lanes]
        - left[k] * wide[row + 1, 7:39, lanes]
        - right[k] * wide[row + 1, 9:41, lanes]
    )


def solve_and_send(io, window, inverse_high, inverse_low, basis, sums, field, tail, head, sent, edges):
    high, low = halves(window)
    parts = [p.astype(F32) for p in halves(basis[...])]
    table = jnp.concatenate(parts, axis=0).astype(BF16)
    got = dot(table, high)
    rhs = got[0:8] + (got[8:16] + dot(table, low)[0:8])
    line = lax.broadcasted_iota(jnp.int32, rhs.shape, 0)
    if sums is not None:
        rhs = jnp.where(line == 4, sums[0], jnp.where(line == 5, sums[1], rhs))
    for k in range(sent.shape[0]):
        sent[k] = rhs
    io.flush(sent)
    io.wait(2)
    field[...] = (
        dot(inverse_high[...], high) + (dot(inverse_high[...], low) + dot(inverse_low[...], high))
    ).reshape(field.shape)
    io.flush(field)
    if len(tail.shape) == 2:
        for i in range(CS):
            tail[i : i + 1, :] = field[i, CS + OV - 1 : CS + OV, :]
            head[i : i + 1, :] = field[i, OV : OV + 1, :]
        edges[0] = field[0]
        edges[1] = field[CS - 1]
        return
    edges[0:3] = field[0:3]
    edges[3:6] = field[CS - 3 :]
    for e in range(3):
        for i in range(CS):
            tail[e, i : i + 1, :] = field[i, CS + OV - 3 + e : CS + OV - 2 + e, :]
            head[e, i : i + 1, :] = field[i, OV + e : OV + e + 1, :]


def first(
    io,
    guess,
    right,
    small,
    from_left,
    from_right,
    above,
    below,
    basis,
    inverse_high,
    inverse_low,
    of_row,
    of_col,
    diag,
    up,
    down,
    left,
    right_w,
    modes_a_high,
    modes_a_low,
    modes_high,
    modes_low,
    residual,
    field,
    tail,
    head,
    sent,
    edges,
    wide,
    modes,
    window,
):
    c = guess.shape[2]
    for i in range(CS):
        wide[3 + i, 10 : 10 + CS, 0:c] = guess[i]
        wide[3 + i, 8:40, 2 * c :] = small[i]
    for i in range(CS):
        wide[3 + i, 10 : 10 + CS, c : 2 * c] = right[i]
    put_first_sides(wide, 3, CS, from_left, from_right, c)
    wide[0:3] = above[...]
    wide[31:34] = below[...]

    s = 2 * c

    @pl.loop(0, XROWS)
    def _(i):
        modes[i] = jnp.where(of_row[i] * of_col[...] > 0.0, wide[i, :, s : s + LANES], 0.0)

    weights = (diag, up, down, left, right_w)

    @pl.loop(0, ES)
    def _(u):
        def cond(row, at):
            return jnp.broadcast_to(wide[row, at : at + ES, s + CONDUCT : s + CONDUCT + 1], (ES, LANES))

        here = cond(u + 1, 8)
        inside = jnp.broadcast_to(wide[u + 1, 8:40, s + INSIDE : s + INSIDE + 1], (ES, LANES))
        total = jnp.full((ES, LANES), REACTION, F32)
        for ref, row, at in ((up, u, 8), (down, u + 2, 8), (left, u + 1, 7), (right_w, u + 1, 9)):
            face = 0.5 * (here + cond(row, at))
            total = total + face
            ref[u] = face * inside
        diag[u] = total * inside

    @pl.loop(0, ES)
    def _(u):
        for k in range(c // LANES):
            lanes = slice(k * LANES, (k + 1) * LANES)
            there = slice(c + k * LANES, c + (k + 1) * LANES)
            window[u, :, lanes] = wide[u + 1, 8:40, there] - stencil(wide, weights, u, lanes)

    def tables(u, _):
        values = stencil(modes, weights, u, slice(None))
        high, low = halves(values)
        modes_a_high[pl.ds(u * ES, ES), :] = high
        modes_a_low[pl.ds(u * ES, ES), :] = low
        return 0

    lax.fori_loop(0, ES, tables, 0)

    def own_tables(i, _):
        high, low = halves(modes[i + 3, 8:40, :])
        modes_high[pl.ds(i * ES, ES), :] = high
        modes_low[pl.ds(i * ES, ES), :] = low
        return 0

    lax.fori_loop(0, CS, own_tables, 0)
    residual[...] = window[OV : OV + CS]
    io.flush(residual, diag, up, down, left, right_w, modes_a_high, modes_a_low, modes_high, modes_low)
    solve_and_send(
        io,
        window[...].reshape(LOCAL, c),
        inverse_high,
        inverse_low,
        basis,
        None,
        field,
        tail,
        head,
        sent,
        edges,
    )


def partial(io, got, table, out):
    c = got.shape[2]
    out[...] = dot_exact(table[...], got[...].reshape(-1, c)).reshape(out.shape)


def coarse_table(io, before, own, after, pick, spread, ones, out):
    rows, cols = own.shape
    lanes = slice(LANES, LANES + cols)
    stacked = jnp.concatenate([before[6, 0:rows, lanes], own[...], after[6, 0:rows, lanes]], axis=0)
    out[...] = dot_exact(dot_exact(pick[...], stacked), spread[...]) + ones[...]


def summed(got):
    total = got[0]
    for k in range(1, got.shape[0]):
        total = total + got[k]
    return total


def assemble(wide, field, from_left, from_right, above, below):
    wide[3:31, 8:40, :] = field[...]
    put_sides(wide, 3, CS, from_left, from_right)
    wide[0:3] = above[...]
    wide[31:34] = below[...]


def column_mask(lanes):
    col = lax.broadcasted_iota(jnp.int32, (ES, lanes), 0)
    return (col >= OV) & (col < OV + CS)


def spread_coarse(table_high, table_low, coarse):
    high, low = halves(coarse)
    return dot(table_high[...], high) + (dot(table_high[...], low) + dot(table_low[...], high))


def coarse_rows(total):
    rows, c = total.shape
    total = jnp.where(lax.broadcasted_iota(jnp.int32, (rows, c), 0) < NB, total, 0.0)
    return jnp.concatenate([total, jnp.zeros((LANES - rows, c), F32)], axis=0)


def step0(
    io,
    field,
    from_left,
    from_right,
    above,
    below,
    got,
    diag,
    up,
    down,
    left,
    right_w,
    modes_a_high,
    modes_a_low,
    basis,
    inverse_high,
    inverse_low,
    residual,
    image_own,
    coarse,
    field_out,
    tail,
    head,
    sent,
    edges,
    wide,
    window,
):
    weights = (diag, up, down, left, right_w)
    c = field.shape[2]
    assemble(wide, field, from_left, from_right, above, below)
    total = coarse_rows(summed(got))
    coarse[...] = total
    window[...] = spread_coarse(modes_a_high, modes_a_low, total).reshape(window.shape)

    io.wait(0)

    @pl.loop(0, ES)
    def _(u):
        for k in range(c // LANES):
            lanes = slice(k * LANES, (k + 1) * LANES)
            window[u, :, lanes] = window[u, :, lanes] + stencil(wide, weights, u, lanes)

    io.wait(1)
    mask = column_mask(c)

    def reduce(i, carry):
        num, den = carry
        image = jnp.where(mask, window[i + OV], 0.0)
        image_own[i] = image
        return num + residual[i] * image, den + image * image

    zero = jnp.zeros((ES, c), F32)
    num, den = lax.fori_loop(0, CS, reduce, (zero, zero))
    sums = (jnp.sum(num, axis=0, keepdims=True), jnp.sum(den, axis=0, keepdims=True))
    io.flush(image_own, coarse)
    solve_and_send(
        io,
        window[...].reshape(LOCAL, c),
        inverse_high,
        inverse_low,
        basis,
        sums,
        field_out,
        tail,
        head,
        sent,
        edges,
    )


def step1(
    io,
    field,
    from_left,
    from_right,
    above,
    below,
    got,
    diag,
    up,
    down,
    left,
    right_w,
    modes_a_high,
    modes_a_low,
    basis,
    inverse_high,
    inverse_low,
    residual,
    image0,
    image_own,
    coarse,
    field_out,
    tail,
    head,
    sent,
    edges,
    scale_out,
    wide,
    window,
):
    weights = (diag, up, down, left, right_w)
    c = field.shape[2]
    assemble(wide, field, from_left, from_right, above, below)
    total = summed(got)
    scale = total[NB : NB + 1] / total[NB + 1 : NB + 2]
    scale_out[...] = jnp.broadcast_to(scale, scale_out.shape)
    total = coarse_rows(total)
    coarse[...] = total
    window[...] = spread_coarse(modes_a_high, modes_a_low, total).reshape(window.shape)

    io.wait(0)

    @pl.loop(0, ES)
    def _(u):
        for k in range(c // LANES):
            lanes = slice(k * LANES, (k + 1) * LANES)
            window[u, :, lanes] = window[u, :, lanes] + stencil(wide, weights, u, lanes)

    io.wait(1)
    mask = column_mask(c)

    def reduce(i, carry):
        num, den = carry
        before = image0[i]
        mine = jnp.where(mask, window[i + OV], 0.0)
        image_own[i] = mine
        image = before - scale * mine
        left_over = residual[i] - scale * before
        return num + left_over * image, den + image * image

    zero = jnp.zeros((ES, c), F32)
    num, den = lax.fori_loop(0, CS, reduce, (zero, zero))
    sums = (jnp.sum(num, axis=0, keepdims=True), jnp.sum(den, axis=0, keepdims=True))
    io.flush(image_own, coarse)
    solve_and_send(
        io,
        window[...].reshape(LOCAL, c),
        inverse_high,
        inverse_low,
        basis,
        sums,
        field_out,
        tail,
        head,
        sent,
        edges,
    )


def step2(
    io,
    field,
    from_left,
    from_right,
    above,
    below,
    got,
    diag,
    up,
    down,
    left,
    right_w,
    modes_a_high,
    modes_a_low,
    residual,
    image0,
    image1,
    scale_in,
    residual_out,
    image_out,
    coarse,
    sent,
    scale_out,
    wide,
    window,
):
    weights = (diag, up, down, left, right_w)
    c = field.shape[2]
    wide[3:31, 8:40, :] = field[...]
    for i in range(CS):
        wide[3 + i, 9:10, :] = from_left[i : i + 1, :]
        wide[3 + i, 38:39, :] = from_right[i : i + 1, :]
    wide[2, 8:40, :] = above[...]
    wide[31, 8:40, :] = below[...]
    total = summed(got)
    scale = total[NB : NB + 1] / total[NB + 1 : NB + 2]
    scale_out[...] = jnp.broadcast_to(scale, scale_out.shape)
    earlier = scale_in[0:1]
    total = coarse_rows(total)
    coarse[...] = total
    own = slice(FIRST, FIRST + OWNROWS)
    high, low = halves(total)
    table = modes_a_high[own, :]
    window[...] = (
        dot(table, high) + (dot(table, low) + dot(modes_a_low[own, :], high))
    ).reshape(window.shape)
    io.wait(0)
    mask = column_mask(LANES)

    def reduce(i, carry):
        out = []
        for k in range(c // LANES):
            lanes = slice(k * LANES, (k + 1) * LANES)
            num, den = carry[2 * k], carry[2 * k + 1]
            mine = window[i, :, lanes] + stencil(wide, weights, i + OV, lanes)
            mine = jnp.where(mask, mine, 0.0)
            s0 = earlier[:, lanes]
            s1 = scale[:, lanes]
            q0 = image0[i, :, lanes]
            q1 = image1[i, :, lanes]
            before = q0 - s0 * q1
            left_over = residual[i, :, lanes] - s0 * q0 - s1 * before
            image = before - s1 * (q1 - s0 * mine)
            residual_out[i, :, lanes] = left_over
            image_out[i, :, lanes] = image
            out += [num + left_over * image, den + image * image]
        return tuple(out)

    zero = jnp.zeros((ES, LANES), F32)
    sums = lax.fori_loop(0, CS, reduce, (zero,) * (2 * (c // LANES)))
    sums = [jnp.sum(x, axis=0, keepdims=True) for x in sums]
    num = jnp.concatenate(sums[0::2], axis=1)
    den = jnp.concatenate(sums[1::2], axis=1)
    both = jnp.concatenate([num, den], axis=1)
    for k in range(sent.shape[0]):
        sent[k] = both


def resend(io, got, sent):
    total = summed(got)
    for k in range(sent.shape[0]):
        sent[k] = total


def directions(
    io,
    guess,
    field0,
    field1,
    field2,
    coarse0,
    coarse1,
    coarse2,
    modes_high,
    modes_low,
    scale0,
    scale1,
    partial_out,
    last_out,
    p0,
    p1,
    p2,
    change,
):
    for p, coarse, field in ((p0, coarse0, field0), (p1, coarse1, field1), (p2, coarse2, field2)):
        p[...] = spread_coarse(modes_high, modes_low, coarse[...]).reshape(p.shape)
    s0 = scale0[0:1]
    s1 = scale1[0:1]

    @pl.loop(0, CS)
    def _(i):
        first_p = p0[i] + field0[i]
        second = p1[i] + field1[i]
        direction1 = first_p - s0 * second
        direction2 = direction1 - s1 * (second - s0 * (p2[i] + field2[i]))
        change[...] = s0 * first_p + s1 * direction1
        partial_out[i] = guess[i] + change[OV : OV + CS, :]
        last_out[i] = direction2


def finish(io, got, guess_sum, last, residual, image, answer, residual_out):
    total = summed(got)
    c = guess_sum.shape[2]
    scale = total[:, 0:c] / total[:, c:]

    @pl.loop(0, CS)
    def _(i):
        answer[i] = guess_sum[i] + scale * last[i, OV : OV + CS, :]
        residual_out[i] = (
            residual[i, OV : OV + CS, :] - scale * image[i, OV : OV + CS, :]
        )


def mode_tables():
    of_row = np.zeros((XROWS, 1, LANES), np.float32)
    of_col = np.zeros((XCOLS, LANES), np.float32)
    region = [0] * 3 + [1] * CS + [2] * 3
    for db in range(3):
        for da in range(3):
            for m in range(MODES):
                lane = (db * 3 + da) * MODES + m
                for e in range(XROWS):
                    of_row[e, 0, lane] = region[e] == da
                    of_col[7 + e, lane] = region[e] == db
    return of_row, of_col


def coarse_tables(nw, nn):
    pick = np.zeros((nn * SLOT, 3 * nn * MODES), np.float32)
    spread = np.zeros((nw * MODES, nw * 8), np.float32)
    ones = np.zeros((nn * SLOT, nw * 8), np.float32)
    for to in range(nn):
        for db in range(3):
            for da in range(3):
                a = to + da - 1
                for m in range(MODES):
                    if 0 <= a < nn:
                        row = to * SLOT + (db * 3 + da) * MODES + m
                        pick[row, (db * nn + a) * MODES + m] = 1.0
        for b in range(nw):
            ones[to * SLOT + NB, b * 8 + 4] = 1.0
            ones[to * SLOT + NB + 1, b * 8 + 5] = 1.0
    for b in range(nw):
        for m in range(MODES):
            spread[b * MODES + m, b * 8 + m] = 1.0
    return pick, spread, ones


def local(
    right_side,
    initial_guess,
    class_map,
    class_conductivity,
    window_index,
    local_inverse,
    coarse_basis,
    coarse_inverse,
):
    nw = lax.axis_size("wide")
    nn = lax.axis_size("narrow")
    c = right_side.shape[2]
    lanes = 2 * c + LANES
    own = ((CS, ES, c), F32)
    side = ((3, CS, c), F32)
    line = ((CS, c), F32)
    edge = ((6, ES, c), F32)
    rows = ((3, XCOLS, c), F32)
    to_wide = ((nw, 8, c), F32)
    weight = ((ES, ES, LANES), F32)
    extended = pltpu.VMEM((XROWS, XCOLS, c), F32)
    window = pltpu.VMEM((ES, ES, c), F32)
    inverse = ((OWNROWS, LOCAL), BF16)
    of_row, of_col = (jnp.asarray(x) for x in mode_tables())
    pick, coarse_spread, ones = (jnp.asarray(x) for x in coarse_tables(nw, nn))

    def exchange(x, axis):
        return lax.all_to_all(x, axis, 0, 0, tiled=True)

    tail, head, small, basis = call(
        prepare,
        [
            ((7, ES, c), F32),
            ((7, ES, c), F32),
            ((CS, ES, LANES), F32),
            ((8, LOCAL), F32),
        ],
        [
            initial_guess,
            right_side,
            class_map,
            class_conductivity.reshape(1, -1),
            window_index.reshape(1, LOCAL),
            coarse_basis.reshape(MODES, LOCAL),
            coarse_inverse,
        ],
        [pltpu.VMEM((LOCAL, LOCAL), BF16)],
    )
    from_left = shift(tail, "wide", 1)
    from_right = shift(head, "wide", -1)
    inverse_high, inverse_low = call(
        reorder,
        [inverse, inverse],
        [window_index.reshape(1, LOCAL), local_inverse.reshape(LOCAL, LOCAL)],
        [pltpu.VMEM((LOCAL, LOCAL), BF16), pltpu.VMEM((OWNROWS, LOCAL), BF16)],
        late=((1,),),
    )
    tail, head = call(
        first_rows,
        [((3, XCOLS, lanes), F32)] * 2,
        [initial_guess, right_side, small, from_left, from_right],
    )
    above = shift(tail, "narrow", 1)
    below = shift(head, "narrow", -1)
    (table,) = call(
        coarse_table,
        [((nn * SLOT, nw * 8), F32)],
        [from_left, coarse_inverse, from_right, pick, coarse_spread, ones],
    )
    out = call(
        first,
        [weight] * 5
        + [((LOCAL, LANES), BF16)] * 2
        + [((OWNROWS, LANES), BF16)] * 2
        + [own, own, side, side, to_wide, edge],
        [
            initial_guess,
            right_side,
            small,
            from_left,
            from_right,
            above,
            below,
            basis,
            inverse_high,
            inverse_low,
            of_row,
            of_col,
        ],
        [
            pltpu.VMEM((XROWS, XCOLS, lanes), F32),
            pltpu.VMEM((XROWS, XCOLS, LANES), F32),
            window,
        ],
        late=((), (), (8, 9)),
    )
    weights = out[:5]
    modes_a = out[5:7]
    modes = out[7:9]
    residual, field0, tail, head, sent, edges = out[9:]

    def coarse(sent, edges, tail, head):
        got = exchange(sent, "wide")
        from_left = shift(tail, "wide", 1)
        from_right = shift(head, "wide", -1)
        tail, head = call(field_rows, [rows, rows], [edges, from_left, from_right])
        (parts,) = call(partial, [((nn, SLOT, c), F32)], [got, table])
        parts, tail, head = lax.optimization_barrier((parts, tail, head))
        above = shift(tail, "narrow", 1)
        below = shift(head, "narrow", -1)
        return (from_left, from_right, above, below), exchange(parts, "narrow")

    solver = [basis, inverse_high, inverse_low, residual]
    coarse_out = ((LANES, c), F32)
    scale_out = ((8, c), F32)
    near, got = coarse(sent, edges, tail, head)
    image0, coarse0, field1, tail, head, sent, edges = call(
        step0,
        [own, coarse_out, own, side, side, to_wide, edge],
        [field0, *near, got, *weights, *modes_a, *solver],
        [extended, window],
        late=((6, 7, 8, 9, 10), (13, 16), (14, 15)),
    )
    near, got = coarse(sent, edges, tail, head)
    image1, coarse1, field2, tail, head, sent, edges, scale0 = call(
        step1,
        [own, coarse_out, own, line, line, to_wide, ((2, ES, c), F32), scale_out],
        [field1, *near, got, *weights, *modes_a, *solver, image0],
        [extended, window],
        late=((6, 7, 8, 9, 10), (13, 16, 17), (14, 15)),
    )
    got = exchange(sent, "wide")
    near = (
        shift(tail, "wide", 1),
        shift(head, "wide", -1),
        shift(edges[1], "narrow", 1),
        shift(edges[0], "narrow", -1),
    )
    got, near = lax.optimization_barrier((got, near))
    (parts,) = call(partial, [((nn, SLOT, c), F32)], [got, table])
    got = exchange(parts, "narrow")
    residual, image, coarse2, sent, scale1 = call(
        step2,
        [own, own, coarse_out, ((nn, 1, 2 * c), F32), scale_out],
        [field2, *near, got, *weights, *modes_a, residual, image0, image1, scale0],
        [extended, pltpu.VMEM((CS, ES, c), F32)],
        late=((6, 7, 8, 9, 10, 13, 14, 15),),
    )
    got = exchange(sent, "narrow")
    (sent,) = call(resend, [((nw, 1, 2 * c), F32)], [got])
    got = exchange(sent, "wide")
    before_last, last = call(
        directions,
        [((CS, CS, c), F32), own],
        [initial_guess, field0, field1, field2, coarse0, coarse1, coarse2, *modes, scale0, scale1],
        [pltpu.VMEM((CS, ES, c), F32)] * 3 + [pltpu.VMEM((ES, c), F32)],
    )
    return tuple(
        call(
            finish,
            [((CS, CS, c), F32)] * 2,
            [got, before_last, last, residual, image],
        )
    )


def solution(mesh):
    in_specs = (
        P("narrow", "wide", None),
        P("narrow", "wide", None),
        P("narrow", "wide"),
        P(),
        P("narrow", "wide", None),
        P("narrow", "wide", None, None),
        P("narrow", "wide", None, None),
        P("wide", "narrow"),
    )
    out_specs = (P("narrow", "wide", None), P("narrow", "wide", None))
    return jax.shard_map(local, mesh=mesh, in_specs=in_specs, out_specs=out_specs, check_vma=False)
```

```python
import functools

import jax
import jax.numpy as jnp
import numpy as np
from jax import lax
from jax.experimental import pallas as pl
from jax.experimental.pallas import tpu as pltpu
from jax.sharding import PartitionSpec as P

OV = 2
MODES = 4
CS = 28
ES = CS + 2 * OV
LOCAL = ES * ES
LANES = 128
XROWS = ES + 2
XCOLS = 48
OWNROWS = CS * ES
FIRST = OV * ES
SLOT = 40
NB = 9 * MODES
INSIDE = NB + MODES
SMALL_AT = ((5, 0), (5, LANES), (6, 0))
NEAR = {CS - 3: (None, 3, 4), 0: (3, 4, None)}
CONDUCT = LANES - 1

HIGHEST = lax.Precision.HIGHEST
REACTION = 0.01
F32 = jnp.float32
BF16 = jnp.bfloat16
VMEM_LIMIT = 60 * 2**20


def shift(x, axis, step):
    count = lax.axis_size(axis)
    return lax.ppermute(x, axis, [(i, i + step) for i in range(count) if 0 <= i + step < count])


class Copies:
    def __init__(self, buffers, places, sems):
        self.buffers = buffers
        self.copies = [
            pltpu.make_async_copy(b, p, sems.at[k]) for k, (b, p) in enumerate(zip(buffers, places))
        ]
        self.started = [False] * len(buffers)
        self.wait = None

    def flush(self, *refs):
        for k, buffer in enumerate(self.buffers):
            if not self.started[k] and (not refs or any(buffer is r for r in refs)):
                self.copies[k].start()
                self.started[k] = True

    def close(self):
        self.flush()
        for copy in self.copies:
            copy.wait()


def call(body, out, args, scratch=(), late=()):
    delayed = [k for group in late for k in group]
    na, no = len(args), len(out)

    def kernel(*refs):
        sources, places = refs[:na], refs[na : na + no]
        refs = refs[na + no :]
        inputs, buffers, refs = refs[:na], refs[na : na + no], refs[na + no :]
        extra, sems_in, sems_out = refs[:-2], refs[-2], refs[-1]
        copies = [pltpu.make_async_copy(sources[k], inputs[k], sems_in.at[k]) for k in range(na)]
        early = [k for k in range(na) if k not in delayed]
        for k in early + delayed:
            copies[k].start()
        for k in early:
            copies[k].wait()

        def wait(group):
            for k in late[group]:
                copies[k].wait()

        io = Copies(buffers, places, sems_out)
        io.wait = wait
        body(io, *inputs, *buffers, *extra)
        io.close()

    spec = pl.BlockSpec(memory_space=pl.ANY)
    return pl.pallas_call(
        kernel,
        out_shape=[jax.ShapeDtypeStruct(shape, kind) for shape, kind in out],
        in_specs=[spec] * na,
        out_specs=[spec] * no,
        scratch_shapes=[pltpu.VMEM(x.shape, x.dtype) for x in args]
        + [pltpu.VMEM(shape, kind) for shape, kind in out]
        + list(scratch)
        + [pltpu.SemaphoreType.DMA((na,)), pltpu.SemaphoreType.DMA((no,))],
        compiler_params=pltpu.CompilerParams(vmem_limit_bytes=VMEM_LIMIT),
    )(*args)


def dot(a, b):
    return jnp.dot(a, b, preferred_element_type=F32)


def dot_rows(a, b):
    return lax.dot_general(a, b, (((1,), (1,)), ((), ())), preferred_element_type=F32)


def dot_exact(a, b):
    return jnp.dot(a, b, precision=HIGHEST, preferred_element_type=F32)


def halves(x):
    high = x.astype(BF16)
    return high, (x - high.astype(F32)).astype(BF16)


def thirds(x):
    high = x.astype(BF16)
    rest = x - high.astype(F32)
    mid = rest.astype(BF16)
    return high, mid, (rest - mid.astype(F32)).astype(BF16)


def dot_halves(left_high, left_low, x):
    high, low = halves(x)
    return dot(left_high, high) + (dot(left_high, low) + dot(left_low, high))


def put_first_sides(field, row0, rows, from_left, from_right, c, base=0):
    for got, at, near in ((from_left, 7, NEAR[CS - 3]), (from_right, 38, NEAR[0])):
        for e in range(3):
            k, lane = SMALL_AT[e]
            for i in range(rows):
                row, col = row0 + i, slice(at + e, at + e + 1)
                here = slice(base + i, base + i + 1)
                field[row, col, 0:c] = got[e, here, :]
                if near[e] is not None:
                    field[row, col, c : 2 * c] = got[near[e], here, :]
                field[row, col, 2 * c :] = got[k, here, lane : lane + LANES]


def put_sides(field, row0, rows, from_left, from_right, base=0):
    for e in range(3):
        for i in range(rows):
            field[row0 + i, 7 + e : 8 + e, :] = from_left[e, base + i : base + i + 1, :]
            field[row0 + i, 38 + e : 39 + e, :] = from_right[e, base + i : base + i + 1, :]


def fill_select(order, select):
    for i in range(LOCAL // 64):
        place = lax.broadcasted_iota(jnp.int32, (64, LOCAL), 0) + i * 64
        select[i * 64 : i * 64 + 64, :] = jnp.where(place == order[...], 1.0, 0.0).astype(BF16)


def prepare(
    io,
    guess, right, classes, values, order, basis, coarse_own, tail, head, small, basis_out, select
):
    nclass = values.shape[1]
    fill_select(order, select)
    parts = [p.astype(F32) for p in thirds(basis[...])]
    blank = jnp.zeros((MODES, LOCAL), F32)
    stacked = jnp.concatenate([x for p in parts for x in (p, blank)] + [blank, blank], axis=0)
    got = dot_rows(stacked.astype(BF16), select[...])
    basis_out[...] = got[0:8] + (got[8:16] + got[16:24])
    ones = jnp.ones((8, LOCAL), F32)
    none = jnp.zeros((LANES - INSIDE - 8, LOCAL), F32)
    cells = None
    for k, p in enumerate(parts):
        copies = [p] * 9 + [blank, ones if k == 0 else ones * 0.0, none]
        term = dot_rows(
            select[FIRST : FIRST + OWNROWS, :], jnp.concatenate(copies, axis=0).astype(BF16)
        )
        cells = term if cells is None else cells + term
    small[...] = cells.reshape(CS, ES, LANES)
    conduct = jnp.zeros((CS, CS), F32)
    for k in range(nclass):
        conduct = jnp.where(classes[...] == k, values[0:1, k : k + 1], conduct)
    sub = lax.broadcasted_iota(jnp.int32, (ES, CS), 0)
    lane = lax.broadcasted_iota(jnp.int32, (ES, CS), 1)
    here = lax.broadcasted_iota(jnp.int32, (ES, LANES), 1) == CONDUCT
    for i in range(CS):
        spread = jnp.where(sub == lane + OV, jnp.broadcast_to(conduct[i : i + 1, :], (ES, CS)), 0.0)
        column = jnp.sum(spread, axis=1, keepdims=True)
        small[i] = jnp.where(here, column, small[i])
    rows, cols = coarse_own.shape
    for sent, base in ((tail, CS - 3), (head, 0)):
        sent[5:7] = jnp.zeros((2,) + sent.shape[1:], F32)
        sent[6, 0:rows, LANES : LANES + cols] = coarse_own[...]
        for e in range(3):
            k, at = SMALL_AT[e]
            for i in range(CS):
                j = base + e
                sent[e, i : i + 1, :] = guess[i, j : j + 1, :]
                if NEAR[base][e] is not None:
                    sent[NEAR[base][e], i : i + 1, :] = right[i, j : j + 1, :]
                sent[k, i : i + 1, at : at + LANES] = small[i, OV + j : OV + j + 1, :]
    io.flush(tail, head)


def reorder(part, io, order, inverse, out, select, rows):
    step = 256
    fill_select(order, select)
    io.wait(0)
    for n in range(0, LOCAL, step):
        block = halves(inverse[:, n : n + step])[part]
        rows[:, n : n + step] = dot(select[FIRST : FIRST + OWNROWS, :], block).astype(BF16)
    for n in range(0, LOCAL, step):
        out[:, n : n + step] = dot_rows(rows[...], select[n : n + step, :]).astype(BF16)


def first_rows(io, guess, right, small, from_left, from_right, tail, head):
    c = guess.shape[2]
    for sent, base in ((tail, CS - 3), (head, 0)):
        sent[...] = jnp.zeros(sent.shape, F32)
        for r in range(3):
            sent[r, 10 : 10 + CS, 0:c] = guess[base + r]
            sent[r, 10 : 10 + CS, c : 2 * c] = right[base + r]
            sent[r, 8 : 8 + ES, 2 * c :] = small[base + r]
        put_first_sides(sent, 0, 3, from_left, from_right, c, base)


def field_rows(io, edges, from_left, from_right, tail, head):
    for sent, base in ((tail, CS - 3), (head, 0)):
        sent[...] = jnp.zeros(sent.shape, F32)
        for r in range(3):
            sent[r, 8 : 8 + ES, :] = edges[r + (3 if base else 0)]
        put_sides(sent, 0, 3, from_left, from_right, base)


def stencil(wide, weights, row, lanes, wrow=None):
    diag, up, down, left, right = weights
    k = row if wrow is None else wrow
    return (
        diag[k] * wide[row + 1, 8:40, lanes]
        - up[k] * wide[row, 8:40, lanes]
        - down[k] * wide[row + 2, 8:40, lanes]
        - left[k] * wide[row + 1, 7:39, lanes]
        - right[k] * wide[row + 1, 9:41, lanes]
    )


def solve_and_send(io, window, inverse_high, inverse_low, basis, sums, field, tail, head, sent, edges):
    high, low = halves(window)
    parts = [p.astype(F32) for p in halves(basis[...])]
    table = jnp.concatenate(parts, axis=0).astype(BF16)
    got = dot(table, high)
    rhs = got[0:8] + (got[8:16] + dot(table, low)[0:8])
    line = lax.broadcasted_iota(jnp.int32, rhs.shape, 0)
    if sums is not None:
        rhs = jnp.where(line == 4, sums[0], jnp.where(line == 5, sums[1], rhs))
    for k in range(sent.shape[0]):
        sent[k] = rhs
    io.flush(sent)
    io.wait(2)
    field[...] = (
        dot(inverse_high[...], high) + (dot(inverse_high[...], low) + dot(inverse_low[...], high))
    ).reshape(field.shape)
    io.flush(field)
    if len(tail.shape) == 2:
        for i in range(CS):
            tail[i : i + 1, :] = field[i, CS + OV - 1 : CS + OV, :]
            head[i : i + 1, :] = field[i, OV : OV + 1, :]
        edges[0] = field[0]
        edges[1] = field[CS - 1]
        return
    edges[0:3] = field[0:3]
    edges[3:6] = field[CS - 3 :]
    for e in range(3):
        for i in range(CS):
            tail[e, i : i + 1, :] = field[i, CS + OV - 3 + e : CS + OV - 2 + e, :]
            head[e, i : i + 1, :] = field[i, OV + e : OV + e + 1, :]


def first(
    io,
    guess,
    right,
    small,
    from_left,
    from_right,
    above,
    below,
    basis,
    inverse_high,
    inverse_low,
    of_row,
    of_col,
    diag,
    up,
    down,
    left,
    right_w,
    modes_a_high,
    modes_a_low,
    modes_high,
    modes_low,
    residual,
    field,
    tail,
    head,
    sent,
    edges,
    wide,
    modes,
    window,
):
    c = guess.shape[2]
    for i in range(CS):
        wide[3 + i, 10 : 10 + CS, 0:c] = guess[i]
        wide[3 + i, 8:40, 2 * c :] = small[i]
    for i in range(CS):
        wide[3 + i, 10 : 10 + CS, c : 2 * c] = right[i]
    put_first_sides(wide, 3, CS, from_left, from_right, c)
    wide[0:3] = above[...]
    wide[31:34] = below[...]

    s = 2 * c

    @pl.loop(0, XROWS, unroll=2)
    def _(i):
        modes[i] = jnp.where(of_row[i] * of_col[...] > 0.0, wide[i, :, s : s + LANES], 0.0)

    weights = (diag, up, down, left, right_w)

    @pl.loop(0, ES, unroll=4)
    def _(u):
        def cond(row, at):
            return jnp.broadcast_to(wide[row, at : at + ES, s + CONDUCT : s + CONDUCT + 1], (ES, LANES))

        here = cond(u + 1, 8)
        inside = jnp.broadcast_to(wide[u + 1, 8:40, s + INSIDE : s + INSIDE + 1], (ES, LANES))
        total = jnp.full((ES, LANES), REACTION, F32)
        for ref, row, at in ((up, u, 8), (down, u + 2, 8), (left, u + 1, 7), (right_w, u + 1, 9)):
            face = 0.5 * (here + cond(row, at))
            total = total + face
            ref[u] = face * inside
        diag[u] = total * inside

    @pl.loop(0, ES, unroll=4)
    def _(u):
        for k in range(c // LANES):
            lanes = slice(k * LANES, (k + 1) * LANES)
            there = slice(c + k * LANES, c + (k + 1) * LANES)
            window[u, :, lanes] = wide[u + 1, 8:40, there] - stencil(wide, weights, u, lanes)

    def tables(u, _):
        values = stencil(modes, weights, u, slice(None))
        high, low = halves(values)
        modes_a_high[pl.ds(u * ES, ES), :] = high
        modes_a_low[pl.ds(u * ES, ES), :] = low
        return 0

    lax.fori_loop(0, ES, tables, 0, unroll=2)

    def own_tables(i, _):
        high, low = halves(modes[i + 3, 8:40, :])
        modes_high[pl.ds(i * ES, ES), :] = high
        modes_low[pl.ds(i * ES, ES), :] = low
        return 0

    lax.fori_loop(0, CS, own_tables, 0, unroll=2)
    residual[...] = window[OV : OV + CS]
    io.flush(residual, diag, up, down, left, right_w, modes_a_high, modes_a_low, modes_high, modes_low)
    solve_and_send(
        io,
        window[...].reshape(LOCAL, c),
        inverse_high,
        inverse_low,
        basis,
        None,
        field,
        tail,
        head,
        sent,
        edges,
    )


def partial(io, got, table, out):
    c = got.shape[2]
    out[...] = dot_exact(table[...], got[...].reshape(-1, c)).reshape(out.shape)


def coarse_table(io, before, own, after, pick, spread, ones, out):
    rows, cols = own.shape
    lanes = slice(LANES, LANES + cols)
    stacked = jnp.concatenate([before[6, 0:rows, lanes], own[...], after[6, 0:rows, lanes]], axis=0)
    out[...] = dot_exact(dot_exact(pick[...], stacked), spread[...]) + ones[...]


def summed(got):
    total = got[0]
    for k in range(1, got.shape[0]):
        total = total + got[k]
    return total


def assemble(wide, field, from_left, from_right, above, below):
    wide[3:31, 8:40, :] = field[...]
    put_sides(wide, 3, CS, from_left, from_right)
    wide[0:3] = above[...]
    wide[31:34] = below[...]


def column_mask(lanes):
    col = lax.broadcasted_iota(jnp.int32, (ES, lanes), 0)
    return (col >= OV) & (col < OV + CS)


def spread_coarse(table_high, table_low, coarse):
    high, low = halves(coarse)
    return dot(table_high[...], high) + (dot(table_high[...], low) + dot(table_low[...], high))


def coarse_rows(total):
    rows, c = total.shape
    total = jnp.where(lax.broadcasted_iota(jnp.int32, (rows, c), 0) < NB, total, 0.0)
    return jnp.concatenate([total, jnp.zeros((LANES - rows, c), F32)], axis=0)


def step0(
    io,
    field,
    from_left,
    from_right,
    above,
    below,
    got,
    diag,
    up,
    down,
    left,
    right_w,
    modes_a_high,
    modes_a_low,
    basis,
    inverse_high,
    inverse_low,
    residual,
    image_own,
    coarse,
    field_out,
    tail,
    head,
    sent,
    edges,
    wide,
    window,
):
    weights = (diag, up, down, left, right_w)
    c = field.shape[2]
    assemble(wide, field, from_left, from_right, above, below)
    total = coarse_rows(summed(got))
    coarse[...] = total
    window[...] = spread_coarse(modes_a_high, modes_a_low, total).reshape(window.shape)

    io.wait(0)

    @pl.loop(0, ES, unroll=4)
    def _(u):
        for k in range(c // LANES):
            lanes = slice(k * LANES, (k + 1) * LANES)
            window[u, :, lanes] = window[u, :, lanes] + stencil(wide, weights, u, lanes)

    io.wait(1)
    mask = column_mask(c)

    def reduce(i, carry):
        num, den = carry
        image = jnp.where(mask, window[i + OV], 0.0)
        image_own[i] = image
        return num + residual[i] * image, den + image * image

    zero = jnp.zeros((ES, c), F32)
    num, den = lax.fori_loop(0, CS, reduce, (zero, zero), unroll=2)
    sums = (jnp.sum(num, axis=0, keepdims=True), jnp.sum(den, axis=0, keepdims=True))
    io.flush(image_own, coarse)
    solve_and_send(
        io,
        window[...].reshape(LOCAL, c),
        inverse_high,
        inverse_low,
        basis,
        sums,
        field_out,
        tail,
        head,
        sent,
        edges,
    )


def step1(
    io,
    field,
    from_left,
    from_right,
    above,
    below,
    got,
    diag,
    up,
    down,
    left,
    right_w,
    modes_a_high,
    modes_a_low,
    basis,
    inverse_high,
    inverse_low,
    residual,
    image0,
    image_own,
    coarse,
    field_out,
    tail,
    head,
    sent,
    edges,
    scale_out,
    wide,
    window,
):
    weights = (diag, up, down, left, right_w)
    c = field.shape[2]
    assemble(wide, field, from_left, from_right, above, below)
    total = summed(got)
    scale = total[NB : NB + 1] / total[NB + 1 : NB + 2]
    scale_out[...] = jnp.broadcast_to(scale, scale_out.shape)
    total = coarse_rows(total)
    coarse[...] = total
    window[...] = spread_coarse(modes_a_high, modes_a_low, total).reshape(window.shape)

    io.wait(0)

    @pl.loop(0, ES, unroll=4)
    def _(u):
        for k in range(c // LANES):
            lanes = slice(k * LANES, (k + 1) * LANES)
            window[u, :, lanes] = window[u, :, lanes] + stencil(wide, weights, u, lanes)

    io.wait(1)
    mask = column_mask(c)

    def reduce(i, carry):
        num, den = carry
        before = image0[i]
        mine = jnp.where(mask, window[i + OV], 0.0)
        image_own[i] = mine
        image = before - scale * mine
        left_over = residual[i] - scale * before
        return num + left_over * image, den + image * image

    zero = jnp.zeros((ES, c), F32)
    num, den = lax.fori_loop(0, CS, reduce, (zero, zero), unroll=2)
    sums = (jnp.sum(num, axis=0, keepdims=True), jnp.sum(den, axis=0, keepdims=True))
    io.flush(image_own, coarse)
    solve_and_send(
        io,
        window[...].reshape(LOCAL, c),
        inverse_high,
        inverse_low,
        basis,
        sums,
        field_out,
        tail,
        head,
        sent,
        edges,
    )


def step2(
    io,
    field,
    from_left,
    from_right,
    above,
    below,
    got,
    diag,
    up,
    down,
    left,
    right_w,
    modes_a_high,
    modes_a_low,
    residual,
    image0,
    image1,
    scale_in,
    residual_out,
    image_out,
    coarse,
    sent,
    scale_out,
    wide,
    window,
):
    weights = (diag, up, down, left, right_w)
    c = field.shape[2]
    wide[3:31, 8:40, :] = field[...]
    for i in range(CS):
        wide[3 + i, 9:10, :] = from_left[i : i + 1, :]
        wide[3 + i, 38:39, :] = from_right[i : i + 1, :]
    wide[2, 8:40, :] = above[...]
    wide[31, 8:40, :] = below[...]
    total = summed(got)
    scale = total[NB : NB + 1] / total[NB + 1 : NB + 2]
    scale_out[...] = jnp.broadcast_to(scale, scale_out.shape)
    earlier = scale_in[0:1]
    total = coarse_rows(total)
    coarse[...] = total
    own = slice(FIRST, FIRST + OWNROWS)
    high, low = halves(total)
    table = modes_a_high[own, :]
    window[...] = (
        dot(table, high) + (dot(table, low) + dot(modes_a_low[own, :], high))
    ).reshape(window.shape)
    io.wait(0)
    mask = column_mask(LANES)

    def reduce(i, carry):
        out = []
        for k in range(c // LANES):
            lanes = slice(k * LANES, (k + 1) * LANES)
            num, den = carry[2 * k], carry[2 * k + 1]
            mine = window[i, :, lanes] + stencil(wide, weights, i + OV, lanes)
            mine = jnp.where(mask, mine, 0.0)
            s0 = earlier[:, lanes]
            s1 = scale[:, lanes]
            q0 = image0[i, :, lanes]
            q1 = image1[i, :, lanes]
            before = q0 - s0 * q1
            left_over = residual[i, :, lanes] - s0 * q0 - s1 * before
            image = before - s1 * (q1 - s0 * mine)
            residual_out[i, :, lanes] = left_over
            image_out[i, :, lanes] = image
            out += [num + left_over * image, den + image * image]
        return tuple(out)

    zero = jnp.zeros((ES, LANES), F32)
    sums = lax.fori_loop(0, CS, reduce, (zero,) * (2 * (c // LANES)), unroll=2)
    sums = [jnp.sum(x, axis=0, keepdims=True) for x in sums]
    num = jnp.concatenate(sums[0::2], axis=1)
    den = jnp.concatenate(sums[1::2], axis=1)
    both = jnp.concatenate([num, den], axis=1)
    for k in range(sent.shape[0]):
        sent[k] = both


def resend(io, got, sent):
    total = summed(got)
    for k in range(sent.shape[0]):
        sent[k] = total


def early_directions(
    io,
    guess,
    field0,
    field1,
    coarse0,
    coarse1,
    modes_high,
    modes_low,
    scale0,
    base_out,
    direction_out,
    second_out,
    p0,
    p1,
    change,
):
    for p, coarse in ((p0, coarse0), (p1, coarse1)):
        p[...] = spread_coarse(modes_high, modes_low, coarse[...]).reshape(p.shape)
    s0 = scale0[0:1]

    @pl.loop(0, CS, unroll=2)
    def _(i):
        first_p = p0[i] + field0[i]
        second = p1[i] + field1[i]
        direction_out[i] = first_p - s0 * second
        second_out[i] = second
        change[i] = s0 * first_p
        base_out[i] = guess[i] + change[i, OV : OV + CS, :]


def late_directions(
    io,
    base,
    direction,
    second,
    field2,
    coarse2,
    modes_high,
    modes_low,
    scale0,
    scale1,
    partial_out,
    last_out,
    p2,
):
    p2[...] = spread_coarse(modes_high, modes_low, coarse2[...]).reshape(p2.shape)
    s0 = scale0[0:1]
    s1 = scale1[0:1]

    @pl.loop(0, CS, unroll=2)
    def _(i):
        last_out[i] = direction[i] - s1 * (second[i] - s0 * (p2[i] + field2[i]))
        partial_out[i] = base[i] + s1 * direction[i, OV : OV + CS, :]


def finish(io, got, guess_sum, last, residual, image, answer, residual_out):
    total = summed(got)
    c = guess_sum.shape[2]
    scale = total[:, 0:c] / total[:, c:]

    @pl.loop(0, CS, unroll=4)
    def _(i):
        answer[i] = guess_sum[i] + scale * last[i, OV : OV + CS, :]
        residual_out[i] = (
            residual[i, OV : OV + CS, :] - scale * image[i, OV : OV + CS, :]
        )


def mode_tables():
    of_row = np.zeros((XROWS, 1, LANES), np.float32)
    of_col = np.zeros((XCOLS, LANES), np.float32)
    region = [0] * 3 + [1] * CS + [2] * 3
    for db in range(3):
        for da in range(3):
            for m in range(MODES):
                lane = (db * 3 + da) * MODES + m
                for e in range(XROWS):
                    of_row[e, 0, lane] = region[e] == da
                    of_col[7 + e, lane] = region[e] == db
    return of_row, of_col


def coarse_tables(nw, nn):
    pick = np.zeros((nn * SLOT, 3 * nn * MODES), np.float32)
    spread = np.zeros((nw * MODES, nw * 8), np.float32)
    ones = np.zeros((nn * SLOT, nw * 8), np.float32)
    for to in range(nn):
        for db in range(3):
            for da in range(3):
                a = to + da - 1
                for m in range(MODES):
                    if 0 <= a < nn:
                        row = to * SLOT + (db * 3 + da) * MODES + m
                        pick[row, (db * nn + a) * MODES + m] = 1.0
        for b in range(nw):
            ones[to * SLOT + NB, b * 8 + 4] = 1.0
            ones[to * SLOT + NB + 1, b * 8 + 5] = 1.0
    for b in range(nw):
        for m in range(MODES):
            spread[b * MODES + m, b * 8 + m] = 1.0
    return pick, spread, ones


def local(
    right_side,
    initial_guess,
    class_map,
    class_conductivity,
    window_index,
    local_inverse,
    coarse_basis,
    coarse_inverse,
):
    nw = lax.axis_size("wide")
    nn = lax.axis_size("narrow")
    c = right_side.shape[2]
    lanes = 2 * c + LANES
    own = ((CS, ES, c), F32)
    side = ((3, CS, c), F32)
    line = ((CS, c), F32)
    edge = ((6, ES, c), F32)
    rows = ((3, XCOLS, c), F32)
    to_wide = ((nw, 8, c), F32)
    weight = ((ES, ES, LANES), F32)
    extended = pltpu.VMEM((XROWS, XCOLS, c), F32)
    window = pltpu.VMEM((ES, ES, c), F32)
    inverse = ((OWNROWS, LOCAL), BF16)
    of_row, of_col = (jnp.asarray(x) for x in mode_tables())
    pick, coarse_spread, ones = (jnp.asarray(x) for x in coarse_tables(nw, nn))

    def exchange(x, axis):
        return lax.all_to_all(x, axis, 0, 0, tiled=True)

    def within(x, groups):
        return lax.all_to_all(
            x, ("wide", "narrow"), 0, 0, axis_index_groups=groups, tiled=True
        )

    tail, head, small, basis = call(
        prepare,
        [
            ((7, ES, c), F32),
            ((7, ES, c), F32),
            ((CS, ES, LANES), F32),
            ((8, LOCAL), F32),
        ],
        [
            initial_guess,
            right_side,
            class_map,
            class_conductivity.reshape(1, -1),
            window_index.reshape(1, LOCAL),
            coarse_basis.reshape(MODES, LOCAL),
            coarse_inverse,
        ],
        [pltpu.VMEM((LOCAL, LOCAL), BF16)],
    )
    from_left = shift(tail, "wide", 1)
    from_right = shift(head, "wide", -1)
    inverse_high, inverse_low = [
        call(
            functools.partial(reorder, part),
            [inverse],
            [window_index.reshape(1, LOCAL), local_inverse.reshape(LOCAL, LOCAL)],
            [pltpu.VMEM((LOCAL, LOCAL), BF16), pltpu.VMEM((OWNROWS, LOCAL), BF16)],
            late=((1,),),
        )[0]
        for part in range(2)
    ]
    from_left, from_right, inverse_high = lax.optimization_barrier(
        (from_left, from_right, inverse_high)
    )
    tail, head = call(
        first_rows,
        [((3, XCOLS, lanes), F32)] * 2,
        [initial_guess, right_side, small, from_left, from_right],
    )
    above = shift(tail, "narrow", 1)
    below = shift(head, "narrow", -1)
    (table,) = call(
        coarse_table,
        [((nn * SLOT, nw * 8), F32)],
        [from_left, coarse_inverse, from_right, pick, coarse_spread, ones],
    )
    out = call(
        first,
        [weight] * 5
        + [((LOCAL, LANES), BF16)] * 2
        + [((OWNROWS, LANES), BF16)] * 2
        + [own, own, side, side, to_wide, edge],
        [
            initial_guess,
            right_side,
            small,
            from_left,
            from_right,
            above,
            below,
            basis,
            inverse_high,
            inverse_low,
            of_row,
            of_col,
        ],
        [
            pltpu.VMEM((XROWS, XCOLS, lanes), F32),
            pltpu.VMEM((XROWS, XCOLS, LANES), F32),
            window,
        ],
        late=((), (), (8, 9)),
    )
    weights = out[:5]
    modes_a = out[5:7]
    modes = out[7:9]
    residual, field0, tail, head, sent, edges = out[9:]

    def coarse(sent, edges, tail, head):
        got = exchange(sent, "wide")
        from_left = shift(tail, "wide", 1)
        from_right = shift(head, "wide", -1)
        (parts,) = call(partial, [((nn, SLOT, c), F32)], [got, table])
        parts, from_left, from_right = lax.optimization_barrier((parts, from_left, from_right))
        tail, head = call(field_rows, [rows, rows], [edges, from_left, from_right])
        above = shift(tail, "narrow", 1)
        below = shift(head, "narrow", -1)
        return (from_left, from_right, above, below), exchange(parts, "narrow")

    solver = [basis, inverse_high, inverse_low, residual]
    coarse_out = ((LANES, c), F32)
    scale_out = ((8, c), F32)
    near, got = coarse(sent, edges, tail, head)
    image0, coarse0, field1, tail, head, sent, edges = call(
        step0,
        [own, coarse_out, own, side, side, to_wide, edge],
        [field0, *near, got, *weights, *modes_a, *solver],
        [extended, window],
        late=((6, 7, 8, 9, 10), (13, 16), (14, 15)),
    )
    near, got = coarse(sent, edges, tail, head)
    image1, coarse1, field2, tail, head, sent, edges, scale0 = call(
        step1,
        [own, coarse_out, own, line, line, to_wide, ((2, ES, c), F32), scale_out],
        [field1, *near, got, *weights, *modes_a, *solver, image0],
        [extended, window],
        late=((6, 7, 8, 9, 10), (13, 16, 17), (14, 15)),
    )
    got = exchange(sent, "wide")
    near = (
        shift(tail, "wide", 1),
        shift(head, "wide", -1),
        shift(edges[1], "narrow", 1),
        shift(edges[0], "narrow", -1),
    )
    got, near = lax.optimization_barrier((got, near))
    (parts,) = call(partial, [((nn, SLOT, c), F32)], [got, table])
    early = call(
        early_directions,
        [((CS, CS, c), F32), own, own],
        [initial_guess, field0, field1, coarse0, coarse1, *modes, scale0],
        [pltpu.VMEM((CS, ES, c), F32)] * 3,
    )
    got = exchange(parts, "narrow")
    got, early = lax.optimization_barrier((got, early))
    residual, image, coarse2, sent, scale1 = call(
        step2,
        [own, own, coarse_out, ((2 * nn, 1, 2 * c), F32), scale_out],
        [field2, *near, got, *weights, *modes_a, residual, image0, image1, scale0],
        [extended, pltpu.VMEM((CS, ES, c), F32)],
        late=((6, 7, 8, 9, 10, 13, 14, 15),),
    )
    group = 2 * nn
    count = nw // 2
    inner = [[k * group + r for r in range(group)] for k in range(count)]
    outer = [[k * group + r for k in range(count)] for r in range(group)]
    got = within(sent, inner)
    (sent,) = call(resend, [((count, 1, 2 * c), F32)], [got])
    got = within(sent, outer)
    before_last, last = call(
        late_directions,
        [((CS, CS, c), F32), own],
        [*early, field2, coarse2, *modes, scale0, scale1],
        [pltpu.VMEM((CS, ES, c), F32)],
    )
    return tuple(
        call(
            finish,
            [((CS, CS, c), F32)] * 2,
            [got, before_last, last, residual, image],
        )
    )


def solution(mesh):
    in_specs = (
        P("narrow", "wide", None),
        P("narrow", "wide", None),
        P("narrow", "wide"),
        P(),
        P("narrow", "wide", None),
        P("narrow", "wide", None, None),
        P("narrow", "wide", None, None),
        P("wide", "narrow"),
    )
    out_specs = (P("narrow", "wide", None), P("narrow", "wide", None))
    return jax.shard_map(local, mesh=mesh, in_specs=in_specs, out_specs=out_specs, check_vma=False)
```

```python
import functools

import jax
import jax.numpy as jnp
import numpy as np
from jax import lax
from jax.experimental import pallas as pl
from jax.experimental.pallas import tpu as pltpu
from jax.sharding import PartitionSpec as P

OV = 2
MODES = 4
CS = 28
ES = CS + 2 * OV
LOCAL = ES * ES
LANES = 128
XROWS = ES + 2
XCOLS = 48
OWNROWS = CS * ES
FIRST = OV * ES
SLOT = 40
NB = 9 * MODES
INSIDE = NB + MODES
SMALL_AT = ((5, 0), (5, LANES), (6, 0))
NEAR = {CS - 3: (None, 3, 4), 0: (3, 4, None)}
CONDUCT = LANES - 1

HIGHEST = lax.Precision.HIGHEST
REACTION = 0.01
F32 = jnp.float32
BF16 = jnp.bfloat16
VMEM_LIMIT = 60 * 2**20


def shift(x, axis, step):
    count = lax.axis_size(axis)
    return lax.ppermute(x, axis, [(i, i + step) for i in range(count) if 0 <= i + step < count])


class Copies:
    def __init__(self, buffers, places, sems):
        self.buffers = buffers
        self.copies = [
            pltpu.make_async_copy(b, p, sems.at[k]) for k, (b, p) in enumerate(zip(buffers, places))
        ]
        self.started = [False] * len(buffers)
        self.wait = None

    def flush(self, *refs):
        for k, buffer in enumerate(self.buffers):
            if not self.started[k] and (not refs or any(buffer is r for r in refs)):
                self.copies[k].start()
                self.started[k] = True

    def close(self):
        self.flush()
        for copy in self.copies:
            copy.wait()


def call(body, out, args, scratch=(), late=()):
    delayed = [k for group in late for k in group]
    na, no = len(args), len(out)

    def kernel(*refs):
        sources, places = refs[:na], refs[na : na + no]
        refs = refs[na + no :]
        inputs, buffers, refs = refs[:na], refs[na : na + no], refs[na + no :]
        extra, sems_in, sems_out = refs[:-2], refs[-2], refs[-1]
        copies = [pltpu.make_async_copy(sources[k], inputs[k], sems_in.at[k]) for k in range(na)]
        early = [k for k in range(na) if k not in delayed]
        for k in early + delayed:
            copies[k].start()
        for k in early:
            copies[k].wait()

        def wait(group):
            for k in late[group]:
                copies[k].wait()

        io = Copies(buffers, places, sems_out)
        io.wait = wait
        body(io, *inputs, *buffers, *extra)
        io.close()

    spec = pl.BlockSpec(memory_space=pl.ANY)
    return pl.pallas_call(
        kernel,
        out_shape=[jax.ShapeDtypeStruct(shape, kind) for shape, kind in out],
        in_specs=[spec] * na,
        out_specs=[spec] * no,
        scratch_shapes=[pltpu.VMEM(x.shape, x.dtype) for x in args]
        + [pltpu.VMEM(shape, kind) for shape, kind in out]
        + list(scratch)
        + [pltpu.SemaphoreType.DMA((na,)), pltpu.SemaphoreType.DMA((no,))],
        compiler_params=pltpu.CompilerParams(vmem_limit_bytes=VMEM_LIMIT),
    )(*args)


def dot(a, b):
    return jnp.dot(a, b, preferred_element_type=F32)


def dot_rows(a, b):
    return lax.dot_general(a, b, (((1,), (1,)), ((), ())), preferred_element_type=F32)


def dot_exact(a, b):
    return jnp.dot(a, b, precision=HIGHEST, preferred_element_type=F32)


def halves(x):
    high = x.astype(BF16)
    return high, (x - high.astype(F32)).astype(BF16)


def thirds(x):
    high = x.astype(BF16)
    rest = x - high.astype(F32)
    mid = rest.astype(BF16)
    return high, mid, (rest - mid.astype(F32)).astype(BF16)


def dot_halves(left_high, left_low, x):
    high, low = halves(x)
    return dot(left_high, high) + (dot(left_high, low) + dot(left_low, high))


def put_first_sides(field, row0, rows, from_left, from_right, c, base=0):
    for got, at, near in ((from_left, 7, NEAR[CS - 3]), (from_right, 38, NEAR[0])):
        for e in range(3):
            k, lane = SMALL_AT[e]
            for i in range(rows):
                row, col = row0 + i, slice(at + e, at + e + 1)
                here = slice(base + i, base + i + 1)
                field[row, col, 0:c] = got[e, here, :]
                if near[e] is not None:
                    field[row, col, c : 2 * c] = got[near[e], here, :]
                field[row, col, 2 * c :] = got[k, here, lane : lane + LANES]


def put_sides(field, row0, rows, from_left, from_right, base=0):
    for e in range(3):
        for i in range(rows):
            field[row0 + i, 7 + e : 8 + e, :] = from_left[e, base + i : base + i + 1, :]
            field[row0 + i, 38 + e : 39 + e, :] = from_right[e, base + i : base + i + 1, :]


def fill_select(order, select):
    for i in range(LOCAL // 64):
        place = lax.broadcasted_iota(jnp.int32, (64, LOCAL), 0) + i * 64
        select[i * 64 : i * 64 + 64, :] = jnp.where(place == order[...], 1.0, 0.0).astype(BF16)


def prepare(
    io,
    guess, right, classes, values, order, basis, coarse_own, tail, head, small, basis_out, select
):
    nclass = values.shape[1]
    fill_select(order, select)
    parts = [p.astype(F32) for p in thirds(basis[...])]
    blank = jnp.zeros((MODES, LOCAL), F32)
    stacked = jnp.concatenate([x for p in parts for x in (p, blank)] + [blank, blank], axis=0)
    got = dot_rows(stacked.astype(BF16), select[...])
    basis_out[...] = got[0:8] + (got[8:16] + got[16:24])
    ones = jnp.ones((8, LOCAL), F32)
    none = jnp.zeros((LANES - INSIDE - 8, LOCAL), F32)
    cells = None
    for k, p in enumerate(parts):
        copies = [p] * 9 + [blank, ones if k == 0 else ones * 0.0, none]
        term = dot_rows(
            select[FIRST : FIRST + OWNROWS, :], jnp.concatenate(copies, axis=0).astype(BF16)
        )
        cells = term if cells is None else cells + term
    small[...] = cells.reshape(CS, ES, LANES)
    conduct = jnp.zeros((CS, CS), F32)
    for k in range(nclass):
        conduct = jnp.where(classes[...] == k, values[0:1, k : k + 1], conduct)
    sub = lax.broadcasted_iota(jnp.int32, (ES, CS), 0)
    lane = lax.broadcasted_iota(jnp.int32, (ES, CS), 1)
    here = lax.broadcasted_iota(jnp.int32, (ES, LANES), 1) == CONDUCT
    for i in range(CS):
        spread = jnp.where(sub == lane + OV, jnp.broadcast_to(conduct[i : i + 1, :], (ES, CS)), 0.0)
        column = jnp.sum(spread, axis=1, keepdims=True)
        small[i] = jnp.where(here, column, small[i])
    io.wait(0)
    rows, cols = coarse_own.shape
    for sent, base in ((tail, CS - 3), (head, 0)):
        sent[5:7] = jnp.zeros((2,) + sent.shape[1:], F32)
        sent[6, 0:rows, LANES : LANES + cols] = coarse_own[...]
        for e in range(3):
            k, at = SMALL_AT[e]
            for i in range(CS):
                j = base + e
                sent[e, i : i + 1, :] = guess[i, j : j + 1, :]
                if NEAR[base][e] is not None:
                    sent[NEAR[base][e], i : i + 1, :] = right[i, j : j + 1, :]
                sent[k, i : i + 1, at : at + LANES] = small[i, OV + j : OV + j + 1, :]
    io.flush(tail, head)


def reorder(part, io, order, inverse, out, select, rows):
    step = 256
    fill_select(order, select)
    io.wait(0)
    for n in range(0, LOCAL, step):
        block = halves(inverse[:, n : n + step])[part]
        rows[:, n : n + step] = dot(select[FIRST : FIRST + OWNROWS, :], block).astype(BF16)
    for n in range(0, LOCAL, step):
        out[:, n : n + step] = dot_rows(rows[...], select[n : n + step, :]).astype(BF16)


def first_rows(io, guess, right, small, from_left, from_right, tail, head):
    c = guess.shape[2]
    for sent, base in ((tail, CS - 3), (head, 0)):
        sent[...] = jnp.zeros(sent.shape, F32)
        for r in range(3):
            sent[r, 10 : 10 + CS, 0:c] = guess[base + r]
            sent[r, 10 : 10 + CS, c : 2 * c] = right[base + r]
            sent[r, 8 : 8 + ES, 2 * c :] = small[base + r]
        put_first_sides(sent, 0, 3, from_left, from_right, c, base)


def field_rows(io, edges, from_left, from_right, tail, head):
    for sent, base in ((tail, CS - 3), (head, 0)):
        sent[...] = jnp.zeros(sent.shape, F32)
        for r in range(3):
            sent[r, 8 : 8 + ES, :] = edges[r + (3 if base else 0)]
        put_sides(sent, 0, 3, from_left, from_right, base)


def stencil(wide, weights, row, lanes, wrow=None):
    diag, up, down, left, right = weights
    k = row if wrow is None else wrow
    return (
        diag[k] * wide[row + 1, 8:40, lanes]
        - up[k] * wide[row, 8:40, lanes]
        - down[k] * wide[row + 2, 8:40, lanes]
        - left[k] * wide[row + 1, 7:39, lanes]
        - right[k] * wide[row + 1, 9:41, lanes]
    )


def solve_and_send(io, window, inverse_high, inverse_low, basis, sums, field, tail, head, sent, edges):
    high, low = halves(window)
    parts = [p.astype(F32) for p in halves(basis[...])]
    table = jnp.concatenate(parts, axis=0).astype(BF16)
    got = dot(table, high)
    rhs = got[0:8] + (got[8:16] + dot(table, low)[0:8])
    line = lax.broadcasted_iota(jnp.int32, rhs.shape, 0)
    if sums is not None:
        rhs = jnp.where(line == 4, sums[0], jnp.where(line == 5, sums[1], rhs))
    for k in range(sent.shape[0]):
        sent[k] = rhs
    io.flush(sent)
    io.wait(2)
    field[...] = (
        dot(inverse_high[...], high) + (dot(inverse_high[...], low) + dot(inverse_low[...], high))
    ).reshape(field.shape)
    io.flush(field)
    if len(tail.shape) == 2:
        for i in range(CS):
            tail[i : i + 1, :] = field[i, CS + OV - 1 : CS + OV, :]
            head[i : i + 1, :] = field[i, OV : OV + 1, :]
        edges[0][...] = field[0]
        edges[1][...] = field[CS - 1]
        return
    edges[0:3] = field[0:3]
    edges[3:6] = field[CS - 3 :]
    for e in range(3):
        for i in range(CS):
            tail[e, i : i + 1, :] = field[i, CS + OV - 3 + e : CS + OV - 2 + e, :]
            head[e, i : i + 1, :] = field[i, OV + e : OV + e + 1, :]


def first(
    io,
    guess,
    right,
    small,
    from_left,
    from_right,
    above,
    below,
    basis,
    inverse_high,
    inverse_low,
    of_row,
    of_col,
    diag,
    up,
    down,
    left,
    right_w,
    modes_a_high,
    modes_a_low,
    modes_high,
    modes_low,
    residual,
    field,
    tail,
    head,
    sent,
    edges,
    wide,
    modes,
    window,
):
    c = guess.shape[2]
    for i in range(CS):
        wide[3 + i, 10 : 10 + CS, 0:c] = guess[i]
        wide[3 + i, 8:40, 2 * c :] = small[i]
    for i in range(CS):
        wide[3 + i, 10 : 10 + CS, c : 2 * c] = right[i]
    put_first_sides(wide, 3, CS, from_left, from_right, c)
    wide[0:3] = above[...]
    wide[31:34] = below[...]

    s = 2 * c

    @pl.loop(0, XROWS, unroll=2)
    def _(i):
        modes[i] = jnp.where(of_row[i] * of_col[...] > 0.0, wide[i, :, s : s + LANES], 0.0)

    weights = (diag, up, down, left, right_w)

    @pl.loop(0, ES, unroll=4)
    def _(u):
        def cond(row, at):
            return jnp.broadcast_to(wide[row, at : at + ES, s + CONDUCT : s + CONDUCT + 1], (ES, LANES))

        here = cond(u + 1, 8)
        inside = jnp.broadcast_to(wide[u + 1, 8:40, s + INSIDE : s + INSIDE + 1], (ES, LANES))
        total = jnp.full((ES, LANES), REACTION, F32)
        for ref, row, at in ((up, u, 8), (down, u + 2, 8), (left, u + 1, 7), (right_w, u + 1, 9)):
            face = 0.5 * (here + cond(row, at))
            total = total + face
            ref[u] = face * inside
        diag[u] = total * inside

    @pl.loop(0, ES, unroll=4)
    def _(u):
        for k in range(c // LANES):
            lanes = slice(k * LANES, (k + 1) * LANES)
            there = slice(c + k * LANES, c + (k + 1) * LANES)
            window[u, :, lanes] = wide[u + 1, 8:40, there] - stencil(wide, weights, u, lanes)

    def tables(u, _):
        values = stencil(modes, weights, u, slice(None))
        high, low = halves(values)
        modes_a_high[pl.ds(u * ES, ES), :] = high
        modes_a_low[pl.ds(u * ES, ES), :] = low
        return 0

    lax.fori_loop(0, ES, tables, 0, unroll=2)

    def own_tables(i, _):
        high, low = halves(modes[i + 3, 8:40, :])
        modes_high[pl.ds(i * ES, ES), :] = high
        modes_low[pl.ds(i * ES, ES), :] = low
        return 0

    lax.fori_loop(0, CS, own_tables, 0, unroll=2)
    residual[...] = window[OV : OV + CS]
    io.flush(residual, diag, up, down, left, right_w, modes_a_high, modes_a_low, modes_high, modes_low)
    solve_and_send(
        io,
        window[...].reshape(LOCAL, c),
        inverse_high,
        inverse_low,
        basis,
        None,
        field,
        tail,
        head,
        sent,
        edges,
    )


def partial(io, got, table, out):
    c = got.shape[2]
    out[...] = dot_exact(table[...], got[...].reshape(-1, c)).reshape(out.shape)


def coarse_table(io, before, own, after, pick, spread, ones, out):
    rows, cols = own.shape
    lanes = slice(LANES, LANES + cols)
    stacked = jnp.concatenate([before[6, 0:rows, lanes], own[...], after[6, 0:rows, lanes]], axis=0)
    out[...] = dot_exact(dot_exact(pick[...], stacked), spread[...]) + ones[...]


def summed(got):
    total = got[0]
    for k in range(1, got.shape[0]):
        total = total + got[k]
    return total


def assemble(wide, field, from_left, from_right, above, below):
    wide[3:31, 8:40, :] = field[...]
    put_sides(wide, 3, CS, from_left, from_right)
    wide[0:3] = above[...]
    wide[31:34] = below[...]


def column_mask(lanes):
    col = lax.broadcasted_iota(jnp.int32, (ES, lanes), 0)
    return (col >= OV) & (col < OV + CS)


def spread_coarse(table_high, table_low, coarse):
    high, low = halves(coarse)
    return dot(table_high[...], high) + (dot(table_high[...], low) + dot(table_low[...], high))


def coarse_rows(total):
    rows, c = total.shape
    total = jnp.where(lax.broadcasted_iota(jnp.int32, (rows, c), 0) < NB, total, 0.0)
    return jnp.concatenate([total, jnp.zeros((LANES - rows, c), F32)], axis=0)


def step0(
    io,
    field,
    from_left,
    from_right,
    above,
    below,
    got,
    diag,
    up,
    down,
    left,
    right_w,
    modes_a_high,
    modes_a_low,
    basis,
    inverse_high,
    inverse_low,
    residual,
    image_own,
    coarse,
    field_out,
    tail,
    head,
    sent,
    edges,
    wide,
    window,
):
    weights = (diag, up, down, left, right_w)
    c = field.shape[2]
    assemble(wide, field, from_left, from_right, above, below)
    total = coarse_rows(summed(got))
    coarse[...] = total
    window[...] = spread_coarse(modes_a_high, modes_a_low, total).reshape(window.shape)

    io.wait(0)

    @pl.loop(0, ES, unroll=4)
    def _(u):
        for k in range(c // LANES):
            lanes = slice(k * LANES, (k + 1) * LANES)
            window[u, :, lanes] = window[u, :, lanes] + stencil(wide, weights, u, lanes)

    io.wait(1)
    mask = column_mask(c)

    def reduce(i, carry):
        num, den = carry
        image = jnp.where(mask, window[i + OV], 0.0)
        image_own[i] = image
        return num + residual[i] * image, den + image * image

    zero = jnp.zeros((ES, c), F32)
    num, den = lax.fori_loop(0, CS, reduce, (zero, zero), unroll=2)
    sums = (jnp.sum(num, axis=0, keepdims=True), jnp.sum(den, axis=0, keepdims=True))
    io.flush(image_own, coarse)
    solve_and_send(
        io,
        window[...].reshape(LOCAL, c),
        inverse_high,
        inverse_low,
        basis,
        sums,
        field_out,
        tail,
        head,
        sent,
        edges,
    )


def step1(
    io,
    field,
    from_left,
    from_right,
    above,
    below,
    got,
    diag,
    up,
    down,
    left,
    right_w,
    modes_a_high,
    modes_a_low,
    basis,
    inverse_high,
    inverse_low,
    residual,
    image0,
    image_own,
    coarse,
    field_out,
    tail,
    head,
    sent,
    top,
    bottom,
    scale_out,
    wide,
    window,
):
    weights = (diag, up, down, left, right_w)
    c = field.shape[2]
    assemble(wide, field, from_left, from_right, above, below)
    total = summed(got)
    scale = total[NB : NB + 1] / total[NB + 1 : NB + 2]
    scale_out[...] = jnp.broadcast_to(scale, scale_out.shape)
    total = coarse_rows(total)
    coarse[...] = total
    window[...] = spread_coarse(modes_a_high, modes_a_low, total).reshape(window.shape)

    io.wait(0)

    @pl.loop(0, ES, unroll=4)
    def _(u):
        for k in range(c // LANES):
            lanes = slice(k * LANES, (k + 1) * LANES)
            window[u, :, lanes] = window[u, :, lanes] + stencil(wide, weights, u, lanes)

    io.wait(1)
    mask = column_mask(c)

    def reduce(i, carry):
        num, den = carry
        before = image0[i]
        mine = jnp.where(mask, window[i + OV], 0.0)
        image_own[i] = mine
        image = before - scale * mine
        left_over = residual[i] - scale * before
        return num + left_over * image, den + image * image

    zero = jnp.zeros((ES, c), F32)
    num, den = lax.fori_loop(0, CS, reduce, (zero, zero), unroll=2)
    sums = (jnp.sum(num, axis=0, keepdims=True), jnp.sum(den, axis=0, keepdims=True))
    io.flush(image_own, coarse)
    solve_and_send(
        io,
        window[...].reshape(LOCAL, c),
        inverse_high,
        inverse_low,
        basis,
        sums,
        field_out,
        tail,
        head,
        sent,
        (top, bottom),
    )


def step2(
    io,
    field,
    from_left,
    from_right,
    above,
    below,
    got,
    diag,
    up,
    down,
    left,
    right_w,
    modes_a_high,
    modes_a_low,
    residual,
    image0,
    image1,
    scale_in,
    residual_out,
    image_out,
    coarse,
    sent,
    scale_out,
    wide,
    window,
):
    weights = (diag, up, down, left, right_w)
    c = field.shape[2]
    wide[3:31, 8:40, :] = field[...]
    for i in range(CS):
        wide[3 + i, 9:10, :] = from_left[i : i + 1, :]
        wide[3 + i, 38:39, :] = from_right[i : i + 1, :]
    wide[2, 8:40, :] = above[...]
    wide[31, 8:40, :] = below[...]
    total = summed(got)
    scale = total[NB : NB + 1] / total[NB + 1 : NB + 2]
    scale_out[...] = jnp.broadcast_to(scale, scale_out.shape)
    earlier = scale_in[0:1]
    total = coarse_rows(total)
    coarse[...] = total
    own = slice(FIRST, FIRST + OWNROWS)
    high, low = halves(total)
    table = modes_a_high[own, :]
    window[...] = (
        dot(table, high) + (dot(table, low) + dot(modes_a_low[own, :], high))
    ).reshape(window.shape)
    io.wait(0)
    mask = column_mask(LANES)

    def reduce(i, carry):
        out = []
        for k in range(c // LANES):
            lanes = slice(k * LANES, (k + 1) * LANES)
            num, den = carry[2 * k], carry[2 * k + 1]
            mine = window[i, :, lanes] + stencil(wide, weights, i + OV, lanes)
            mine = jnp.where(mask, mine, 0.0)
            s0 = earlier[:, lanes]
            s1 = scale[:, lanes]
            q0 = image0[i, :, lanes]
            q1 = image1[i, :, lanes]
            before = q0 - s0 * q1
            left_over = residual[i, :, lanes] - s0 * q0 - s1 * before
            image = before - s1 * (q1 - s0 * mine)
            residual_out[i, :, lanes] = left_over
            image_out[i, :, lanes] = image
            out += [num + left_over * image, den + image * image]
        return tuple(out)

    zero = jnp.zeros((ES, LANES), F32)
    sums = lax.fori_loop(0, CS, reduce, (zero,) * (2 * (c // LANES)), unroll=2)
    sums = [jnp.sum(x, axis=0, keepdims=True) for x in sums]
    num = jnp.concatenate(sums[0::2], axis=1)
    den = jnp.concatenate(sums[1::2], axis=1)
    both = jnp.concatenate([num, den], axis=1)
    for k in range(sent.shape[0]):
        sent[k] = both


def resend(io, got, sent):
    total = summed(got)
    for k in range(sent.shape[0]):
        sent[k] = total


def early_directions(
    io,
    guess,
    field0,
    field1,
    coarse0,
    coarse1,
    modes_high,
    modes_low,
    scale0,
    base_out,
    direction_out,
    second_out,
    p0,
    p1,
    change,
):
    for p, coarse in ((p0, coarse0), (p1, coarse1)):
        p[...] = spread_coarse(modes_high, modes_low, coarse[...]).reshape(p.shape)
    s0 = scale0[0:1]

    @pl.loop(0, CS, unroll=2)
    def _(i):
        first_p = p0[i] + field0[i]
        second = p1[i] + field1[i]
        direction_out[i] = first_p - s0 * second
        second_out[i] = second
        change[i] = s0 * first_p
        base_out[i] = guess[i] + change[i, OV : OV + CS, :]


def late_directions(
    io,
    base,
    direction,
    second,
    field2,
    coarse2,
    modes_high,
    modes_low,
    scale0,
    scale1,
    partial_out,
    last_out,
    p2,
):
    p2[...] = spread_coarse(modes_high, modes_low, coarse2[...]).reshape(p2.shape)
    s0 = scale0[0:1]
    s1 = scale1[0:1]

    @pl.loop(0, CS, unroll=2)
    def _(i):
        last_out[i] = direction[i] - s1 * (second[i] - s0 * (p2[i] + field2[i]))
        partial_out[i] = base[i] + s1 * direction[i, OV : OV + CS, :]


def finish(io, got, guess_sum, last, residual, image, answer, residual_out):
    total = summed(got)
    c = guess_sum.shape[2]
    scale = total[:, 0:c] / total[:, c:]

    io.wait(0)

    @pl.loop(0, CS, unroll=4)
    def _(i):
        answer[i] = guess_sum[i] + scale * last[i, OV : OV + CS, :]

    io.flush(answer)
    io.wait(1)

    @pl.loop(0, CS, unroll=4)
    def _(i):
        residual_out[i] = (
            residual[i, OV : OV + CS, :] - scale * image[i, OV : OV + CS, :]
        )


def mode_tables():
    of_row = np.zeros((XROWS, 1, LANES), np.float32)
    of_col = np.zeros((XCOLS, LANES), np.float32)
    region = [0] * 3 + [1] * CS + [2] * 3
    for db in range(3):
        for da in range(3):
            for m in range(MODES):
                lane = (db * 3 + da) * MODES + m
                for e in range(XROWS):
                    of_row[e, 0, lane] = region[e] == da
                    of_col[7 + e, lane] = region[e] == db
    return of_row, of_col


def coarse_tables(nw, nn):
    pick = np.zeros((nn * SLOT, 3 * nn * MODES), np.float32)
    spread = np.zeros((nw * MODES, nw * 8), np.float32)
    ones = np.zeros((nn * SLOT, nw * 8), np.float32)
    for to in range(nn):
        for db in range(3):
            for da in range(3):
                a = to + da - 1
                for m in range(MODES):
                    if 0 <= a < nn:
                        row = to * SLOT + (db * 3 + da) * MODES + m
                        pick[row, (db * nn + a) * MODES + m] = 1.0
        for b in range(nw):
            ones[to * SLOT + NB, b * 8 + 4] = 1.0
            ones[to * SLOT + NB + 1, b * 8 + 5] = 1.0
    for b in range(nw):
        for m in range(MODES):
            spread[b * MODES + m, b * 8 + m] = 1.0
    return pick, spread, ones


def local(
    right_side,
    initial_guess,
    class_map,
    class_conductivity,
    window_index,
    local_inverse,
    coarse_basis,
    coarse_inverse,
):
    nw = lax.axis_size("wide")
    nn = lax.axis_size("narrow")
    c = right_side.shape[2]
    lanes = 2 * c + LANES
    own = ((CS, ES, c), F32)
    side = ((3, CS, c), F32)
    line = ((CS, c), F32)
    strip = ((ES, c), F32)
    edge = ((6, ES, c), F32)
    rows = ((3, XCOLS, c), F32)
    to_wide = ((nw, 8, c), F32)
    weight = ((ES, ES, LANES), F32)
    extended = pltpu.VMEM((XROWS, XCOLS, c), F32)
    window = pltpu.VMEM((ES, ES, c), F32)
    inverse = ((OWNROWS, LOCAL), BF16)
    of_row, of_col = (jnp.asarray(x) for x in mode_tables())
    pick, coarse_spread, ones = (jnp.asarray(x) for x in coarse_tables(nw, nn))

    def exchange(x, axis):
        return lax.all_to_all(x, axis, 0, 0, tiled=True)

    def within(x, groups):
        return lax.all_to_all(
            x, ("wide", "narrow"), 0, 0, axis_index_groups=groups, tiled=True
        )

    tail, head, small, basis = call(
        prepare,
        [
            ((7, ES, c), F32),
            ((7, ES, c), F32),
            ((CS, ES, LANES), F32),
            ((8, LOCAL), F32),
        ],
        [
            initial_guess,
            right_side,
            class_map,
            class_conductivity.reshape(1, -1),
            window_index.reshape(1, LOCAL),
            coarse_basis.reshape(MODES, LOCAL),
            coarse_inverse,
        ],
        [pltpu.VMEM((LOCAL, LOCAL), BF16)],
        late=((0, 1),),
    )
    from_left = shift(tail, "wide", 1)
    from_right = shift(head, "wide", -1)
    inverse_high, inverse_low = [
        call(
            functools.partial(reorder, part),
            [inverse],
            [window_index.reshape(1, LOCAL), local_inverse.reshape(LOCAL, LOCAL)],
            [pltpu.VMEM((LOCAL, LOCAL), BF16), pltpu.VMEM((OWNROWS, LOCAL), BF16)],
            late=((1,),),
        )[0]
        for part in range(2)
    ]
    from_left, from_right, inverse_high = lax.optimization_barrier(
        (from_left, from_right, inverse_high)
    )
    tail, head = call(
        first_rows,
        [((3, XCOLS, lanes), F32)] * 2,
        [initial_guess, right_side, small, from_left, from_right],
    )
    above = shift(tail, "narrow", 1)
    below = shift(head, "narrow", -1)
    (table,) = call(
        coarse_table,
        [((nn * SLOT, nw * 8), F32)],
        [from_left, coarse_inverse, from_right, pick, coarse_spread, ones],
    )
    out = call(
        first,
        [weight] * 5
        + [((LOCAL, LANES), BF16)] * 2
        + [((OWNROWS, LANES), BF16)] * 2
        + [own, own, side, side, to_wide, edge],
        [
            initial_guess,
            right_side,
            small,
            from_left,
            from_right,
            above,
            below,
            basis,
            inverse_high,
            inverse_low,
            of_row,
            of_col,
        ],
        [
            pltpu.VMEM((XROWS, XCOLS, lanes), F32),
            pltpu.VMEM((XROWS, XCOLS, LANES), F32),
            window,
        ],
        late=((), (), (8, 9)),
    )
    weights = out[:5]
    modes_a = out[5:7]
    modes = out[7:9]
    residual, field0, tail, head, sent, edges = out[9:]

    def coarse(sent, edges, tail, head):
        got = exchange(sent, "wide")
        from_left = shift(tail, "wide", 1)
        from_right = shift(head, "wide", -1)
        (parts,) = call(partial, [((nn, SLOT, c), F32)], [got, table])
        parts, from_left, from_right = lax.optimization_barrier((parts, from_left, from_right))
        tail, head = call(field_rows, [rows, rows], [edges, from_left, from_right])
        above = shift(tail, "narrow", 1)
        below = shift(head, "narrow", -1)
        return (from_left, from_right, above, below), exchange(parts, "narrow")

    solver = [basis, inverse_high, inverse_low, residual]
    coarse_out = ((LANES, c), F32)
    scale_out = ((8, c), F32)
    near, got = coarse(sent, edges, tail, head)
    image0, coarse0, field1, tail, head, sent, edges = call(
        step0,
        [own, coarse_out, own, side, side, to_wide, edge],
        [field0, *near, got, *weights, *modes_a, *solver],
        [extended, window],
        late=((6, 7, 8, 9, 10), (13, 16), (14, 15)),
    )
    near, got = coarse(sent, edges, tail, head)
    image1, coarse1, field2, tail, head, sent, top, bottom, scale0 = call(
        step1,
        [own, coarse_out, own, line, line, to_wide, strip, strip, scale_out],
        [field1, *near, got, *weights, *modes_a, *solver, image0],
        [extended, window],
        late=((6, 7, 8, 9, 10), (13, 16, 17), (14, 15)),
    )
    got = exchange(sent, "wide")
    from_left = shift(tail, "wide", 1)
    from_right = shift(head, "wide", -1)
    early = call(
        early_directions,
        [((CS, CS, c), F32), own, own],
        [initial_guess, field0, field1, coarse0, coarse1, *modes, scale0],
        [pltpu.VMEM((CS, ES, c), F32)] * 3,
    )
    got, early, from_left, from_right = lax.optimization_barrier(
        (got, early, from_left, from_right)
    )
    (parts,) = call(partial, [((nn, SLOT, c), F32)], [got, table])
    above = shift(bottom, "narrow", 1)
    below = shift(top, "narrow", -1)
    near = (from_left, from_right, above, below)
    got = exchange(parts, "narrow")
    residual, image, coarse2, sent, scale1 = call(
        step2,
        [own, own, coarse_out, ((2 * nn, 1, 2 * c), F32), scale_out],
        [field2, *near, got, *weights, *modes_a, residual, image0, image1, scale0],
        [extended, pltpu.VMEM((CS, ES, c), F32)],
        late=((6, 7, 8, 9, 10, 13, 14, 15),),
    )
    group = 2 * nn
    count = nw // 2
    inner = [[k * group + r for r in range(group)] for k in range(count)]
    outer = [[k * group + r for k in range(count)] for r in range(group)]
    got = within(sent, inner)
    (sent,) = call(resend, [((count, 1, 2 * c), F32)], [got])
    got = within(sent, outer)
    before_last, last = call(
        late_directions,
        [((CS, CS, c), F32), own],
        [*early, field2, coarse2, *modes, scale0, scale1],
        [pltpu.VMEM((CS, ES, c), F32)],
    )
    return tuple(
        call(
            finish,
            [((CS, CS, c), F32)] * 2,
            [got, before_last, last, residual, image],
            late=((1, 2), (3, 4)),
        )
    )


def solution(mesh):
    in_specs = (
        P("narrow", "wide", None),
        P("narrow", "wide", None),
        P("narrow", "wide"),
        P(),
        P("narrow", "wide", None),
        P("narrow", "wide", None, None),
        P("narrow", "wide", None, None),
        P("wide", "narrow"),
    )
    out_specs = (P("narrow", "wide", None), P("narrow", "wide", None))
    return jax.shard_map(local, mesh=mesh, in_specs=in_specs, out_specs=out_specs, check_vma=False)
```

```python
import functools

import jax
import jax.numpy as jnp
import numpy as np
from jax import lax
from jax.experimental import pallas as pl
from jax.experimental.pallas import tpu as pltpu
from jax.sharding import PartitionSpec as P

OV = 2
MODES = 4
CS = 28
ES = CS + 2 * OV
LOCAL = ES * ES
LANES = 128
XROWS = ES + 2
XCOLS = 48
OWNROWS = CS * ES
FIRST = OV * ES
SLOT = 40
NB = 9 * MODES
INSIDE = NB + MODES
SMALL_AT = ((5, 0), (5, LANES), (6, 0))
NEAR = {CS - 3: (None, 3, 4), 0: (3, 4, None)}
CONDUCT = LANES - 1

HIGHEST = lax.Precision.HIGHEST
REACTION = 0.01
F32 = jnp.float32
BF16 = jnp.bfloat16
VMEM_LIMIT = 60 * 2**20


def shift(x, axis, step):
    count = lax.axis_size(axis)
    return lax.ppermute(x, axis, [(i, i + step) for i in range(count) if 0 <= i + step < count])


class Copies:
    def __init__(self, buffers, places, sems):
        self.buffers = buffers
        self.copies = [
            pltpu.make_async_copy(b, p, sems.at[k]) for k, (b, p) in enumerate(zip(buffers, places))
        ]
        self.started = [False] * len(buffers)
        self.wait = None

    def flush(self, *refs):
        for k, buffer in enumerate(self.buffers):
            if not self.started[k] and (not refs or any(buffer is r for r in refs)):
                self.copies[k].start()
                self.started[k] = True

    def close(self):
        self.flush()
        for copy in self.copies:
            copy.wait()


def call(body, out, args, scratch=(), late=()):
    delayed = [k for group in late for k in group]
    na, no = len(args), len(out)

    def kernel(*refs):
        sources, places = refs[:na], refs[na : na + no]
        refs = refs[na + no :]
        inputs, buffers, refs = refs[:na], refs[na : na + no], refs[na + no :]
        extra, sems_in, sems_out = refs[:-2], refs[-2], refs[-1]
        copies = [pltpu.make_async_copy(sources[k], inputs[k], sems_in.at[k]) for k in range(na)]
        early = [k for k in range(na) if k not in delayed]
        for k in early + delayed:
            copies[k].start()
        for k in early:
            copies[k].wait()

        def wait(group):
            for k in late[group]:
                copies[k].wait()

        io = Copies(buffers, places, sems_out)
        io.wait = wait
        body(io, *inputs, *buffers, *extra)
        io.close()

    spec = pl.BlockSpec(memory_space=pl.ANY)
    return pl.pallas_call(
        kernel,
        out_shape=[jax.ShapeDtypeStruct(shape, kind) for shape, kind in out],
        in_specs=[spec] * na,
        out_specs=[spec] * no,
        scratch_shapes=[pltpu.VMEM(x.shape, x.dtype) for x in args]
        + [pltpu.VMEM(shape, kind) for shape, kind in out]
        + list(scratch)
        + [pltpu.SemaphoreType.DMA((na,)), pltpu.SemaphoreType.DMA((no,))],
        compiler_params=pltpu.CompilerParams(vmem_limit_bytes=VMEM_LIMIT),
    )(*args)


def dot(a, b):
    return jnp.dot(a, b, preferred_element_type=F32)


def dot_rows(a, b):
    return lax.dot_general(a, b, (((1,), (1,)), ((), ())), preferred_element_type=F32)


def dot_exact(a, b):
    return jnp.dot(a, b, precision=HIGHEST, preferred_element_type=F32)


def halves(x):
    high = x.astype(BF16)
    return high, (x - high.astype(F32)).astype(BF16)


def thirds(x):
    high = x.astype(BF16)
    rest = x - high.astype(F32)
    mid = rest.astype(BF16)
    return high, mid, (rest - mid.astype(F32)).astype(BF16)


def dot_halves(left_high, left_low, x):
    high, low = halves(x)
    return dot(left_high, high) + (dot(left_high, low) + dot(left_low, high))


def put_first_sides(field, row0, rows, from_left, from_right, c, base=0):
    for got, at, near in ((from_left, 7, NEAR[CS - 3]), (from_right, 38, NEAR[0])):
        for e in range(3):
            k, lane = SMALL_AT[e]
            for i in range(rows):
                row, col = row0 + i, slice(at + e, at + e + 1)
                here = slice(base + i, base + i + 1)
                field[row, col, 0:c] = got[e, here, :]
                if near[e] is not None:
                    field[row, col, c : 2 * c] = got[near[e], here, :]
                field[row, col, 2 * c :] = got[k, here, lane : lane + LANES]


def put_sides(field, row0, rows, from_left, from_right, base=0):
    for e in range(3):
        for i in range(rows):
            field[row0 + i, 7 + e : 8 + e, :] = from_left[e, base + i : base + i + 1, :]
            field[row0 + i, 38 + e : 39 + e, :] = from_right[e, base + i : base + i + 1, :]


def fill_select(order, select):
    for i in range(LOCAL // 64):
        place = lax.broadcasted_iota(jnp.int32, (64, LOCAL), 0) + i * 64
        select[i * 64 : i * 64 + 64, :] = jnp.where(place == order[...], 1.0, 0.0).astype(BF16)


def prepare(
    io,
    guess, right, classes, values, order, basis, coarse_own, tail, head, small, basis_out, select
):
    nclass = values.shape[1]
    fill_select(order, select)
    parts = [p.astype(F32) for p in thirds(basis[...])]
    blank = jnp.zeros((MODES, LOCAL), F32)
    stacked = jnp.concatenate([x for p in parts for x in (p, blank)] + [blank, blank], axis=0)
    got = dot_rows(stacked.astype(BF16), select[...])
    basis_out[...] = got[0:8] + (got[8:16] + got[16:24])
    ones = jnp.ones((8, LOCAL), F32)
    none = jnp.zeros((LANES - INSIDE - 8, LOCAL), F32)
    cells = None
    for k, p in enumerate(parts):
        copies = [p] * 9 + [blank, ones if k == 0 else ones * 0.0, none]
        term = dot_rows(
            select[FIRST : FIRST + OWNROWS, :], jnp.concatenate(copies, axis=0).astype(BF16)
        )
        cells = term if cells is None else cells + term
    small[...] = cells.reshape(CS, ES, LANES)
    conduct = jnp.zeros((CS, CS), F32)
    for k in range(nclass):
        conduct = jnp.where(classes[...] == k, values[0:1, k : k + 1], conduct)
    sub = lax.broadcasted_iota(jnp.int32, (ES, CS), 0)
    lane = lax.broadcasted_iota(jnp.int32, (ES, CS), 1)
    here = lax.broadcasted_iota(jnp.int32, (ES, LANES), 1) == CONDUCT
    for i in range(CS):
        spread = jnp.where(sub == lane + OV, jnp.broadcast_to(conduct[i : i + 1, :], (ES, CS)), 0.0)
        column = jnp.sum(spread, axis=1, keepdims=True)
        small[i] = jnp.where(here, column, small[i])
    io.wait(0)
    rows, cols = coarse_own.shape
    for sent, base in ((tail, CS - 3), (head, 0)):
        sent[5:7] = jnp.zeros((2,) + sent.shape[1:], F32)
        sent[6, 0:rows, LANES : LANES + cols] = coarse_own[...]
        for e in range(3):
            k, at = SMALL_AT[e]
            for i in range(CS):
                j = base + e
                sent[e, i : i + 1, :] = guess[i, j : j + 1, :]
                if NEAR[base][e] is not None:
                    sent[NEAR[base][e], i : i + 1, :] = right[i, j : j + 1, :]
                sent[k, i : i + 1, at : at + LANES] = small[i, OV + j : OV + j + 1, :]
    io.flush(tail, head)


def reorder(part, io, order, inverse, out, select, rows):
    step = 256
    fill_select(order, select)
    io.wait(0)
    for n in range(0, LOCAL, step):
        block = halves(inverse[:, n : n + step])[part]
        rows[:, n : n + step] = dot(select[FIRST : FIRST + OWNROWS, :], block).astype(BF16)
    for n in range(0, LOCAL, step):
        out[:, n : n + step] = dot_rows(rows[...], select[n : n + step, :]).astype(BF16)


def first_rows(io, guess, right, small, from_left, from_right, tail, head):
    c = guess.shape[2]
    for sent, base in ((tail, CS - 3), (head, 0)):
        sent[...] = jnp.zeros(sent.shape, F32)
        for r in range(3):
            sent[r, 10 : 10 + CS, 0:c] = guess[base + r]
            sent[r, 10 : 10 + CS, c : 2 * c] = right[base + r]
            sent[r, 8 : 8 + ES, 2 * c :] = small[base + r]
        put_first_sides(sent, 0, 3, from_left, from_right, c, base)


def field_rows(io, edges, from_left, from_right, tail, head):
    for sent, base in ((tail, CS - 3), (head, 0)):
        sent[...] = jnp.zeros(sent.shape, F32)
        for r in range(3):
            sent[r, 8 : 8 + ES, :] = edges[r + (3 if base else 0)]
        put_sides(sent, 0, 3, from_left, from_right, base)


def stencil(wide, weights, row, lanes, wrow=None):
    diag, up, down, left, right = weights
    k = row if wrow is None else wrow
    return (
        diag[k] * wide[row + 1, 8:40, lanes]
        - up[k] * wide[row, 8:40, lanes]
        - down[k] * wide[row + 2, 8:40, lanes]
        - left[k] * wide[row + 1, 7:39, lanes]
        - right[k] * wide[row + 1, 9:41, lanes]
    )


def solve_and_send(io, window, inverse_high, inverse_low, basis, sums, field, tail, head, sent, edges):
    high, low = halves(window)
    parts = [p.astype(F32) for p in halves(basis[...])]
    table = jnp.concatenate(parts, axis=0).astype(BF16)
    got = dot(table, high)
    rhs = got[0:8] + (got[8:16] + dot(table, low)[0:8])
    line = lax.broadcasted_iota(jnp.int32, rhs.shape, 0)
    if sums is not None:
        rhs = jnp.where(line == 4, sums[0], jnp.where(line == 5, sums[1], rhs))
    for k in range(sent.shape[0]):
        sent[k] = rhs
    io.flush(sent)
    io.wait(2)
    field[...] = (
        dot(inverse_high[...], high) + (dot(inverse_high[...], low) + dot(inverse_low[...], high))
    ).reshape(field.shape)
    io.flush(field)
    if len(tail.shape) == 2:
        for i in range(CS):
            tail[i : i + 1, :] = field[i, CS + OV - 1 : CS + OV, :]
            head[i : i + 1, :] = field[i, OV : OV + 1, :]
        edges[0][...] = field[0]
        edges[1][...] = field[CS - 1]
        return
    edges[0:3] = field[0:3]
    edges[3:6] = field[CS - 3 :]
    for e in range(3):
        for i in range(CS):
            tail[e, i : i + 1, :] = field[i, CS + OV - 3 + e : CS + OV - 2 + e, :]
            head[e, i : i + 1, :] = field[i, OV + e : OV + e + 1, :]


def first(
    io,
    guess,
    right,
    small,
    from_left,
    from_right,
    above,
    below,
    basis,
    inverse_high,
    inverse_low,
    of_row,
    of_col,
    diag,
    up,
    down,
    left,
    right_w,
    modes_a_high,
    modes_a_low,
    modes_high,
    modes_low,
    residual,
    field,
    tail,
    head,
    sent,
    edges,
    wide,
    modes,
    window,
):
    c = guess.shape[2]
    for i in range(CS):
        wide[3 + i, 10 : 10 + CS, 0:c] = guess[i]
        wide[3 + i, 8:40, 2 * c :] = small[i]
    for i in range(CS):
        wide[3 + i, 10 : 10 + CS, c : 2 * c] = right[i]
    put_first_sides(wide, 3, CS, from_left, from_right, c)
    wide[0:3] = above[...]
    wide[31:34] = below[...]

    s = 2 * c

    @pl.loop(0, XROWS, unroll=2)
    def _(i):
        modes[i] = jnp.where(of_row[i] * of_col[...] > 0.0, wide[i, :, s : s + LANES], 0.0)

    weights = (diag, up, down, left, right_w)

    @pl.loop(0, ES, unroll=4)
    def _(u):
        def cond(row, at):
            return jnp.broadcast_to(wide[row, at : at + ES, s + CONDUCT : s + CONDUCT + 1], (ES, LANES))

        here = cond(u + 1, 8)
        inside = jnp.broadcast_to(wide[u + 1, 8:40, s + INSIDE : s + INSIDE + 1], (ES, LANES))
        total = jnp.full((ES, LANES), REACTION, F32)
        for ref, row, at in ((up, u, 8), (down, u + 2, 8), (left, u + 1, 7), (right_w, u + 1, 9)):
            face = 0.5 * (here + cond(row, at))
            total = total + face
            ref[u] = face * inside
        diag[u] = total * inside

    @pl.loop(0, ES, unroll=4)
    def _(u):
        for k in range(c // LANES):
            lanes = slice(k * LANES, (k + 1) * LANES)
            there = slice(c + k * LANES, c + (k + 1) * LANES)
            window[u, :, lanes] = wide[u + 1, 8:40, there] - stencil(wide, weights, u, lanes)

    def tables(u, _):
        values = stencil(modes, weights, u, slice(None))
        high, low = halves(values)
        modes_a_high[pl.ds(u * ES, ES), :] = high
        modes_a_low[pl.ds(u * ES, ES), :] = low
        return 0

    lax.fori_loop(0, ES, tables, 0, unroll=2)

    def own_tables(i, _):
        high, low = halves(modes[i + 3, 8:40, :])
        modes_high[pl.ds(i * ES, ES), :] = high
        modes_low[pl.ds(i * ES, ES), :] = low
        return 0

    lax.fori_loop(0, CS, own_tables, 0, unroll=2)
    residual[...] = window[OV : OV + CS]
    io.flush(residual, diag, up, down, left, right_w, modes_a_high, modes_a_low, modes_high, modes_low)
    solve_and_send(
        io,
        window[...].reshape(LOCAL, c),
        inverse_high,
        inverse_low,
        basis,
        None,
        field,
        tail,
        head,
        sent,
        edges,
    )


def partial(io, got, table, out):
    c = got.shape[2]
    high, low = halves(table[...])
    out[...] = dot_halves(high, low, got[...].reshape(-1, c)).reshape(out.shape)


def coarse_table(io, before, own, after, pick, spread, ones, out):
    rows, cols = own.shape
    lanes = slice(LANES, LANES + cols)
    stacked = jnp.concatenate([before[6, 0:rows, lanes], own[...], after[6, 0:rows, lanes]], axis=0)
    out[...] = dot_exact(dot_exact(pick[...], stacked), spread[...]) + ones[...]


def summed(got):
    total = got[0]
    for k in range(1, got.shape[0]):
        total = total + got[k]
    return total


def assemble(wide, field, from_left, from_right, above, below):
    wide[3:31, 8:40, :] = field[...]
    put_sides(wide, 3, CS, from_left, from_right)
    wide[0:3] = above[...]
    wide[31:34] = below[...]


def column_mask(lanes):
    col = lax.broadcasted_iota(jnp.int32, (ES, lanes), 0)
    return (col >= OV) & (col < OV + CS)


def spread_coarse(table_high, table_low, coarse):
    high, low = halves(coarse)
    return dot(table_high[...], high) + (dot(table_high[...], low) + dot(table_low[...], high))


def coarse_rows(total):
    rows, c = total.shape
    total = jnp.where(lax.broadcasted_iota(jnp.int32, (rows, c), 0) < NB, total, 0.0)
    return jnp.concatenate([total, jnp.zeros((LANES - rows, c), F32)], axis=0)


def step0(
    io,
    field,
    from_left,
    from_right,
    above,
    below,
    got,
    diag,
    up,
    down,
    left,
    right_w,
    modes_a_high,
    modes_a_low,
    basis,
    inverse_high,
    inverse_low,
    residual,
    image_own,
    coarse,
    field_out,
    tail,
    head,
    sent,
    edges,
    wide,
    window,
):
    weights = (diag, up, down, left, right_w)
    c = field.shape[2]
    total = coarse_rows(summed(got))
    coarse[...] = total
    window[...] = spread_coarse(modes_a_high, modes_a_low, total).reshape(window.shape)

    io.wait(0)
    assemble(wide, field, from_left, from_right, above, below)

    @pl.loop(0, ES, unroll=4)
    def _(u):
        for k in range(c // LANES):
            lanes = slice(k * LANES, (k + 1) * LANES)
            window[u, :, lanes] = window[u, :, lanes] + stencil(wide, weights, u, lanes)

    io.wait(1)
    mask = column_mask(c)

    def reduce(i, carry):
        num, den = carry
        image = jnp.where(mask, window[i + OV], 0.0)
        image_own[i] = image
        return num + residual[i] * image, den + image * image

    zero = jnp.zeros((ES, c), F32)
    num, den = lax.fori_loop(0, CS, reduce, (zero, zero), unroll=2)
    sums = (jnp.sum(num, axis=0, keepdims=True), jnp.sum(den, axis=0, keepdims=True))
    io.flush(image_own, coarse)
    solve_and_send(
        io,
        window[...].reshape(LOCAL, c),
        inverse_high,
        inverse_low,
        basis,
        sums,
        field_out,
        tail,
        head,
        sent,
        edges,
    )


def step1(
    io,
    field,
    from_left,
    from_right,
    above,
    below,
    got,
    diag,
    up,
    down,
    left,
    right_w,
    modes_a_high,
    modes_a_low,
    basis,
    inverse_high,
    inverse_low,
    residual,
    image0,
    image_own,
    coarse,
    field_out,
    tail,
    head,
    sent,
    top,
    bottom,
    scale_out,
    wide,
    window,
):
    weights = (diag, up, down, left, right_w)
    c = field.shape[2]
    total = summed(got)
    scale = total[NB : NB + 1] / total[NB + 1 : NB + 2]
    scale_out[...] = jnp.broadcast_to(scale, scale_out.shape)
    total = coarse_rows(total)
    coarse[...] = total
    window[...] = spread_coarse(modes_a_high, modes_a_low, total).reshape(window.shape)

    io.wait(0)
    assemble(wide, field, from_left, from_right, above, below)

    @pl.loop(0, ES, unroll=4)
    def _(u):
        for k in range(c // LANES):
            lanes = slice(k * LANES, (k + 1) * LANES)
            window[u, :, lanes] = window[u, :, lanes] + stencil(wide, weights, u, lanes)

    io.wait(1)
    mask = column_mask(c)

    def reduce(i, carry):
        num, den = carry
        before = image0[i]
        mine = jnp.where(mask, window[i + OV], 0.0)
        image_own[i] = mine
        image = before - scale * mine
        left_over = residual[i] - scale * before
        return num + left_over * image, den + image * image

    zero = jnp.zeros((ES, c), F32)
    num, den = lax.fori_loop(0, CS, reduce, (zero, zero), unroll=2)
    sums = (jnp.sum(num, axis=0, keepdims=True), jnp.sum(den, axis=0, keepdims=True))
    io.flush(image_own, coarse)
    solve_and_send(
        io,
        window[...].reshape(LOCAL, c),
        inverse_high,
        inverse_low,
        basis,
        sums,
        field_out,
        tail,
        head,
        sent,
        (top, bottom),
    )


def step2(
    io,
    field,
    from_left,
    from_right,
    above,
    below,
    got,
    diag,
    up,
    down,
    left,
    right_w,
    modes_a_high,
    modes_a_low,
    residual,
    image0,
    image1,
    scale_in,
    residual_out,
    image_out,
    coarse,
    sent,
    scale_out,
    wide,
    window,
):
    weights = (diag, up, down, left, right_w)
    c = field.shape[2]
    total = summed(got)
    scale = total[NB : NB + 1] / total[NB + 1 : NB + 2]
    scale_out[...] = jnp.broadcast_to(scale, scale_out.shape)
    earlier = scale_in[0:1]
    total = coarse_rows(total)
    coarse[...] = total
    own = slice(FIRST, FIRST + OWNROWS)
    high, low = halves(total)
    table = modes_a_high[own, :]
    window[...] = (
        dot(table, high) + (dot(table, low) + dot(modes_a_low[own, :], high))
    ).reshape(window.shape)
    io.wait(0)
    wide[3:31, 8:40, :] = field[...]
    for i in range(CS):
        wide[3 + i, 9:10, :] = from_left[i : i + 1, :]
        wide[3 + i, 38:39, :] = from_right[i : i + 1, :]
    wide[2, 8:40, :] = above[...]
    wide[31, 8:40, :] = below[...]
    mask = column_mask(LANES)

    def reduce(i, carry):
        out = []
        for k in range(c // LANES):
            lanes = slice(k * LANES, (k + 1) * LANES)
            num, den = carry[2 * k], carry[2 * k + 1]
            mine = window[i, :, lanes] + stencil(wide, weights, i + OV, lanes)
            mine = jnp.where(mask, mine, 0.0)
            s0 = earlier[:, lanes]
            s1 = scale[:, lanes]
            q0 = image0[i, :, lanes]
            q1 = image1[i, :, lanes]
            before = q0 - s0 * q1
            left_over = residual[i, :, lanes] - s0 * q0 - s1 * before
            image = before - s1 * (q1 - s0 * mine)
            residual_out[i, :, lanes] = left_over
            image_out[i, :, lanes] = image
            out += [num + left_over * image, den + image * image]
        return tuple(out)

    zero = jnp.zeros((ES, LANES), F32)
    sums = lax.fori_loop(0, CS, reduce, (zero,) * (2 * (c // LANES)), unroll=2)
    sums = [jnp.sum(x, axis=0, keepdims=True) for x in sums]
    num = jnp.concatenate(sums[0::2], axis=1)
    den = jnp.concatenate(sums[1::2], axis=1)
    both = jnp.concatenate([num, den], axis=1)
    for k in range(sent.shape[0]):
        sent[k] = both


def resend(io, got, sent):
    total = summed(got)
    for k in range(sent.shape[0]):
        sent[k] = total


def early_directions(
    io,
    guess,
    field0,
    field1,
    coarse0,
    coarse1,
    modes_high,
    modes_low,
    scale0,
    base_out,
    direction_out,
    second_out,
    p0,
    p1,
    change,
):
    for p, coarse in ((p0, coarse0), (p1, coarse1)):
        p[...] = spread_coarse(modes_high, modes_low, coarse[...]).reshape(p.shape)
    s0 = scale0[0:1]

    @pl.loop(0, CS, unroll=2)
    def _(i):
        first_p = p0[i] + field0[i]
        second = p1[i] + field1[i]
        direction_out[i] = first_p - s0 * second
        second_out[i] = second
        change[i] = s0 * first_p
        base_out[i] = guess[i] + change[i, OV : OV + CS, :]


def late_directions(
    io,
    base,
    direction,
    second,
    field2,
    coarse2,
    modes_high,
    modes_low,
    scale0,
    scale1,
    partial_out,
    last_out,
    p2,
):
    p2[...] = spread_coarse(modes_high, modes_low, coarse2[...]).reshape(p2.shape)
    s0 = scale0[0:1]
    s1 = scale1[0:1]

    @pl.loop(0, CS, unroll=2)
    def _(i):
        last_out[i] = direction[i] - s1 * (second[i] - s0 * (p2[i] + field2[i]))
        partial_out[i] = base[i] + s1 * direction[i, OV : OV + CS, :]


def finish(io, got, guess_sum, last, residual, image, answer, residual_out):
    total = summed(got)
    c = guess_sum.shape[2]
    scale = total[:, 0:c] / total[:, c:]

    io.wait(0)

    @pl.loop(0, CS, unroll=4)
    def _(i):
        answer[i] = guess_sum[i] + scale * last[i, OV : OV + CS, :]

    io.flush(answer)
    io.wait(1)

    @pl.loop(0, CS, unroll=4)
    def _(i):
        residual_out[i] = (
            residual[i, OV : OV + CS, :] - scale * image[i, OV : OV + CS, :]
        )


def mode_tables():
    of_row = np.zeros((XROWS, 1, LANES), np.float32)
    of_col = np.zeros((XCOLS, LANES), np.float32)
    region = [0] * 3 + [1] * CS + [2] * 3
    for db in range(3):
        for da in range(3):
            for m in range(MODES):
                lane = (db * 3 + da) * MODES + m
                for e in range(XROWS):
                    of_row[e, 0, lane] = region[e] == da
                    of_col[7 + e, lane] = region[e] == db
    return of_row, of_col


def coarse_tables(nw, nn):
    pick = np.zeros((nn * SLOT, 3 * nn * MODES), np.float32)
    spread = np.zeros((nw * MODES, nw * 8), np.float32)
    ones = np.zeros((nn * SLOT, nw * 8), np.float32)
    for to in range(nn):
        for db in range(3):
            for da in range(3):
                a = to + da - 1
                for m in range(MODES):
                    if 0 <= a < nn:
                        row = to * SLOT + (db * 3 + da) * MODES + m
                        pick[row, (db * nn + a) * MODES + m] = 1.0
        for b in range(nw):
            ones[to * SLOT + NB, b * 8 + 4] = 1.0
            ones[to * SLOT + NB + 1, b * 8 + 5] = 1.0
    for b in range(nw):
        for m in range(MODES):
            spread[b * MODES + m, b * 8 + m] = 1.0
    return pick, spread, ones


def local(
    right_side,
    initial_guess,
    class_map,
    class_conductivity,
    window_index,
    local_inverse,
    coarse_basis,
    coarse_inverse,
):
    nw = lax.axis_size("wide")
    nn = lax.axis_size("narrow")
    c = right_side.shape[2]
    lanes = 2 * c + LANES
    own = ((CS, ES, c), F32)
    side = ((3, CS, c), F32)
    line = ((CS, c), F32)
    strip = ((ES, c), F32)
    edge = ((6, ES, c), F32)
    rows = ((3, XCOLS, c), F32)
    to_wide = ((nw, 8, c), F32)
    weight = ((ES, ES, LANES), F32)
    extended = pltpu.VMEM((XROWS, XCOLS, c), F32)
    window = pltpu.VMEM((ES, ES, c), F32)
    inverse = ((OWNROWS, LOCAL), BF16)
    of_row, of_col = (jnp.asarray(x) for x in mode_tables())
    pick, coarse_spread, ones = (jnp.asarray(x) for x in coarse_tables(nw, nn))

    def exchange(x, axis):
        return lax.all_to_all(x, axis, 0, 0, tiled=True)

    def within(x, groups):
        return lax.all_to_all(
            x, ("wide", "narrow"), 0, 0, axis_index_groups=groups, tiled=True
        )

    tail, head, small, basis = call(
        prepare,
        [
            ((7, ES, c), F32),
            ((7, ES, c), F32),
            ((CS, ES, LANES), F32),
            ((8, LOCAL), F32),
        ],
        [
            initial_guess,
            right_side,
            class_map,
            class_conductivity.reshape(1, -1),
            window_index.reshape(1, LOCAL),
            coarse_basis.reshape(MODES, LOCAL),
            coarse_inverse,
        ],
        [pltpu.VMEM((LOCAL, LOCAL), BF16)],
        late=((0, 1),),
    )
    from_left = shift(tail, "wide", 1)
    from_right = shift(head, "wide", -1)
    inverse_high, inverse_low = [
        call(
            functools.partial(reorder, part),
            [inverse],
            [window_index.reshape(1, LOCAL), local_inverse.reshape(LOCAL, LOCAL)],
            [pltpu.VMEM((LOCAL, LOCAL), BF16), pltpu.VMEM((OWNROWS, LOCAL), BF16)],
            late=((1,),),
        )[0]
        for part in range(2)
    ]
    from_left, from_right, inverse_high = lax.optimization_barrier(
        (from_left, from_right, inverse_high)
    )
    tail, head = call(
        first_rows,
        [((3, XCOLS, lanes), F32)] * 2,
        [initial_guess, right_side, small, from_left, from_right],
    )
    above = shift(tail, "narrow", 1)
    below = shift(head, "narrow", -1)
    (table,) = call(
        coarse_table,
        [((nn * SLOT, nw * 8), F32)],
        [from_left, coarse_inverse, from_right, pick, coarse_spread, ones],
    )
    out = call(
        first,
        [weight] * 5
        + [((LOCAL, LANES), BF16)] * 2
        + [((OWNROWS, LANES), BF16)] * 2
        + [own, own, side, side, to_wide, edge],
        [
            initial_guess,
            right_side,
            small,
            from_left,
            from_right,
            above,
            below,
            basis,
            inverse_high,
            inverse_low,
            of_row,
            of_col,
        ],
        [
            pltpu.VMEM((XROWS, XCOLS, lanes), F32),
            pltpu.VMEM((XROWS, XCOLS, LANES), F32),
            window,
        ],
        late=((), (), (8, 9)),
    )
    weights = out[:5]
    modes_a = out[5:7]
    modes = out[7:9]
    residual, field0, tail, head, sent, edges = out[9:]

    def coarse(sent, edges, tail, head):
        got = exchange(sent, "wide")
        from_left = shift(tail, "wide", 1)
        from_right = shift(head, "wide", -1)
        (parts,) = call(partial, [((nn, SLOT, c), F32)], [got, table])
        parts, from_left, from_right = lax.optimization_barrier((parts, from_left, from_right))
        tail, head = call(field_rows, [rows, rows], [edges, from_left, from_right])
        above = shift(tail, "narrow", 1)
        below = shift(head, "narrow", -1)
        return (from_left, from_right, above, below), exchange(parts, "narrow")

    solver = [basis, inverse_high, inverse_low, residual]
    coarse_out = ((LANES, c), F32)
    scale_out = ((8, c), F32)
    near, got = coarse(sent, edges, tail, head)
    image0, coarse0, field1, tail, head, sent, edges = call(
        step0,
        [own, coarse_out, own, side, side, to_wide, edge],
        [field0, *near, got, *weights, *modes_a, *solver],
        [extended, window],
        late=((0, 1, 2, 3, 4, 6, 7, 8, 9, 10), (13, 16), (14, 15)),
    )
    near, got = coarse(sent, edges, tail, head)
    image1, coarse1, field2, tail, head, sent, top, bottom, scale0 = call(
        step1,
        [own, coarse_out, own, line, line, to_wide, strip, strip, scale_out],
        [field1, *near, got, *weights, *modes_a, *solver, image0],
        [extended, window],
        late=((0, 1, 2, 3, 4, 6, 7, 8, 9, 10), (13, 16, 17), (14, 15)),
    )
    got = exchange(sent, "wide")
    from_left = shift(tail, "wide", 1)
    from_right = shift(head, "wide", -1)
    early = call(
        early_directions,
        [((CS, CS, c), F32), own, own],
        [initial_guess, field0, field1, coarse0, coarse1, *modes, scale0],
        [pltpu.VMEM((CS, ES, c), F32)] * 3,
    )
    got, early, from_left, from_right = lax.optimization_barrier(
        (got, early, from_left, from_right)
    )
    (parts,) = call(partial, [((nn, SLOT, c), F32)], [got, table])
    above = shift(bottom, "narrow", 1)
    below = shift(top, "narrow", -1)
    near = (from_left, from_right, above, below)
    got = exchange(parts, "narrow")
    residual, image, coarse2, sent, scale1 = call(
        step2,
        [own, own, coarse_out, ((2 * nn, 1, 2 * c), F32), scale_out],
        [field2, *near, got, *weights, *modes_a, residual, image0, image1, scale0],
        [extended, pltpu.VMEM((CS, ES, c), F32)],
        late=((0, 1, 2, 3, 4, 6, 7, 8, 9, 10, 13, 14, 15),),
    )
    group = 2 * nn
    count = nw // 2
    inner = [[k * group + r for r in range(group)] for k in range(count)]
    outer = [[k * group + r for k in range(count)] for r in range(group)]
    got = within(sent, inner)
    (sent,) = call(resend, [((count, 1, 2 * c), F32)], [got])
    got = within(sent, outer)
    before_last, last = call(
        late_directions,
        [((CS, CS, c), F32), own],
        [*early, field2, coarse2, *modes, scale0, scale1],
        [pltpu.VMEM((CS, ES, c), F32)],
    )
    return tuple(
        call(
            finish,
            [((CS, CS, c), F32)] * 2,
            [got, before_last, last, residual, image],
            late=((1, 2), (3, 4)),
        )
    )


def solution(mesh):
    in_specs = (
        P("narrow", "wide", None),
        P("narrow", "wide", None),
        P("narrow", "wide"),
        P(),
        P("narrow", "wide", None),
        P("narrow", "wide", None, None),
        P("narrow", "wide", None, None),
        P("wide", "narrow"),
    )
    out_specs = (P("narrow", "wide", None), P("narrow", "wide", None))
    return jax.shard_map(local, mesh=mesh, in_specs=in_specs, out_specs=out_specs, check_vma=False)
```

```python
import functools

import jax
import jax.numpy as jnp
import numpy as np
from jax import lax
from jax.experimental import pallas as pl
from jax.experimental.pallas import tpu as pltpu
from jax.sharding import PartitionSpec as P

OV = 2
MODES = 4
CS = 28
ES = CS + 2 * OV
LOCAL = ES * ES
LANES = 128
XROWS = ES + 2
XCOLS = 48
OWNROWS = CS * ES
FIRST = OV * ES
SLOT = 40
NB = 9 * MODES
INSIDE = NB + MODES
SMALL_AT = ((5, 0), (5, LANES), (6, 0))
NEAR = {CS - 3: (None, 3, 4), 0: (3, 4, None)}
CONDUCT = LANES - 1

HIGHEST = lax.Precision.HIGHEST
REACTION = 0.01
F32 = jnp.float32
BF16 = jnp.bfloat16
VMEM_LIMIT = 60 * 2**20


def shift(x, axis, step):
    count = lax.axis_size(axis)
    return lax.ppermute(x, axis, [(i, i + step) for i in range(count) if 0 <= i + step < count])


class Copies:
    def __init__(self, buffers, places, sems):
        self.buffers = buffers
        self.copies = [
            pltpu.make_async_copy(b, p, sems.at[k]) for k, (b, p) in enumerate(zip(buffers, places))
        ]
        self.started = [False] * len(buffers)
        self.wait = None

    def flush(self, *refs):
        for k, buffer in enumerate(self.buffers):
            if not self.started[k] and (not refs or any(buffer is r for r in refs)):
                self.copies[k].start()
                self.started[k] = True

    def close(self):
        self.flush()
        for copy in self.copies:
            copy.wait()


def call(body, out, args, scratch=(), late=()):
    delayed = [k for group in late for k in group]
    na, no = len(args), len(out)

    def kernel(*refs):
        sources, places = refs[:na], refs[na : na + no]
        refs = refs[na + no :]
        inputs, buffers, refs = refs[:na], refs[na : na + no], refs[na + no :]
        extra, sems_in, sems_out = refs[:-2], refs[-2], refs[-1]
        copies = [pltpu.make_async_copy(sources[k], inputs[k], sems_in.at[k]) for k in range(na)]
        early = [k for k in range(na) if k not in delayed]
        for k in early + delayed:
            copies[k].start()
        for k in early:
            copies[k].wait()

        def wait(group):
            for k in late[group]:
                copies[k].wait()

        io = Copies(buffers, places, sems_out)
        io.wait = wait
        body(io, *inputs, *buffers, *extra)
        io.close()

    spec = pl.BlockSpec(memory_space=pl.ANY)
    return pl.pallas_call(
        kernel,
        out_shape=[jax.ShapeDtypeStruct(shape, kind) for shape, kind in out],
        in_specs=[spec] * na,
        out_specs=[spec] * no,
        scratch_shapes=[pltpu.VMEM(x.shape, x.dtype) for x in args]
        + [pltpu.VMEM(shape, kind) for shape, kind in out]
        + list(scratch)
        + [pltpu.SemaphoreType.DMA((na,)), pltpu.SemaphoreType.DMA((no,))],
        compiler_params=pltpu.CompilerParams(vmem_limit_bytes=VMEM_LIMIT),
    )(*args)


def dot(a, b):
    return jnp.dot(a, b, preferred_element_type=F32)


def dot_rows(a, b):
    return lax.dot_general(a, b, (((1,), (1,)), ((), ())), preferred_element_type=F32)


def dot_exact(a, b):
    return jnp.dot(a, b, precision=HIGHEST, preferred_element_type=F32)


def halves(x):
    high = x.astype(BF16)
    return high, (x - high.astype(F32)).astype(BF16)


def thirds(x):
    high = x.astype(BF16)
    rest = x - high.astype(F32)
    mid = rest.astype(BF16)
    return high, mid, (rest - mid.astype(F32)).astype(BF16)


def dot_halves(left_high, left_low, x):
    high, low = halves(x)
    return dot(left_high, high) + (dot(left_high, low) + dot(left_low, high))


def put_first_sides(field, row0, rows, from_left, from_right, c, base=0):
    for got, at, near in ((from_left, 7, NEAR[CS - 3]), (from_right, 38, NEAR[0])):
        for e in range(3):
            k, lane = SMALL_AT[e]
            for i in range(rows):
                row, col = row0 + i, slice(at + e, at + e + 1)
                here = slice(base + i, base + i + 1)
                field[row, col, 0:c] = got[e, here, :]
                if near[e] is not None:
                    field[row, col, c : 2 * c] = got[near[e], here, :]
                field[row, col, 2 * c :] = got[k, here, lane : lane + LANES]


def put_sides(field, row0, rows, from_left, from_right, base=0):
    for e in range(3):
        for i in range(rows):
            field[row0 + i, 7 + e : 8 + e, :] = from_left[e, base + i : base + i + 1, :]
            field[row0 + i, 38 + e : 39 + e, :] = from_right[e, base + i : base + i + 1, :]


def fill_select(order, select):
    for i in range(LOCAL // 64):
        place = lax.broadcasted_iota(jnp.int32, (64, LOCAL), 0) + i * 64
        select[i * 64 : i * 64 + 64, :] = jnp.where(place == order[...], 1.0, 0.0).astype(BF16)


def prepare(
    io,
    guess, right, classes, values, order, basis, coarse_own, tail, head, small, basis_out, select
):
    nclass = values.shape[1]
    fill_select(order, select)
    parts = [p.astype(F32) for p in thirds(basis[...])]
    blank = jnp.zeros((MODES, LOCAL), F32)
    stacked = jnp.concatenate([x for p in parts for x in (p, blank)] + [blank, blank], axis=0)
    got = dot_rows(stacked.astype(BF16), select[...])
    basis_out[...] = got[0:8] + (got[8:16] + got[16:24])
    ones = jnp.ones((8, LOCAL), F32)
    none = jnp.zeros((LANES - INSIDE - 8, LOCAL), F32)
    cells = None
    for k, p in enumerate(parts):
        copies = [p] * 9 + [blank, ones if k == 0 else ones * 0.0, none]
        term = dot_rows(
            select[FIRST : FIRST + OWNROWS, :], jnp.concatenate(copies, axis=0).astype(BF16)
        )
        cells = term if cells is None else cells + term
    small[...] = cells.reshape(CS, ES, LANES)
    conduct = jnp.zeros((CS, CS), F32)
    for k in range(nclass):
        conduct = jnp.where(classes[...] == k, values[0:1, k : k + 1], conduct)
    sub = lax.broadcasted_iota(jnp.int32, (ES, CS), 0)
    lane = lax.broadcasted_iota(jnp.int32, (ES, CS), 1)
    here = lax.broadcasted_iota(jnp.int32, (ES, LANES), 1) == CONDUCT
    for i in range(CS):
        spread = jnp.where(sub == lane + OV, jnp.broadcast_to(conduct[i : i + 1, :], (ES, CS)), 0.0)
        column = jnp.sum(spread, axis=1, keepdims=True)
        small[i] = jnp.where(here, column, small[i])
    io.wait(0)
    rows, cols = coarse_own.shape
    for sent, base in ((tail, CS - 3), (head, 0)):
        sent[5:7] = jnp.zeros((2,) + sent.shape[1:], F32)
        sent[6, 0:rows, LANES : LANES + cols] = coarse_own[...]
        for e in range(3):
            k, at = SMALL_AT[e]
            for i in range(CS):
                j = base + e
                sent[e, i : i + 1, :] = guess[i, j : j + 1, :]
                if NEAR[base][e] is not None:
                    sent[NEAR[base][e], i : i + 1, :] = right[i, j : j + 1, :]
                sent[k, i : i + 1, at : at + LANES] = small[i, OV + j : OV + j + 1, :]
    io.flush(tail, head)


def reorder(part, io, order, inverse, out, select, rows):
    step = 256
    fill_select(order, select)
    io.wait(0)
    for n in range(0, LOCAL, step):
        block = halves(inverse[:, n : n + step])[part]
        rows[:, n : n + step] = dot(select[FIRST : FIRST + OWNROWS, :], block).astype(BF16)
    for n in range(0, LOCAL, step):
        out[:, n : n + step] = dot_rows(rows[...], select[n : n + step, :]).astype(BF16)


def first_rows(io, guess, right, small, from_left, from_right, tail, head):
    c = guess.shape[2]
    for sent, base in ((tail, CS - 3), (head, 0)):
        sent[...] = jnp.zeros(sent.shape, F32)
        for r in range(3):
            sent[r, 10 : 10 + CS, 0:c] = guess[base + r]
            sent[r, 10 : 10 + CS, c : 2 * c] = right[base + r]
            sent[r, 8 : 8 + ES, 2 * c :] = small[base + r]
        put_first_sides(sent, 0, 3, from_left, from_right, c, base)


def field_rows(io, edges, from_left, from_right, tail, head):
    for sent, base in ((tail, CS - 3), (head, 0)):
        sent[...] = jnp.zeros(sent.shape, F32)
        for r in range(3):
            sent[r, 8 : 8 + ES, :] = edges[r + (3 if base else 0)]
        put_sides(sent, 0, 3, from_left, from_right, base)


def stencil(wide, weights, row, lanes, wrow=None):
    diag, up, down, left, right = weights
    k = row if wrow is None else wrow
    return (
        diag[k] * wide[row + 1, 8:40, lanes]
        - up[k] * wide[row, 8:40, lanes]
        - down[k] * wide[row + 2, 8:40, lanes]
        - left[k] * wide[row + 1, 7:39, lanes]
        - right[k] * wide[row + 1, 9:41, lanes]
    )


def solve_and_send(io, window, inverse_high, inverse_low, basis, sums, field, tail, head, sent, edges):
    high, low = halves(window)
    parts = [p.astype(F32) for p in halves(basis[...])]
    table = jnp.concatenate(parts, axis=0).astype(BF16)
    got = dot(table, high)
    rhs = got[0:8] + (got[8:16] + dot(table, low)[0:8])
    line = lax.broadcasted_iota(jnp.int32, rhs.shape, 0)
    if sums is not None:
        rhs = jnp.where(line == 4, sums[0], jnp.where(line == 5, sums[1], rhs))
    for k in range(sent.shape[0]):
        sent[k] = rhs
    io.flush(sent)
    io.wait(2)
    field[...] = (
        dot(inverse_high[...], high) + (dot(inverse_high[...], low) + dot(inverse_low[...], high))
    ).reshape(field.shape)
    io.flush(field)
    if len(tail.shape) == 2:
        for i in range(CS):
            tail[i : i + 1, :] = field[i, CS + OV - 1 : CS + OV, :]
            head[i : i + 1, :] = field[i, OV : OV + 1, :]
        edges[0][...] = field[0]
        edges[1][...] = field[CS - 1]
        return
    edges[0:3] = field[0:3]
    edges[3:6] = field[CS - 3 :]
    for e in range(3):
        for i in range(CS):
            tail[e, i : i + 1, :] = field[i, CS + OV - 3 + e : CS + OV - 2 + e, :]
            head[e, i : i + 1, :] = field[i, OV + e : OV + e + 1, :]


def first(
    io,
    guess,
    right,
    small,
    from_left,
    from_right,
    above,
    below,
    basis,
    inverse_high,
    inverse_low,
    of_row,
    of_col,
    diag,
    up,
    down,
    left,
    right_w,
    modes_a_high,
    modes_a_low,
    modes_high,
    modes_low,
    residual,
    field,
    tail,
    head,
    sent,
    edges,
    wide,
    modes,
    window,
):
    c = guess.shape[2]
    for i in range(CS):
        wide[3 + i, 10 : 10 + CS, 0:c] = guess[i]
        wide[3 + i, 8:40, 2 * c :] = small[i]
    for i in range(CS):
        wide[3 + i, 10 : 10 + CS, c : 2 * c] = right[i]
    put_first_sides(wide, 3, CS, from_left, from_right, c)
    wide[0:3] = above[...]
    wide[31:34] = below[...]

    s = 2 * c

    @pl.loop(0, XROWS, unroll=2)
    def _(i):
        modes[i] = jnp.where(of_row[i] * of_col[...] > 0.0, wide[i, :, s : s + LANES], 0.0)

    weights = (diag, up, down, left, right_w)

    @pl.loop(0, ES, unroll=4)
    def _(u):
        def cond(row, at):
            return jnp.broadcast_to(wide[row, at : at + ES, s + CONDUCT : s + CONDUCT + 1], (ES, LANES))

        here = cond(u + 1, 8)
        inside = jnp.broadcast_to(wide[u + 1, 8:40, s + INSIDE : s + INSIDE + 1], (ES, LANES))
        total = jnp.full((ES, LANES), REACTION, F32)
        for ref, row, at in ((up, u, 8), (down, u + 2, 8), (left, u + 1, 7), (right_w, u + 1, 9)):
            face = 0.5 * (here + cond(row, at))
            total = total + face
            ref[u] = face * inside
        diag[u] = total * inside

    @pl.loop(0, ES, unroll=4)
    def _(u):
        for k in range(c // LANES):
            lanes = slice(k * LANES, (k + 1) * LANES)
            there = slice(c + k * LANES, c + (k + 1) * LANES)
            window[u, :, lanes] = wide[u + 1, 8:40, there] - stencil(wide, weights, u, lanes)

    def tables(u, _):
        values = stencil(modes, weights, u, slice(None))
        high, low = halves(values)
        modes_a_high[pl.ds(u * ES, ES), :] = high
        modes_a_low[pl.ds(u * ES, ES), :] = low
        return 0

    lax.fori_loop(0, ES, tables, 0, unroll=2)

    def own_tables(i, _):
        high, low = halves(modes[i + 3, 8:40, :])
        modes_high[pl.ds(i * ES, ES), :] = high
        modes_low[pl.ds(i * ES, ES), :] = low
        return 0

    lax.fori_loop(0, CS, own_tables, 0, unroll=2)
    residual[...] = window[OV : OV + CS]
    io.flush(residual, diag, up, down, left, right_w, modes_a_high, modes_a_low, modes_high, modes_low)
    solve_and_send(
        io,
        window[...].reshape(LOCAL, c),
        inverse_high,
        inverse_low,
        basis,
        None,
        field,
        tail,
        head,
        sent,
        edges,
    )


def partial(io, got, table, out):
    c = got.shape[2]
    out[...] = dot_exact(table[...], got[...].reshape(-1, c)).reshape(out.shape)


def coarse_table(io, before, own, after, pick, spread, ones, out):
    rows, cols = own.shape
    lanes = slice(LANES, LANES + cols)
    stacked = jnp.concatenate([before[6, 0:rows, lanes], own[...], after[6, 0:rows, lanes]], axis=0)
    out[...] = dot_exact(dot_exact(pick[...], stacked), spread[...]) + ones[...]


def summed(got):
    total = got[0]
    for k in range(1, got.shape[0]):
        total = total + got[k]
    return total


def assemble(wide, field, from_left, from_right, above, below):
    wide[3:31, 8:40, :] = field[...]
    put_sides(wide, 3, CS, from_left, from_right)
    wide[0:3] = above[...]
    wide[31:34] = below[...]


def column_mask(lanes):
    col = lax.broadcasted_iota(jnp.int32, (ES, lanes), 0)
    return (col >= OV) & (col < OV + CS)


def spread_coarse(table_high, table_low, coarse):
    high, low = halves(coarse)
    return dot(table_high[...], high) + (dot(table_high[...], low) + dot(table_low[...], high))


def coarse_rows(total):
    rows, c = total.shape
    total = jnp.where(lax.broadcasted_iota(jnp.int32, (rows, c), 0) < NB, total, 0.0)
    return jnp.concatenate([total, jnp.zeros((LANES - rows, c), F32)], axis=0)


def step0(
    io,
    field,
    from_left,
    from_right,
    above,
    below,
    got,
    diag,
    up,
    down,
    left,
    right_w,
    modes_a_high,
    modes_a_low,
    basis,
    inverse_high,
    inverse_low,
    residual,
    image_own,
    coarse,
    field_out,
    tail,
    head,
    sent,
    edges,
    wide,
    window,
):
    weights = (diag, up, down, left, right_w)
    c = field.shape[2]
    assemble(wide, field, from_left, from_right, above, below)
    total = coarse_rows(summed(got))
    coarse[...] = total
    window[...] = spread_coarse(modes_a_high, modes_a_low, total).reshape(window.shape)

    io.wait(0)

    @pl.loop(0, ES, unroll=4)
    def _(u):
        for k in range(c // LANES):
            lanes = slice(k * LANES, (k + 1) * LANES)
            window[u, :, lanes] = window[u, :, lanes] + stencil(wide, weights, u, lanes)

    io.wait(1)
    mask = column_mask(c)

    def reduce(i, carry):
        num, den = carry
        image = jnp.where(mask, window[i + OV], 0.0)
        image_own[i] = image
        return num + residual[i] * image, den + image * image

    zero = jnp.zeros((ES, c), F32)
    num, den = lax.fori_loop(0, CS, reduce, (zero, zero), unroll=2)
    sums = (jnp.sum(num, axis=0, keepdims=True), jnp.sum(den, axis=0, keepdims=True))
    io.flush(image_own, coarse)
    solve_and_send(
        io,
        window[...].reshape(LOCAL, c),
        inverse_high,
        inverse_low,
        basis,
        sums,
        field_out,
        tail,
        head,
        sent,
        edges,
    )


def step1(
    io,
    field,
    from_left,
    from_right,
    above,
    below,
    got,
    diag,
    up,
    down,
    left,
    right_w,
    modes_a_high,
    modes_a_low,
    basis,
    inverse_high,
    inverse_low,
    residual,
    image0,
    image_own,
    coarse,
    field_out,
    tail,
    head,
    sent,
    top,
    bottom,
    scale_out,
    wide,
    window,
):
    weights = (diag, up, down, left, right_w)
    c = field.shape[2]
    assemble(wide, field, from_left, from_right, above, below)
    total = summed(got)
    scale = total[NB : NB + 1] / total[NB + 1 : NB + 2]
    scale_out[...] = jnp.broadcast_to(scale, scale_out.shape)
    total = coarse_rows(total)
    coarse[...] = total
    window[...] = spread_coarse(modes_a_high, modes_a_low, total).reshape(window.shape)

    io.wait(0)

    @pl.loop(0, ES, unroll=4)
    def _(u):
        for k in range(c // LANES):
            lanes = slice(k * LANES, (k + 1) * LANES)
            window[u, :, lanes] = window[u, :, lanes] + stencil(wide, weights, u, lanes)

    io.wait(1)
    mask = column_mask(c)

    def reduce(i, carry):
        num, den = carry
        before = image0[i]
        mine = jnp.where(mask, window[i + OV], 0.0)
        image_own[i] = mine
        image = before - scale * mine
        left_over = residual[i] - scale * before
        return num + left_over * image, den + image * image

    zero = jnp.zeros((ES, c), F32)
    num, den = lax.fori_loop(0, CS, reduce, (zero, zero), unroll=2)
    sums = (jnp.sum(num, axis=0, keepdims=True), jnp.sum(den, axis=0, keepdims=True))
    io.flush(image_own, coarse)
    solve_and_send(
        io,
        window[...].reshape(LOCAL, c),
        inverse_high,
        inverse_low,
        basis,
        sums,
        field_out,
        tail,
        head,
        sent,
        (top, bottom),
    )


def step2(
    io,
    field,
    from_left,
    from_right,
    above,
    below,
    got,
    diag,
    up,
    down,
    left,
    right_w,
    modes_a_high,
    modes_a_low,
    residual,
    image0,
    image1,
    scale_in,
    residual_out,
    image_out,
    coarse,
    sent,
    scale_out,
    wide,
    window,
):
    weights = (diag, up, down, left, right_w)
    c = field.shape[2]
    wide[3:31, 8:40, :] = field[...]
    for i in range(CS):
        wide[3 + i, 9:10, :] = from_left[i : i + 1, :]
        wide[3 + i, 38:39, :] = from_right[i : i + 1, :]
    wide[2, 8:40, :] = above[...]
    wide[31, 8:40, :] = below[...]
    total = summed(got)
    scale = total[NB : NB + 1] / total[NB + 1 : NB + 2]
    scale_out[...] = jnp.broadcast_to(scale, scale_out.shape)
    earlier = scale_in[0:1]
    total = coarse_rows(total)
    coarse[...] = total
    own = slice(FIRST, FIRST + OWNROWS)
    high, low = halves(total)
    table = modes_a_high[own, :]
    window[...] = (
        dot(table, high) + (dot(table, low) + dot(modes_a_low[own, :], high))
    ).reshape(window.shape)
    io.wait(0)
    mask = column_mask(LANES)

    def reduce(i, carry):
        out = []
        for k in range(c // LANES):
            lanes = slice(k * LANES, (k + 1) * LANES)
            num, den = carry[2 * k], carry[2 * k + 1]
            mine = window[i, :, lanes] + stencil(wide, weights, i + OV, lanes)
            mine = jnp.where(mask, mine, 0.0)
            s0 = earlier[:, lanes]
            s1 = scale[:, lanes]
            q0 = image0[i, :, lanes]
            q1 = image1[i, :, lanes]
            before = q0 - s0 * q1
            left_over = residual[i, :, lanes] - s0 * q0 - s1 * before
            image = before - s1 * (q1 - s0 * mine)
            residual_out[i, :, lanes] = left_over
            image_out[i, :, lanes] = image
            out += [num + left_over * image, den + image * image]
        return tuple(out)

    zero = jnp.zeros((ES, LANES), F32)
    sums = lax.fori_loop(0, CS, reduce, (zero,) * (2 * (c // LANES)), unroll=2)
    sums = [jnp.sum(x, axis=0, keepdims=True) for x in sums]
    num = jnp.concatenate(sums[0::2], axis=1)
    den = jnp.concatenate(sums[1::2], axis=1)
    both = jnp.concatenate([num, den], axis=1)
    for k in range(sent.shape[0]):
        sent[k] = both


def resend(io, got, sent):
    total = summed(got)
    for k in range(sent.shape[0]):
        sent[k] = total


def early_directions(
    io,
    guess,
    field0,
    field1,
    coarse0,
    coarse1,
    modes_high,
    modes_low,
    scale0,
    base_out,
    direction_out,
    second_out,
    p0,
    p1,
    change,
):
    for p, coarse in ((p0, coarse0), (p1, coarse1)):
        p[...] = spread_coarse(modes_high, modes_low, coarse[...]).reshape(p.shape)
    s0 = scale0[0:1]

    @pl.loop(0, CS, unroll=2)
    def _(i):
        first_p = p0[i] + field0[i]
        second = p1[i] + field1[i]
        direction_out[i] = first_p - s0 * second
        second_out[i] = second
        change[i] = s0 * first_p
        base_out[i] = guess[i] + change[i, OV : OV + CS, :]


def late_directions(
    io,
    base,
    direction,
    second,
    field2,
    coarse2,
    modes_high,
    modes_low,
    scale0,
    scale1,
    partial_out,
    last_out,
    p2,
):
    p2[...] = spread_coarse(modes_high, modes_low, coarse2[...]).reshape(p2.shape)
    s0 = scale0[0:1]
    s1 = scale1[0:1]

    @pl.loop(0, CS, unroll=2)
    def _(i):
        last_out[i] = direction[i] - s1 * (second[i] - s0 * (p2[i] + field2[i]))
        partial_out[i] = base[i] + s1 * direction[i, OV : OV + CS, :]


def finish(io, got, guess_sum, last, residual, image, answer, residual_out):
    total = summed(got)
    c = guess_sum.shape[2]
    scale = total[:, 0:c] / total[:, c:]

    io.wait(0)

    @pl.loop(0, CS, unroll=4)
    def _(i):
        answer[i] = guess_sum[i] + scale * last[i, OV : OV + CS, :]

    io.flush(answer)
    io.wait(1)

    @pl.loop(0, CS, unroll=4)
    def _(i):
        residual_out[i] = (
            residual[i, OV : OV + CS, :] - scale * image[i, OV : OV + CS, :]
        )


def mode_tables():
    of_row = np.zeros((XROWS, 1, LANES), np.float32)
    of_col = np.zeros((XCOLS, LANES), np.float32)
    region = [0] * 3 + [1] * CS + [2] * 3
    for db in range(3):
        for da in range(3):
            for m in range(MODES):
                lane = (db * 3 + da) * MODES + m
                for e in range(XROWS):
                    of_row[e, 0, lane] = region[e] == da
                    of_col[7 + e, lane] = region[e] == db
    return of_row, of_col


def coarse_tables(nw, nn):
    pick = np.zeros((nn * SLOT, 3 * nn * MODES), np.float32)
    spread = np.zeros((nw * MODES, nw * 8), np.float32)
    ones = np.zeros((nn * SLOT, nw * 8), np.float32)
    for to in range(nn):
        for db in range(3):
            for da in range(3):
                a = to + da - 1
                for m in range(MODES):
                    if 0 <= a < nn:
                        row = to * SLOT + (db * 3 + da) * MODES + m
                        pick[row, (db * nn + a) * MODES + m] = 1.0
        for b in range(nw):
            ones[to * SLOT + NB, b * 8 + 4] = 1.0
            ones[to * SLOT + NB + 1, b * 8 + 5] = 1.0
    for b in range(nw):
        for m in range(MODES):
            spread[b * MODES + m, b * 8 + m] = 1.0
    return pick, spread, ones


def local(
    right_side,
    initial_guess,
    class_map,
    class_conductivity,
    window_index,
    local_inverse,
    coarse_basis,
    coarse_inverse,
):
    nw = lax.axis_size("wide")
    nn = lax.axis_size("narrow")
    c = right_side.shape[2]
    lanes = 2 * c + LANES
    own = ((CS, ES, c), F32)
    side = ((3, CS, c), F32)
    line = ((CS, c), F32)
    strip = ((ES, c), F32)
    edge = ((6, ES, c), F32)
    rows = ((3, XCOLS, c), F32)
    to_wide = ((nw, 8, c), F32)
    weight = ((ES, ES, LANES), F32)
    extended = pltpu.VMEM((XROWS, XCOLS, c), F32)
    window = pltpu.VMEM((ES, ES, c), F32)
    inverse = ((OWNROWS, LOCAL), BF16)
    of_row, of_col = (jnp.asarray(x) for x in mode_tables())
    pick, coarse_spread, ones = (jnp.asarray(x) for x in coarse_tables(nw, nn))

    def exchange(x, axis):
        return lax.all_to_all(x, axis, 0, 0, tiled=True)

    def within(x, groups):
        return lax.all_to_all(
            x, ("wide", "narrow"), 0, 0, axis_index_groups=groups, tiled=True
        )

    tail, head, small, basis = call(
        prepare,
        [
            ((7, ES, c), F32),
            ((7, ES, c), F32),
            ((CS, ES, LANES), F32),
            ((8, LOCAL), F32),
        ],
        [
            initial_guess,
            right_side,
            class_map,
            class_conductivity.reshape(1, -1),
            window_index.reshape(1, LOCAL),
            coarse_basis.reshape(MODES, LOCAL),
            coarse_inverse,
        ],
        [pltpu.VMEM((LOCAL, LOCAL), BF16)],
        late=((0, 1),),
    )
    from_left = shift(tail, "wide", 1)
    from_right = shift(head, "wide", -1)
    inverse_high, inverse_low = [
        call(
            functools.partial(reorder, part),
            [inverse],
            [window_index.reshape(1, LOCAL), local_inverse.reshape(LOCAL, LOCAL)],
            [pltpu.VMEM((LOCAL, LOCAL), BF16), pltpu.VMEM((OWNROWS, LOCAL), BF16)],
            late=((1,),),
        )[0]
        for part in range(2)
    ]
    from_left, from_right, inverse_high = lax.optimization_barrier(
        (from_left, from_right, inverse_high)
    )
    tail, head = call(
        first_rows,
        [((3, XCOLS, lanes), F32)] * 2,
        [initial_guess, right_side, small, from_left, from_right],
    )
    above = shift(tail, "narrow", 1)
    below = shift(head, "narrow", -1)
    (table,) = call(
        coarse_table,
        [((nn * SLOT, nw * 8), F32)],
        [from_left, coarse_inverse, from_right, pick, coarse_spread, ones],
    )
    out = call(
        first,
        [weight] * 5
        + [((LOCAL, LANES), BF16)] * 2
        + [((OWNROWS, LANES), BF16)] * 2
        + [own, own, side, side, to_wide, edge],
        [
            initial_guess,
            right_side,
            small,
            from_left,
            from_right,
            above,
            below,
            basis,
            inverse_high,
            inverse_low,
            of_row,
            of_col,
        ],
        [
            pltpu.VMEM((XROWS, XCOLS, lanes), F32),
            pltpu.VMEM((XROWS, XCOLS, LANES), F32),
            window,
        ],
        late=((), (), (8, 9)),
    )
    weights = out[:5]
    modes_a = out[5:7]
    modes = out[7:9]
    residual, field0, tail, head, sent, edges = out[9:]

    def coarse(sent, edges, tail, head):
        got = exchange(sent, "wide")
        from_left = shift(tail, "wide", 1)
        from_right = shift(head, "wide", -1)
        (parts,) = call(partial, [((nn, SLOT, c), F32)], [got, table])
        parts, from_left, from_right = lax.optimization_barrier((parts, from_left, from_right))
        tail, head = call(field_rows, [rows, rows], [edges, from_left, from_right])
        above = shift(tail, "narrow", 1)
        below = shift(head, "narrow", -1)
        return (from_left, from_right, above, below), exchange(parts, "narrow")

    solver = [basis, inverse_high, inverse_low, residual]
    coarse_out = ((LANES, c), F32)
    scale_out = ((8, c), F32)
    near, got = coarse(sent, edges, tail, head)
    image0, coarse0, field1, tail, head, sent, edges = call(
        step0,
        [own, coarse_out, own, side, side, to_wide, edge],
        [field0, *near, got, *weights, *modes_a, *solver],
        [extended, window],
        late=((6, 7, 8, 9, 10), (13, 16), (14, 15)),
    )
    near, got = coarse(sent, edges, tail, head)
    image1, coarse1, field2, tail, head, sent, top, bottom, scale0 = call(
        step1,
        [own, coarse_out, own, line, line, to_wide, strip, strip, scale_out],
        [field1, *near, got, *weights, *modes_a, *solver, image0],
        [extended, window],
        late=((6, 7, 8, 9, 10), (13, 16, 17), (14, 15)),
    )
    got = exchange(sent, "wide")
    from_left = shift(tail, "wide", 1)
    from_right = shift(head, "wide", -1)
    early = call(
        early_directions,
        [((CS, CS, c), F32), own, own],
        [initial_guess, field0, field1, coarse0, coarse1, *modes, scale0],
        [pltpu.VMEM((CS, ES, c), F32)] * 3,
    )
    got, early, from_left, from_right = lax.optimization_barrier(
        (got, early, from_left, from_right)
    )
    (parts,) = call(partial, [((nn, SLOT, c), F32)], [got, table])
    above = shift(bottom, "narrow", 1)
    below = shift(top, "narrow", -1)
    near = (from_left, from_right, above, below)
    got = exchange(parts, "narrow")
    residual, image, coarse2, sent, scale1 = call(
        step2,
        [own, own, coarse_out, ((4 * nn, 1, 2 * c), F32), scale_out],
        [field2, *near, got, *weights, *modes_a, residual, image0, image1, scale0],
        [extended, pltpu.VMEM((CS, ES, c), F32)],
        late=((6, 7, 8, 9, 10, 13, 14, 15),),
    )
    group = 4 * nn
    count = nw // 4
    inner = [[k * group + r for r in range(group)] for k in range(count)]
    outer = [[k * group + r for k in range(count)] for r in range(group)]
    got = within(sent, inner)
    (sent,) = call(resend, [((count, 1, 2 * c), F32)], [got])
    got = within(sent, outer)
    before_last, last = call(
        late_directions,
        [((CS, CS, c), F32), own],
        [*early, field2, coarse2, *modes, scale0, scale1],
        [pltpu.VMEM((CS, ES, c), F32)],
    )
    return tuple(
        call(
            finish,
            [((CS, CS, c), F32)] * 2,
            [got, before_last, last, residual, image],
            late=((1, 2), (3, 4)),
        )
    )


def solution(mesh):
    in_specs = (
        P("narrow", "wide", None),
        P("narrow", "wide", None),
        P("narrow", "wide"),
        P(),
        P("narrow", "wide", None),
        P("narrow", "wide", None, None),
        P("narrow", "wide", None, None),
        P("wide", "narrow"),
    )
    out_specs = (P("narrow", "wide", None), P("narrow", "wide", None))
    return jax.shard_map(local, mesh=mesh, in_specs=in_specs, out_specs=out_specs, check_vma=False)
```
